512 devices in a mesh: ctx: 64 (over z, x, core), head: 8 (over y).
Axes of the slice: x: 4, y: 8, z: 8, core: 2. Of those that a mesh axis runs over, the one named last changes fastest.
Arguments:
- queries: bfloat16 [8192, 4096], P('ctx', 'head'), may hold values from -60 to 60
- keys: bfloat16 [8192, 1024], P('ctx', 'head'), may hold values from -50 to 50
- values: bfloat16 [8192, 1024], P('ctx', 'head'), may hold values from -6 to 6
- vertical: int32 [8, 32], P('head'), may hold values from 0 to 127, as said below
- offsets: int32 [32, 64], P('head'), may hold values from 0 to 127, as said below
- send_order: int32 [64, 64], P('ctx'), may hold values from 0 to 63, each once within a row
- out_weight: bfloat16 [4096, 4096], P('head'), may hold values from -0.125 to 0.125
Outputs:
- output: bfloat16 [8192, 4096], P('ctx', 'head')
The draws below stay inside these ranges and needn't reach their ends.
Inputs may be any that keep to these rules, and one draw needn't show every extreme that they name: `vertical`: each row holds 32 distinct block numbers in increasing order; of one row, at most 2 lie among the blocks of the positions of one index of ctx (2 blocks), and some index holds exactly 2 of them. Each row holds 64 distinct offsets and always contains 0, 1 and 127. `send_order`: each row is a permutation of the piece numbers.
All inputs are finite; a program needn't handle non-finite values.
Results may differ from the reference program's by a relative error of at most 0.0055.
Values may be sent and summed in bfloat16 or wider, within the bound.
No kernel may reach another device: no remote copies, remote signals or barrier semaphores. Data moves between devices by JAX's collectives and lax.ppermute only.
A program may use at most 64 MiB of HBM per device.

```python
import math
import jax
import jax.numpy as jnp
from jax import lax

QUERY_HEADS = 32
KEY_VALUE_HEADS = 8
HEAD_SIZE = 128
D = 4096
LOCAL_SEQUENCE = 128
BLK = 64
NV = 32
CAPV = 2
SLASH_COUNT = 64
TOTAL_TOKENS = 8192
N_CTX = 64


def draw_queries(key, part):
    key = jax.random.fold_in(key, 7)
    sampled_values = jnp.clip(jax.random.normal(key, (TOTAL_TOKENS, QUERY_HEADS, HEAD_SIZE), jnp.float32), -6.0, 6.0)
    return sampled_values.reshape(TOTAL_TOKENS, QUERY_HEADS * HEAD_SIZE).astype(jnp.bfloat16)


def draw_keys(key, part):
    key = jax.random.fold_in(key, 9)
    sampled_values = jnp.clip(jax.random.normal(key, (TOTAL_TOKENS, KEY_VALUE_HEADS, HEAD_SIZE), jnp.float32), -6.0, 6.0)
    return sampled_values.reshape(TOTAL_TOKENS, KEY_VALUE_HEADS * HEAD_SIZE).astype(jnp.bfloat16)


def draw_vertical(key, part):
    key = jax.random.fold_in(key, 11)
    per_dev = LOCAL_SEQUENCE // BLK
    lowest = max(1, -(-(NV - N_CTX) // (CAPV - 1)))
    highest = NV // CAPV

    def single_head(head_key):
        first, second, third = jax.random.split(head_key, 3)
        full_count = jax.random.randint(first, (), lowest, highest + 1)
        singles = NV - CAPV * full_count
        dev_rank = jnp.argsort(jax.random.permutation(second, N_CTX))
        counts = jnp.where(dev_rank < full_count, CAPV, jnp.where(dev_rank < full_count + singles, 1, 0))
        block_perm = jax.vmap(lambda sub: jax.random.permutation(sub, per_dev))(jax.random.split(third, N_CTX))
        block_rank = jnp.argsort(block_perm, axis=1)
        chosen = block_rank < counts[:, None]
        numbers = jnp.arange(N_CTX)[:, None] * per_dev + jnp.arange(per_dev)[None, :]
        listed = jnp.where(chosen, numbers, N_CTX * per_dev).reshape(-1)
        return jnp.sort(listed)[:NV].astype(jnp.int32)
    return jax.vmap(single_head)(jax.random.split(key, KEY_VALUE_HEADS))


def draw_offsets(key, part):
    key = jax.random.fold_in(key, 13)

    def single_head(head_key):
        middle = jax.random.permutation(head_key, LOCAL_SEQUENCE - 3)[:SLASH_COUNT - 3] + 2
        fixed_part = jnp.array([0, 1, LOCAL_SEQUENCE - 1], jnp.int32)
        return jnp.concatenate([fixed_part, middle.astype(jnp.int32)])
    return jax.vmap(single_head)(jax.random.split(key, QUERY_HEADS))


def spiked(entries, own_key, source, target, parts, factor):
    def block_of(dim):
        return (jnp.arange(entries.shape[dim]) // (entries.shape[dim] // parts)).reshape((-1,) + (1,) * (entries.ndim - 1 - dim))

    near = jax.random.permutation(own_key, parts)[block_of(target)]
    other_side = (block_of(target) + parts // 2) % parts
    return jnp.where((block_of(source) == near) | (block_of(source) == other_side), factor * entries, entries)


def levels(stream_key, shape, shards, least, high):
    loudness = 1.0
    for axis_at, shards_of in shards:
        steps = jax.random.uniform(jax.random.fold_in(jax.random.fold_in(stream_key, 6), axis_at), (shards_of,), jnp.float32, least / len(shards), high / len(shards))
        loudness = loudness * jnp.repeat(jnp.exp(steps), shape[axis_at] // shards_of).reshape((-1,) + (1,) * (len(shape) - 1 - axis_at))
    return loudness


def normal_values(rng, dims, spread, most, pieces=(), held_as=jnp.bfloat16):
    drawn = jax.random.normal(rng, dims, jnp.float32) * spread
    if len(pieces) > 0:
        drawn = levels(rng, dims, pieces, -0.22, 0.18) * drawn
    return jnp.clip(drawn, min=-most, max=most).astype(held_as)


def heavy_noise(key, shape, width, reach, cuts, heavy, held_as=jnp.bfloat16):
    values = width * jax.random.normal(key, shape, jnp.float32)
    if cuts:
        values = values * levels(key, shape, cuts, -0.22, 0.18)
    return jnp.clip(spiked(values, jax.random.fold_in(key, 3), *heavy), -reach, reach).astype(held_as)


def setup_inputs(seed: int = 0) -> dict:
    splits = jax.random.split(jax.random.key(seed), 8)
    queries = draw_queries(jax.random.fold_in(splits[7], 71), 0)
    keys = draw_keys(jax.random.fold_in(splits[7], 71), 0)
    values = normal_values(splits[2], (TOTAL_TOKENS, KEY_VALUE_HEADS * HEAD_SIZE), 1.0, 6.0, ((0, 64), (1, 8)))
    vertical = draw_vertical(jax.random.fold_in(splits[7], 71), 0)
    offsets = draw_offsets(jax.random.fold_in(splits[7], 71), 0)
    send_order = jax.vmap(lambda own: jax.random.permutation(own, N_CTX))(jax.random.split(splits[5], N_CTX)).reshape((N_CTX, N_CTX)).astype(jnp.int32)
    out_weight = heavy_noise(splits[6], (QUERY_HEADS * HEAD_SIZE, D), D ** -0.5, 0.125, ((0, 8),), (0, 1, 8, 2.0))
    return dict(queries=queries, keys=keys, values=values, vertical=vertical, offsets=offsets, send_order=send_order, out_weight=out_weight)


def attend(query_block, vert_keys, vert_vals, vert_pos, band_keys, band_vals, band_pos, query_pos, in_vert, slash_mask):
    score_scale = 1.0 / math.sqrt(HEAD_SIZE)
    vert_scores = jnp.einsum('ird,kd->rik', query_block, vert_keys) * score_scale
    band_scores = jnp.einsum('ird,kd->rik', query_block, band_keys) * score_scale
    vert_mask = (vert_pos[None, :] <= query_pos[:, None])[None]
    band_mask = slash_mask & jnp.logical_not(in_vert)[None, None, :] & (band_pos >= 0)[None, None, :]
    row_max = jnp.maximum(lax.optimization_barrier(jnp.max(jnp.where(vert_mask, vert_scores, -jnp.inf), axis=2)), lax.optimization_barrier(jnp.max(jnp.where(band_mask, band_scores, -jnp.inf), axis=2)))
    vert_weights = jnp.where(vert_mask, jnp.exp(vert_scores - row_max[:, :, None]), 0.0)
    band_weights = jnp.where(band_mask, jnp.exp(band_scores - row_max[:, :, None]), 0.0)
    row_total = lax.optimization_barrier(jnp.sum(vert_weights, axis=2)) + lax.optimization_barrier(jnp.sum(band_weights, axis=2))
    vert_round = lax.optimization_barrier(vert_weights.astype(jnp.bfloat16)).astype(jnp.float32)
    band_round = lax.optimization_barrier(band_weights.astype(jnp.bfloat16)).astype(jnp.float32)
    weighted = jnp.einsum('rik,kd->rid', vert_round, vert_vals) + jnp.einsum('rik,kd->rid', band_round, band_vals)
    return (weighted / row_total[:, :, None]).astype(jnp.bfloat16)

def reference(queries, keys, values, vertical, offsets, send_order, out_weight):
    query_group_width = QUERY_HEADS // KEY_VALUE_HEADS
    query_head_list = queries.astype(jnp.float32).reshape(N_CTX, LOCAL_SEQUENCE, KEY_VALUE_HEADS, query_group_width, HEAD_SIZE).transpose(2, 0, 1, 3, 4)
    key_head_list = keys.astype(jnp.float32).reshape(TOTAL_TOKENS, KEY_VALUE_HEADS, HEAD_SIZE).transpose(1, 0, 2)
    value_head_list = values.astype(jnp.float32).reshape(TOTAL_TOKENS, KEY_VALUE_HEADS, HEAD_SIZE).transpose(1, 0, 2)
    shifted_groups = offsets.reshape(KEY_VALUE_HEADS, query_group_width, SLASH_COUNT)
    lag_index = (jnp.arange(LOCAL_SEQUENCE)[:, None] - jnp.arange(2 * LOCAL_SEQUENCE)[None, :] + 2 * LOCAL_SEQUENCE).astype(jnp.int32)

    def per_head(args):
        q_head, k_head, v_head, vert_list, off_group = args
        vert_keys = k_head.reshape(TOTAL_TOKENS // BLK, BLK, HEAD_SIZE)[vert_list].reshape(NV * BLK, HEAD_SIZE)
        vert_vals = v_head.reshape(TOTAL_TOKENS // BLK, BLK, HEAD_SIZE)[vert_list].reshape(NV * BLK, HEAD_SIZE)
        vert_pos = (vert_list[:, None] * BLK + jnp.arange(BLK).astype(jnp.int32)[None, :]).reshape(NV * BLK)
        shifted = (jnp.arange(3 * LOCAL_SEQUENCE) - LOCAL_SEQUENCE).astype(jnp.int32)
        offset_table = jnp.any(off_group[:, None, :] == shifted[None, :, None], axis=2)
        slash_mask = offset_table[:, lag_index]
        k_pad = jnp.concatenate([jnp.zeros((LOCAL_SEQUENCE, HEAD_SIZE), jnp.float32), k_head], axis=0)
        v_pad = jnp.concatenate([jnp.zeros((LOCAL_SEQUENCE, HEAD_SIZE), jnp.float32), v_head], axis=0)

        def per_block(block_id):
            start = (block_id * LOCAL_SEQUENCE).astype(jnp.int32)
            band_keys = lax.dynamic_slice_in_dim(k_pad, start, 2 * LOCAL_SEQUENCE, 0)
            band_vals = lax.dynamic_slice_in_dim(v_pad, start, 2 * LOCAL_SEQUENCE, 0)
            band_pos = ((block_id - 1) * LOCAL_SEQUENCE + jnp.arange(2 * LOCAL_SEQUENCE)).astype(jnp.int32)
            query_pos = (block_id * LOCAL_SEQUENCE + jnp.arange(LOCAL_SEQUENCE)).astype(jnp.int32)
            in_vert = jnp.any((band_pos // BLK)[:, None] == vert_list[None, :], axis=1)
            return attend(q_head[block_id], vert_keys, vert_vals, vert_pos, band_keys, band_vals, band_pos, query_pos, in_vert, slash_mask)
        return lax.map(per_block, jnp.arange(N_CTX).astype(jnp.int32))
    attended = lax.map(per_head, (query_head_list, key_head_list, value_head_list, vertical, shifted_groups))
    attended = attended.transpose(1, 3, 0, 2, 4).reshape(TOTAL_TOKENS, QUERY_HEADS * HEAD_SIZE)
    piece_rows = LOCAL_SEQUENCE // N_CTX
    row_parts = attended.reshape(N_CTX, N_CTX, piece_rows, QUERY_HEADS * HEAD_SIZE)
    picked = jnp.take_along_axis(row_parts, send_order[:, :, None, None], axis=1)
    balanced = picked.transpose(1, 0, 2, 3).reshape(TOTAL_TOKENS, QUERY_HEADS * HEAD_SIZE)
    return jnp.dot(balanced, out_weight, preferred_element_type=jnp.float32).astype(jnp.bfloat16)
```

```python
import math

import jax
import jax.numpy as jnp
from jax import lax
from jax.experimental import pallas as pl
from jax.experimental.pallas import tpu as pltpu
from jax.sharding import Mesh, PartitionSpec as P

HEAD = 128
BLK = 64
NV = 32
CTX = ("z", "x", "c")
VMEM = pl.BlockSpec(memory_space=pltpu.VMEM)
SMEM = pl.BlockSpec(memory_space=pltpu.SMEM)
F32 = jnp.float32
BF16 = jnp.bfloat16


def iota(shape, dim):
    return lax.broadcasted_iota(jnp.int32, shape, dim)


def select_kernel(vert, recv, out):
    rows = 2 * NV
    row = iota((rows, HEAD), 0)
    want = jnp.zeros((rows, HEAD), jnp.int32)
    for n in range(NV):
        want = jnp.where(row % NV == n, vert[0, n] * 2 + row // NV, want)
    lane = iota((rows, HEAD), 1)
    picked = jnp.zeros((rows, HEAD), F32)
    for half in range(2):
        one_hot = jnp.where(want == lane + half * HEAD, 1.0, 0.0).astype(BF16)
        picked += jnp.dot(one_hot, recv[pl.ds(half * HEAD, HEAD), :], preferred_element_type=F32)
    picked = picked.astype(BF16)
    for z in range(out.shape[0]):
        out[z] = picked


def dot_t(a, b):
    return lax.dot_general(a, b, (((1,), (1,)), ((), ())), preferred_element_type=F32)


def attention_kernel(place, vert, offsets, q, mine, other, prev, keys, values, target, out):
    rows = q.shape[0]
    band = 2 * rows
    ctx, core = place[0], place[1]
    base = ctx * rows
    lag = rows - iota((8, band), 1)
    table = jnp.zeros((8, band), F32)
    offs = offsets[...]
    for k in range(offs.shape[1]):
        table = jnp.where(offs[:, k : k + 1] == lag, 1.0, table)
    band_block = (base - rows) // BLK + iota((1, band), 1) // BLK
    closed = band_block < 0
    lane = iota((1, HEAD), 1)
    vpos = jnp.zeros((1, HEAD), jnp.int32)
    for n in range(NV):
        block = vert[0, n]
        closed = closed | (band_block == block)
        vpos = jnp.where(lane % NV == n, block * BLK, vpos)
    vpos = vpos + (lane // NV) * 8 - base
    parts = mine.shape[0] * mine.shape[2] // HEAD
    pos_mine, pos_other = [], []
    for m in range(parts):
        step = (m % 2) * 32 + (m // 2) * 2
        pos_mine.append(vpos + (step + core))
        pos_other.append(vpos + (step + 1 - core))
    query = iota((rows, 1), 0)
    mask_mine = jnp.concatenate(pos_mine, axis=1) <= query
    mask_other = jnp.concatenate(pos_other, axis=1) <= query
    k1 = mine[:, 0].reshape(-1, HEAD)
    v1 = mine[:, 1].reshape(-1, HEAD)
    k2 = other[:, 0].reshape(-1, HEAD)
    v2 = other[:, 1].reshape(-1, HEAD)
    kb = jnp.concatenate([prev[0], keys[...]], axis=0)
    vb = jnp.concatenate([prev[1], values[...]], axis=0)
    low = -jnp.inf
    factor = math.log2(math.e) / math.sqrt(HEAD)
    done = []
    for h in range(q.shape[1] // HEAD):
        qh = q[:, h * HEAD : (h + 1) * HEAD]
        spread = jnp.broadcast_to(table[h : h + 1], (rows, band))
        slash = pltpu.roll(spread, 0, 1, stride=1, stride_axis=0)
        mask_band = (slash > 0.5) & jnp.logical_not(closed)
        s0 = jnp.where(mask_band, dot_t(qh, kb), low)
        s1 = jnp.where(mask_mine, dot_t(qh, k1), low)
        s2 = jnp.where(mask_other, dot_t(qh, k2), low)
        top = jnp.maximum(
            jnp.maximum(jnp.max(s1, axis=1, keepdims=True), jnp.max(s2, axis=1, keepdims=True)),
            jnp.max(s0, axis=1, keepdims=True),
        )
        p0 = jnp.exp2((s0 - top) * factor)
        p1 = jnp.exp2((s1 - top) * factor)
        p2 = jnp.exp2((s2 - top) * factor)
        total = (
            jnp.sum(p0, axis=1, keepdims=True)
            + jnp.sum(p1, axis=1, keepdims=True)
            + jnp.sum(p2, axis=1, keepdims=True)
        )
        o = jnp.dot(p0.astype(BF16), vb, preferred_element_type=F32)
        o += jnp.dot(p1.astype(BF16), v1, preferred_element_type=F32)
        o += jnp.dot(p2.astype(BF16), v2, preferred_element_type=F32)
        done.append((o / total).astype(BF16))
    attended = jnp.concatenate(done, axis=1)
    one_hot = jnp.where(iota((rows, rows), 0) == target[...], 1.0, 0.0).astype(BF16)
    out[...] = lax.dot_general(
        one_hot, attended, (((0,), (0,)), ((), ())), preferred_element_type=F32
    ).astype(BF16)


def project_kernel(arrived, weight, out, held):
    rows = held.shape[0]

    @pl.when(pl.program_id(0) == 0)
    def _():
        new = iota((rows, rows), 0)
        old = (new % 16 // 2) * 16 + (new // 16) * 2 + new % 2
        one_hot = jnp.where(iota((rows, rows), 1) == old, 1.0, 0.0).astype(BF16)
        held[...] = jnp.dot(one_hot, arrived[...], preferred_element_type=F32).astype(BF16)

    part = jnp.dot(held[...], weight[...], preferred_element_type=F32).astype(BF16)
    out[...] = part.reshape(out.shape)


def local(queries, keys, values, vertical, offsets, send_order, out_weight):
    z_n, x_n, c_n, y_n = (lax.axis_size(a) for a in ("z", "x", "c", "y"))
    rows = queries.shape[0]
    n_ctx = z_n * x_n * c_n
    ctx = lax.axis_index(CTX)
    core = lax.axis_index("c")
    place = jnp.stack([ctx, core]).astype(jnp.int32)

    prev = lax.ppermute(jnp.stack([keys, values]), CTX, [(i, i + 1) for i in range(n_ctx - 1)])

    lanes = jnp.concatenate([keys[:BLK], values[:BLK], keys[BLK:], values[BLK:]], axis=1)
    recv = lax.all_to_all(lanes.reshape(n_ctx, 4, HEAD), CTX, 0, 0, tiled=True)
    picked = pl.pallas_call(
        select_kernel,
        out_shape=jax.ShapeDtypeStruct((z_n, 2 * NV, HEAD), BF16),
        in_specs=[SMEM, VMEM],
        out_specs=VMEM,
        name="select_rows",
    )(vertical, recv.reshape(4 * n_ctx, HEAD))
    by_z = lax.all_to_all(picked, "z", 0, 0, tiled=True)
    by_x = lax.all_to_all(jnp.broadcast_to(by_z[None], (x_n,) + by_z.shape), "x", 0, 0, tiled=True)
    mine = by_x.reshape(x_n * z_n, 2, NV, HEAD)
    other = lax.ppermute(mine, "c", [(0, 1), (1, 0)])

    order = send_order.reshape(z_n, x_n * c_n).T.reshape(1, n_ctx)
    target = (order[:, :, None] * 2 + jnp.arange(2)[None, None, :]).reshape(1, rows)
    padded = jnp.concatenate([offsets, offsets], axis=0)
    attended = pl.pallas_call(
        attention_kernel,
        out_shape=jax.ShapeDtypeStruct(queries.shape, BF16),
        in_specs=[SMEM, SMEM] + [VMEM] * 8,
        out_specs=VMEM,
        name="attention",
        compiler_params=pltpu.CompilerParams(vmem_limit_bytes=48 * 1024 * 1024),
    )(place, vertical, padded, queries, mine, other, prev, keys, values, target)

    arrived = lax.all_to_all(
        attended.reshape(x_n * c_n, z_n * 2, queries.shape[1]), ("x", "c"), 0, 0, tiled=True
    ).reshape(rows, queries.shape[1])
    width = out_weight.shape[1] // y_n
    partial = pl.pallas_call(
        project_kernel,
        grid=(y_n,),
        out_shape=jax.ShapeDtypeStruct((z_n, y_n, rows // z_n, width), BF16),
        in_specs=[
            pl.BlockSpec(arrived.shape, lambda j: (0, 0)),
            pl.BlockSpec((out_weight.shape[0], width), lambda j: (0, j)),
        ],
        out_specs=pl.BlockSpec((z_n, 1, rows // z_n, width), lambda j: (0, j, 0, 0)),
        scratch_shapes=[pltpu.VMEM(arrived.shape, BF16)],
        name="project",
    )(arrived, out_weight)
    sums = lax.all_to_all(
        partial.reshape(z_n * y_n, rows // z_n, width), ("z", "y"), 0, 0, tiled=True
    ).reshape(z_n, y_n, rows // z_n, width)
    return jnp.sum(sums.astype(F32), axis=1).astype(BF16).reshape(rows, width)


def solution(mesh):
    cut = Mesh(mesh.devices.reshape(8, 4, 2, 8), ("z", "x", "c", "y"))
    placed = (
        P(CTX, "y"),
        P(CTX, "y"),
        P(CTX, "y"),
        P("y", None),
        P("y", None),
        P(CTX, None),
        P("y", None),
    )
    return jax.shard_map(
        local, mesh=cut, in_specs=placed, out_specs=P(CTX, "y"), check_vma=False
    )
```

```python
import math

import jax
import jax.numpy as jnp
from jax import lax
from jax.experimental import pallas as pl
from jax.experimental.pallas import tpu as pltpu
from jax.sharding import Mesh, PartitionSpec as P

HEAD = 128
BLK = 64
NV = 32
CTX = ("z", "x", "c")
VMEM = pl.BlockSpec(memory_space=pltpu.VMEM)
SMEM = pl.BlockSpec(memory_space=pltpu.SMEM)
HBM = pl.BlockSpec(memory_space=pltpu.HBM)
F32 = jnp.float32
BF16 = jnp.bfloat16


def iota(shape, dim):
    return lax.broadcasted_iota(jnp.int32, shape, dim)


def pick(one_hot, rows):
    one_hot = jnp.where(one_hot, 1.0, 0.0).astype(BF16)
    return jnp.dot(one_hot, rows, preferred_element_type=F32).astype(BF16)


def select_kernel(vert, recv, out):
    rows = 2 * NV
    count = recv.shape[0]
    row = iota((rows, 1), 0)
    want = jnp.zeros((rows, 1), jnp.int32)
    for n in range(NV):
        want = jnp.where(row % NV == n, vert[0, n] * 2, want)
    want = want + row // NV
    held = recv[...]
    picked = pick(iota((rows, count), 1) == want, held)
    ahead = pick(iota((count, count), 1) == (iota((count, 1), 0) + (count - 4)) % count, held)
    for chip in range(out.shape[0]):
        out[chip, :rows] = picked
        out[chip, rows:] = ahead[chip * 8 : chip * 8 + 8]


def dot_t(a, b):
    return lax.dot_general(a, b, (((1,), (1,)), ((), ())), preferred_element_type=F32)


def attention_kernel(
    place, vert, q_in, keys_in, values_in, offsets_in, order_in, weight_in, mine, other, out, weight,
    q, keys, values, offsets, order, sems,
):
    moves = [
        pltpu.make_async_copy(a, b, sems.at[i])
        for i, (a, b) in enumerate(
            [(q_in, q), (keys_in, keys), (values_in, values), (offsets_in, offsets), (order_in, order), (weight_in, weight)]
        )
    ]
    for move in moves:
        move.start()
    rows = q.shape[0]
    heads = q.shape[1] // HEAD
    band = 2 * rows
    ctx, core = place[0], place[1]
    base = ctx * rows
    band_block = (base - rows) // BLK + iota((1, band), 1) // BLK
    closed = band_block < 0
    lane = iota((1, HEAD), 1)
    vpos = jnp.zeros((1, HEAD), jnp.int32)
    for n in range(NV):
        block = vert[0, n]
        closed = closed | (band_block == block)
        vpos = jnp.where(lane % NV == n, block * BLK, vpos)
    vpos = vpos + (lane // NV) * 2 - base
    parts = mine.shape[0] * NV // HEAD
    mask_at = [
        jnp.concatenate([vpos + (m * (2 * HEAD // NV) + side) for m in range(parts)], axis=1)
        for side in (core, 1 - core)
    ]
    query = iota((rows, 1), 0)
    mask_mine = mask_at[0] <= query
    mask_other = mask_at[1] <= query
    k1 = mine[:, :NV].reshape(-1, HEAD)
    v1 = mine[:, NV : 2 * NV].reshape(-1, HEAD)
    k2 = other[:, :NV].reshape(-1, HEAD)
    v2 = other[:, NV : 2 * NV].reshape(-1, HEAD)
    at = iota((band, 1), 0)
    k_of = at % BLK
    source = (k_of // 2) * 8 + core * 4 + (at // BLK % 2) * 2 + at // rows
    from_mine = jnp.where(k_of % 2 == core, source, -1)
    from_other = jnp.where(k_of % 2 == core, -1, source)
    cols = iota((band, band), 1)
    ahead = pick(cols == from_mine, mine[:, 2 * NV :].reshape(-1, HEAD)) + pick(
        cols == from_other, other[:, 2 * NV :].reshape(-1, HEAD)
    )
    for move in moves[:5]:
        move.wait()
    kb = jnp.concatenate([ahead[:rows], keys[...]], axis=0)
    vb = jnp.concatenate([ahead[rows:], values[...]], axis=0)
    lag = rows - iota((heads, band), 1)
    table = jnp.zeros((heads, band), F32)
    offs = offsets[...]
    for k in range(offs.shape[1]):
        table = jnp.where(offs[:, k : k + 1] == lag, 1.0, table)
    low = -jnp.inf
    factor = math.log2(math.e) / math.sqrt(HEAD)
    done = []
    for h in range(heads):
        qh = q[:, h * HEAD : (h + 1) * HEAD]
        spread = jnp.broadcast_to(table[h : h + 1], (rows, band))
        slash = pltpu.roll(spread, 0, 1, stride=1, stride_axis=0)
        mask_band = (slash > 0.5) & jnp.logical_not(closed)
        s0 = jnp.where(mask_band, dot_t(qh, kb), low)
        s1 = jnp.where(mask_mine, dot_t(qh, k1), low)
        s2 = jnp.where(mask_other, dot_t(qh, k2), low)
        top = jnp.maximum(
            jnp.maximum(jnp.max(s1, axis=1, keepdims=True), jnp.max(s2, axis=1, keepdims=True)),
            jnp.max(s0, axis=1, keepdims=True),
        )
        p0 = jnp.exp2((s0 - top) * factor)
        p1 = jnp.exp2((s1 - top) * factor)
        p2 = jnp.exp2((s2 - top) * factor)
        total = (
            jnp.sum(p0, axis=1, keepdims=True)
            + jnp.sum(p1, axis=1, keepdims=True)
            + jnp.sum(p2, axis=1, keepdims=True)
        )
        o = jnp.dot(p0.astype(BF16), vb, preferred_element_type=F32)
        o += jnp.dot(p1.astype(BF16), v1, preferred_element_type=F32)
        o += jnp.dot(p2.astype(BF16), v2, preferred_element_type=F32)
        done.append((o / total).astype(BF16))
    lanes = rows * heads
    spread = iota((order.shape[1], lanes), 0) == iota((order.shape[1], lanes), 1) // (2 * heads)
    target = jnp.dot(
        order[...].astype(F32).astype(BF16),
        jnp.where(spread, 1.0, 0.0).astype(BF16),
        preferred_element_type=F32,
    ).astype(jnp.int32)
    row = iota((1, lanes), 1)
    target = target * 2 + row % 2 + (row // 2 % heads) * rows
    one_hot = jnp.where(iota((lanes, lanes), 0) == target, 1.0, 0.0).astype(BF16)
    moved = lax.dot_general(
        one_hot,
        jnp.concatenate(done, axis=0),
        (((0,), (0,)), ((), ())),
        preferred_element_type=F32,
    ).astype(BF16)
    out[...] = moved.reshape(out.shape)
    moves[5].wait()


def project_kernel(arrived, weight, out):
    heads = arrived.shape[1] // 2
    rows = out.shape[1]
    held = arrived[...].reshape(-1, HEAD)
    row = iota((rows, 1), 0)
    at = iota((rows, rows * heads), 1)
    full = jnp.concatenate(
        [pick(at == (row // 2) * (2 * heads) + h * 2 + row % 2, held) for h in range(heads)], axis=1
    )
    width = out.shape[2]
    for j in range(out.shape[0]):
        out[j] = jnp.dot(
            full, weight[:, j * width : (j + 1) * width], preferred_element_type=F32
        ).astype(BF16)


def local(queries, keys, values, vertical, offsets, send_order, out_weight):
    z_n, x_n, c_n, y_n = (lax.axis_size(a) for a in ("z", "x", "c", "y"))
    rows = queries.shape[0]
    heads = queries.shape[1] // HEAD
    n_ctx = z_n * x_n * c_n
    chips = z_n * x_n
    place = jnp.stack([lax.axis_index(CTX), lax.axis_index("c")]).astype(jnp.int32)

    lanes = jnp.concatenate([keys[:BLK], values[:BLK], keys[BLK:], values[BLK:]], axis=1)
    recv = lax.all_to_all(lanes.reshape(n_ctx, 4, HEAD), CTX, 0, 0, tiled=True)
    picked = pl.pallas_call(
        select_kernel,
        out_shape=jax.ShapeDtypeStruct((chips, 2 * NV + 8, HEAD), BF16),
        in_specs=[SMEM, VMEM],
        out_specs=VMEM,
        name="select_rows",
    )(vertical, recv.reshape(4 * n_ctx, HEAD))
    mine = lax.all_to_all(picked, ("z", "x"), 0, 0, tiled=True)
    other = lax.ppermute(mine, "c", [(0, 1), (1, 0)])

    attended, weight = pl.pallas_call(
        attention_kernel,
        out_shape=[
            jax.ShapeDtypeStruct((n_ctx, 2 * heads, HEAD), BF16),
            jax.ShapeDtypeStruct(out_weight.shape, BF16),
        ],
        in_specs=[SMEM, SMEM] + [HBM] * 6 + [VMEM] * 2,
        out_specs=[VMEM, VMEM],
        scratch_shapes=[
            pltpu.VMEM(queries.shape, BF16),
            pltpu.VMEM(keys.shape, BF16),
            pltpu.VMEM(values.shape, BF16),
            pltpu.VMEM(offsets.shape, jnp.int32),
            pltpu.VMEM(send_order.shape, jnp.int32),
            pltpu.SemaphoreType.DMA((6,)),
        ],
        name="attention",
        compiler_params=pltpu.CompilerParams(vmem_limit_bytes=32 * 1024 * 1024),
    )(place, vertical, queries, keys, values, offsets, send_order, out_weight, mine, other)

    arrived = lax.all_to_all(attended, CTX, 0, 0, tiled=True)
    width = out_weight.shape[1] // y_n
    partial = pl.pallas_call(
        project_kernel,
        out_shape=jax.ShapeDtypeStruct((y_n, rows, width), BF16),
        in_specs=[VMEM, VMEM],
        out_specs=VMEM,
        name="project",
        compiler_params=pltpu.CompilerParams(vmem_limit_bytes=32 * 1024 * 1024),
    )(arrived, weight)
    sums = lax.all_to_all(partial, "y", 0, 0, tiled=True)
    return jnp.sum(sums.astype(F32), axis=0).astype(BF16)


def solution(mesh):
    cut = Mesh(mesh.devices.reshape(8, 4, 2, 8), ("z", "x", "c", "y"))
    placed = (
        P(CTX, "y"),
        P(CTX, "y"),
        P(CTX, "y"),
        P("y", None),
        P("y", None),
        P(CTX, None),
        P("y", None),
    )
    return jax.shard_map(
        local, mesh=cut, in_specs=placed, out_specs=P(CTX, "y"), check_vma=False
    )
```

```python
import math

import jax
import jax.numpy as jnp
from jax import lax
from jax.experimental import pallas as pl
from jax.experimental.pallas import tpu as pltpu
from jax.sharding import Mesh, PartitionSpec as P

HEAD = 128
BLK = 64
NV = 32
CTX = ("z", "x", "c")
VMEM = pl.BlockSpec(memory_space=pltpu.VMEM)
HBM = pl.BlockSpec(memory_space=pltpu.HBM)
F32 = jnp.float32
BF16 = jnp.bfloat16
LOW = -1e30
FACTOR = math.log2(math.e) / math.sqrt(HEAD)
ORDER, VERT, PLACE, CORE = 4, 5, 6, 7


def iota(shape, dim):
    return lax.broadcasted_iota(jnp.int32, shape, dim)


def bits(mask):
    return jnp.where(mask, 1.0, 0.0).astype(BF16)


def pick(mask, rows):
    return jnp.dot(bits(mask), rows, preferred_element_type=F32).astype(BF16)


def pick_t(mask, rows):
    return lax.dot_general(
        bits(mask), rows, (((0,), (0,)), ((), ())), preferred_element_type=F32
    ).astype(BF16)


def dot_t(a, b):
    return lax.dot_general(a, b, (((1,), (1,)), ((), ())), preferred_element_type=F32)


def by_destination(order, rows, heads):
    lanes = rows * heads
    count = rows // 2
    spread = bits(iota((count, lanes), 0) == iota((count, lanes), 1) // (2 * heads))
    piece = jnp.dot(order.astype(F32).astype(BF16), spread, preferred_element_type=F32)
    at = iota((1, lanes), 1)
    target = piece.astype(jnp.int32) * 2 + at % 2 + (at // 2 % heads) * rows
    return iota((lanes, lanes), 0) == target


def head_rows(ref, first, heads):
    return jnp.concatenate(
        [ref[:, (first + h) * HEAD : (first + h + 1) * HEAD] for h in range(heads)], axis=0
    )


def pack_kernel(ints, qkv, out, kv):
    rows = qkv.shape[0]
    heads = qkv.shape[1] // HEAD - 2
    count = rows // 2
    order = ints[ORDER : ORDER + 1, :count]
    kv[...] = qkv[:, heads * HEAD :]
    moved = pick_t(by_destination(order, rows, heads), head_rows(qkv, 0, heads))
    out[:, :8] = moved.reshape(count, 8, HEAD)
    new = iota((8 * count, 1), 0)
    slot = new % 8
    source = jnp.where(slot < 4, (slot % 2) * rows + (slot // 2) * BLK + new // 8, -1)
    kv_rows = jnp.dot(
        bits(iota((8 * count, 2 * rows), 1) == source),
        head_rows(qkv, heads, 2),
        preferred_element_type=F32,
    )
    diagonal = iota((count, count), 0) == iota((count, count), 1)
    number = jnp.sum(jnp.where(diagonal, order.astype(F32), 0.0), axis=1, keepdims=True)
    number = jnp.broadcast_to(number, (count, HEAD)).astype(BF16)
    owner = jnp.where(slot == 4, new // 8, -1)
    numbers = jnp.dot(
        bits(iota((8 * count, count), 1) == owner), number, preferred_element_type=F32
    )
    out[:, 8:] = (kv_rows + numbers).astype(BF16).reshape(count, 8, HEAD)


def split3(x):
    high = x.astype(BF16).astype(F32)
    middle = (x - high).astype(BF16).astype(F32)
    return high, middle, x - high - middle


def band_kernel(ints, qkv, prev, recv, out):
    rows = qkv.shape[0]
    heads = qkv.shape[1] // HEAD - 2
    count = rows // 2
    chips = out.shape[0]
    band = 2 * rows
    vert = ints[VERT : VERT + 1, :]
    ctx = ints[PLACE : PLACE + 1, :1]
    lane = iota((1, 2 * NV), 1)
    block = vert[:, : 2 * NV]
    want = (block // 2) * 8 + (block % 2) * 2 + lane // NV
    held = recv[:, 8:].reshape(8 * count, HEAD)
    picked = pick_t(iota((8 * count, 2 * NV), 0) == want, held)
    closed = jnp.zeros((1, band), F32)
    part = iota((1, band), 1) // BLK
    for j in range(band // BLK):
        number = ctx * (rows // BLK) + (j - rows // BLK)
        hit = jnp.max(jnp.where(vert == number, 1.0, 0.0), axis=1, keepdims=True)
        hit = jnp.where(number < 0, 1.0, hit)
        closed = jnp.where(part == j, hit, closed)
    lag = rows - iota((heads, band), 1)
    table = jnp.zeros((heads, band), F32)
    offs = ints[:heads, :BLK]
    for k in range(BLK):
        table = jnp.where(offs[:, k : k + 1] == lag, 1.0, table)
    kb = jnp.concatenate([prev[:, :HEAD], qkv[:, heads * HEAD : (heads + 1) * HEAD]], axis=0)
    vb = jnp.concatenate([prev[:, HEAD:], qkv[:, (heads + 1) * HEAD :]], axis=0)
    lanes = iota((rows, HEAD), 1) % 8
    done = []
    for h in range(heads):
        spread = jnp.broadcast_to(table[h : h + 1], (rows, band))
        slash = pltpu.roll(spread, 0, 1, stride=1, stride_axis=0)
        mask = (slash > 0.5) & (closed < 0.5)
        s = jnp.where(mask, dot_t(qkv[:, h * HEAD : (h + 1) * HEAD], kb), LOW)
        top = jnp.max(s, axis=1, keepdims=True)
        p = jnp.where(mask, jnp.exp2((s - top) * FACTOR), 0.0)
        total = jnp.sum(p, axis=1, keepdims=True)
        o = jnp.dot(p.astype(BF16), vb, preferred_element_type=F32)
        o = o / jnp.where(total > 0.0, total, 1.0)
        sums = jnp.zeros((rows, HEAD), F32)
        for j, term in enumerate(split3(top) + split3(total)):
            sums = jnp.where(lanes == j, term, sums)
        done.append(jnp.concatenate([o.astype(BF16), sums.astype(BF16)], axis=1))
    order = ints[ORDER : ORDER + 1, :count]
    moved = pick_t(by_destination(order, rows, heads), jnp.concatenate(done, axis=0))
    size = 8 * count
    own = iota((size, HEAD), 1) // 8 == iota((size, HEAD), 0) % 8
    sums = jnp.where(own, moved[:, HEAD:].astype(F32), 0.0).astype(BF16)
    new = iota((8 * chips, 1), 0)
    owner = jnp.where(new % 8 < 2, (new // 8) * 2 + new % 8, -1)
    sums = pick(iota((8 * chips, size), 1) // 8 == owner, sums)
    out[:, 2 * NV : 2 * NV + 16] = moved[:, :HEAD].reshape(chips, 16, HEAD)
    out[:, 2 * NV + 16 :] = sums.reshape(chips, 8, HEAD)
    for chip in range(chips):
        out[chip, : 2 * NV] = picked


def finish_kernel(ints, recv, mine, other, weight_in, out, weight, sem):
    move = pltpu.make_async_copy(weight_in, weight, sem)
    move.start()
    count = recv.shape[0]
    chips = mine.shape[0]
    size = 8 * count
    rows = out.shape[1]
    heads = size // rows
    vert = ints[VERT : VERT + 1, :]
    core = ints[CORE : CORE + 1, :1]
    first = core == 0
    vpos = vert * BLK + (iota((1, HEAD), 1) // NV) * 2
    step = 2 * HEAD // NV
    parts = chips * NV // HEAD
    pos_mine = jnp.concatenate([vpos + core + m * step for m in range(parts)], axis=1)
    pos_other = jnp.concatenate([vpos + (1 - core) + m * step for m in range(parts)], axis=1)
    slot = iota((count, 8, HEAD), 1)
    number = jnp.sum(
        jnp.where(slot == 4, recv[:, 8:].astype(F32), 0.0), axis=1, keepdims=True
    )
    number = jnp.broadcast_to(number, (count, 8, HEAD)).reshape(size, HEAD)[:, :1]
    at = iota((size, 1), 0)
    qpos = (at // 8) * rows + number.astype(jnp.int32) * 2 + at % 2

    def by_owner(cut):
        a, b = cut(mine), cut(other)
        return jnp.concatenate([jnp.where(first, a, b), jnp.where(first, b, a)], axis=1)

    base = 2 * NV

    def slash_rows(ref):
        return jnp.where(
            first, ref[:, base : base + 8].astype(F32), ref[:, base + 8 : base + 16].astype(F32)
        )

    def sums_row(ref):
        tail = ref[:, base + 16 :].astype(F32)
        which = iota(tail.shape, 1)
        row = jnp.sum(jnp.where(which == core, tail, 0.0), axis=1, keepdims=True)
        return jnp.broadcast_to(row, tail.shape)

    slash = by_owner(slash_rows).reshape(size, HEAD)
    sums = by_owner(sums_row).reshape(size, HEAD)
    lane = iota((size, HEAD), 1)
    own = lane // 8 == iota((size, HEAD), 0) % 8
    top_b = jnp.sum(jnp.where(own & (lane % 8 < 3), sums, 0.0), axis=1, keepdims=True)
    total_b = jnp.sum(jnp.where(own & (lane % 8 >= 3), sums, 0.0), axis=1, keepdims=True)

    q = recv[:, :8].reshape(size, HEAD)
    k1 = mine[:, :NV].reshape(-1, HEAD)
    v1 = mine[:, NV : 2 * NV].reshape(-1, HEAD)
    k2 = other[:, :NV].reshape(-1, HEAD)
    v2 = other[:, NV : 2 * NV].reshape(-1, HEAD)
    done = []
    for b in range(heads):
        cut = slice(b * rows, (b + 1) * rows)
        s1 = jnp.where(pos_mine <= qpos[cut], dot_t(q[cut], k1), -jnp.inf)
        s2 = jnp.where(pos_other <= qpos[cut], dot_t(q[cut], k2), -jnp.inf)
        top = jnp.maximum(jnp.max(s1, axis=1, keepdims=True), jnp.max(s2, axis=1, keepdims=True))
        top = jnp.maximum(top, top_b[cut])
        p1 = jnp.exp2((s1 - top) * FACTOR)
        p2 = jnp.exp2((s2 - top) * FACTOR)
        share = total_b[cut] * jnp.exp2((top_b[cut] - top) * FACTOR)
        total = jnp.sum(p1, axis=1, keepdims=True) + jnp.sum(p2, axis=1, keepdims=True) + share
        o = jnp.dot(p1.astype(BF16), v1, preferred_element_type=F32)
        o += jnp.dot(p2.astype(BF16), v2, preferred_element_type=F32)
        o += share * slash[cut]
        done.append((o / total).astype(BF16))
    attended = jnp.concatenate(done, axis=0)
    row = iota((rows, 1), 0)
    cols = iota((rows, size), 1)
    full = jnp.concatenate(
        [pick(cols == (row // 2) * 8 + h * 2 + row % 2, attended) for h in range(heads)], axis=1
    )
    width = out.shape[2]
    move.wait()
    for j in range(out.shape[0]):
        out[j] = jnp.dot(
            full, weight[:, j * width : (j + 1) * width], preferred_element_type=F32
        ).astype(BF16)


def local(queries, keys, values, vertical, offsets, send_order, out_weight):
    z_n, x_n, c_n, y_n = (lax.axis_size(a) for a in ("z", "x", "c", "y"))
    rows = queries.shape[0]
    n_ctx = z_n * x_n * c_n
    chips = z_n * x_n
    params = pltpu.CompilerParams(vmem_limit_bytes=50 * 1024 * 1024)

    qkv = jnp.concatenate([queries, keys, values], axis=1)
    pad = ((0, 0), (0, HEAD - offsets.shape[1]))
    ints = jnp.concatenate(
        [
            jnp.pad(offsets, pad),
            jnp.pad(send_order, pad),
            jnp.tile(vertical, (1, HEAD // NV)),
            jnp.full((1, HEAD), lax.axis_index(CTX), jnp.int32),
            jnp.full((1, HEAD), lax.axis_index("c"), jnp.int32),
        ],
        axis=0,
    )
    packed, kv = pl.pallas_call(
        pack_kernel,
        out_shape=[
            jax.ShapeDtypeStruct((n_ctx, 16, HEAD), BF16),
            jax.ShapeDtypeStruct((rows, 2 * HEAD), BF16),
        ],
        in_specs=[VMEM, VMEM],
        out_specs=[VMEM, VMEM],
        name="pack",
    )(ints, qkv)
    prev = lax.ppermute(kv, CTX, [(i, i + 1) for i in range(n_ctx - 1)])
    recv = lax.all_to_all(packed, CTX, 0, 0, tiled=True)
    parts = pl.pallas_call(
        band_kernel,
        out_shape=jax.ShapeDtypeStruct((chips, 2 * NV + 24, HEAD), BF16),
        in_specs=[VMEM] * 4,
        out_specs=VMEM,
        name="slash",
        compiler_params=pltpu.CompilerParams(vmem_limit_bytes=32 * 1024 * 1024),
    )(ints, qkv, prev, recv)
    mine = lax.all_to_all(parts, ("z", "x"), 0, 0, tiled=True)
    other = lax.ppermute(mine, "c", [(0, 1), (1, 0)])
    width = out_weight.shape[1] // y_n
    partial = pl.pallas_call(
        finish_kernel,
        out_shape=jax.ShapeDtypeStruct((y_n, rows, width), BF16),
        in_specs=[VMEM] * 4 + [HBM],
        out_specs=VMEM,
        scratch_shapes=[pltpu.VMEM(out_weight.shape, BF16), pltpu.SemaphoreType.DMA],
        name="finish",
        compiler_params=params,
    )(ints, recv, mine, other, out_weight)
    sums = lax.all_to_all(partial, "y", 0, 0, tiled=True)
    return jnp.sum(sums.astype(F32), axis=0).astype(BF16)


def solution(mesh):
    cut = Mesh(mesh.devices.reshape(8, 4, 2, 8), ("z", "x", "c", "y"))
    placed = (
        P(CTX, "y"),
        P(CTX, "y"),
        P(CTX, "y"),
        P("y", None),
        P("y", None),
        P(CTX, None),
        P("y", None),
    )
    return jax.shard_map(
        local, mesh=cut, in_specs=placed, out_specs=P(CTX, "y"), check_vma=False
    )
```

```python
import math

import jax
import jax.numpy as jnp
from jax import lax
from jax.experimental import pallas as pl
from jax.experimental.pallas import tpu as pltpu
from jax.sharding import Mesh, PartitionSpec as P

HEAD = 128
BLK = 64
NV = 32
CTX = ("z", "x", "c")
VMEM = pl.BlockSpec(memory_space=pltpu.VMEM)
HBM = pl.BlockSpec(memory_space=pltpu.HBM)
F32 = jnp.float32
BF16 = jnp.bfloat16
LOW = -1e30
FACTOR = math.log2(math.e) / math.sqrt(HEAD)
SMEM = pl.BlockSpec(memory_space=pltpu.SMEM)
MIB = 1024 * 1024
VERT, WANT, CORE = 0, 1, 2


def iota(shape, dim):
    return lax.broadcasted_iota(jnp.int32, shape, dim)


def bits(mask):
    return jnp.where(mask, 1.0, 0.0).astype(BF16)


def pick(mask, rows):
    return jnp.dot(bits(mask), rows, preferred_element_type=F32).astype(BF16)


def pick_t(mask, rows):
    return lax.dot_general(
        bits(mask), rows, (((0,), (0,)), ((), ())), preferred_element_type=F32
    ).astype(BF16)


def dot_t(a, b):
    return lax.dot_general(a, b, (((1,), (1,)), ((), ())), preferred_element_type=F32)


def by_destination(order, rows, heads):
    lanes = rows * heads
    count = rows // 2
    spread = bits(iota((count, lanes), 0) == iota((count, lanes), 1) // (2 * heads))
    piece = jnp.dot(order.astype(F32).astype(BF16), spread, preferred_element_type=F32)
    at = iota((1, lanes), 1)
    target = piece.astype(jnp.int32) * 2 + at % 2 + (at // 2 % heads) * rows
    return iota((lanes, lanes), 0) == target


def head_rows(ref, heads):
    return jnp.concatenate([ref[:, h * HEAD : (h + 1) * HEAD] for h in range(heads)], axis=0)


def load(pairs, sems):
    moves = [pltpu.make_async_copy(a, b, sems.at[i]) for i, (a, b) in enumerate(pairs)]
    for move in moves:
        move.start()
    for move in moves:
        move.wait()


def pack_kernel(q_in, keys_in, values_in, order_in, out, kv, q, keys, values, order, sems):
    load([(q_in, q), (keys_in, keys), (values_in, values), (order_in, order)], sems)
    rows = q.shape[0]
    heads = q.shape[1] // HEAD
    count = rows // 2
    kv[:, :HEAD] = keys[...]
    kv[:, HEAD:] = values[...]
    moved = pick_t(by_destination(order[...], rows, heads), head_rows(q, heads))
    out[:, :8] = moved.reshape(count, 8, HEAD)
    new = iota((8 * count, 1), 0)
    slot = new % 8
    source = jnp.where(slot < 4, (slot % 2) * rows + (slot // 2) * BLK + new // 8, -1)
    kv_rows = jnp.dot(
        bits(iota((8 * count, 2 * rows), 1) == source),
        jnp.concatenate([keys[...], values[...]], axis=0),
        preferred_element_type=F32,
    )
    diagonal = iota((count, count), 0) == iota((count, count), 1)
    number = jnp.sum(jnp.where(diagonal, order[...].astype(F32), 0.0), axis=1, keepdims=True)
    number = jnp.broadcast_to(number, (count, HEAD)).astype(BF16)
    owner = jnp.where(slot == 4, new // 8, -1)
    numbers = jnp.dot(
        bits(iota((8 * count, count), 1) == owner), number, preferred_element_type=F32
    )
    out[:, 8:] = (kv_rows + numbers).astype(BF16).reshape(count, 8, HEAD)


def split3(x):
    high = x.astype(BF16).astype(F32)
    middle = (x - high).astype(BF16).astype(F32)
    return high, middle, x - high - middle


def band_kernel(
    place, q_in, keys_in, values_in, order_in, offsets_in, vert_in, prev_in, out, ints,
    q, keys, values, order, offsets, vertical, prev, sems,
):
    load(
        [(q_in, q), (keys_in, keys), (values_in, values), (order_in, order), (offsets_in, offsets), (vert_in, vertical), (prev_in, prev)],
        sems,
    )
    rows = q.shape[0]
    heads = q.shape[1] // HEAD
    count = rows // 2
    chips = out.shape[0]
    band = 2 * rows
    ctx, core = place[0], place[1]
    spread = bits(iota((NV, HEAD), 0) == iota((NV, HEAD), 1) % NV)
    vert = jnp.dot(
        vertical[...].astype(F32).astype(BF16), spread, preferred_element_type=F32
    ).astype(jnp.int32)
    table_row = iota(ints.shape, 0)
    want = (vert // 2) * 8 + (vert % 2) * 2 + iota((1, HEAD), 1) // NV
    ints[...] = jnp.where(
        table_row == VERT, vert, jnp.where(table_row == WANT, want, jnp.where(table_row == CORE, core, 0))
    )
    closed = jnp.zeros((1, band), F32)
    part = iota((1, band), 1) // BLK
    for j in range(band // BLK):
        number = ctx * (rows // BLK) + (j - rows // BLK)
        hit = jnp.max(jnp.where(vert == number, 1.0, 0.0), axis=1, keepdims=True)
        hit = jnp.where(number < 0, 1.0, hit)
        closed = jnp.where(part == j, hit, closed)
    lag = rows - iota((heads, band), 1)
    table = jnp.zeros((heads, band), F32)
    offs = offsets[...]
    for k in range(offs.shape[1]):
        table = jnp.where(offs[:, k : k + 1] == lag, 1.0, table)
    kb = jnp.concatenate([prev[:, :HEAD], keys[...]], axis=0)
    vb = jnp.concatenate([prev[:, HEAD:], values[...]], axis=0)
    lanes = iota((rows, HEAD), 1) % 8
    done = []
    for h in range(heads):
        spread = jnp.broadcast_to(table[h : h + 1], (rows, band))
        slash = pltpu.roll(spread, 0, 1, stride=1, stride_axis=0)
        mask = (slash > 0.5) & (closed < 0.5)
        s = jnp.where(mask, dot_t(q[:, h * HEAD : (h + 1) * HEAD], kb), LOW)
        top = jnp.max(s, axis=1, keepdims=True)
        p = jnp.where(mask, jnp.exp2((s - top) * FACTOR), 0.0)
        total = jnp.sum(p, axis=1, keepdims=True)
        o = jnp.dot(p.astype(BF16), vb, preferred_element_type=F32)
        o = o / jnp.where(total > 0.0, total, 1.0)
        sums = jnp.zeros((rows, HEAD), F32)
        for j, term in enumerate(split3(top) + split3(total)):
            sums = jnp.where(lanes == j, term, sums)
        done.append(jnp.concatenate([o.astype(BF16), sums.astype(BF16)], axis=1))
    moved = pick_t(by_destination(order[...], rows, heads), jnp.concatenate(done, axis=0))
    size = 8 * count
    own = iota((size, HEAD), 1) // 8 == iota((size, HEAD), 0) % 8
    sums = jnp.where(own, moved[:, HEAD:].astype(F32), 0.0).astype(BF16)
    new = iota((8 * chips, 1), 0)
    owner = jnp.where(new % 8 < 2, (new // 8) * 2 + new % 8, -1)
    sums = pick(iota((8 * chips, size), 1) // 8 == owner, sums)
    out[:, :16] = moved[:, :HEAD].reshape(chips, 16, HEAD)
    out[:, 16:] = sums.reshape(chips, 8, HEAD)


def select_kernel(ints, recv, slash, out, kept):
    kept[...] = ints[...]
    want = ints[WANT : WANT + 1, : 2 * NV]
    held = recv[:, 8:].reshape(-1, HEAD)
    picked = pick_t(iota((held.shape[0], 2 * NV), 0) == want, held)
    out[:, 2 * NV :] = slash[...]
    for chip in range(out.shape[0]):
        out[chip, : 2 * NV] = picked


def key_positions(ints, core, chips):
    vpos = ints[VERT : VERT + 1, :] * BLK + (iota((1, HEAD), 1) // NV) * 2 + core
    step = 2 * HEAD // NV
    return jnp.concatenate([vpos + m * step for m in range(chips * NV // HEAD)], axis=1)


def row_positions(recv, rows):
    tail = recv[:, 8:].astype(F32)
    size = 8 * tail.shape[0]
    number = jnp.sum(jnp.where(iota(tail.shape, 1) == 4, tail, 0.0), axis=1, keepdims=True)
    number = jnp.broadcast_to(number, tail.shape).reshape(size, HEAD)[:, :1]
    at = iota((size, 1), 0)
    return (at // 8) * rows + number.astype(jnp.int32) * 2 + at % 2


def half_kernel(ints, recv, mine, out):
    core = ints[CORE : CORE + 1, :1]
    size = out.shape[0]
    rows = 2 * recv.shape[0]
    pos = key_positions(ints, core, mine.shape[0])
    qpos = row_positions(recv, rows)
    q = recv[:, :8].reshape(size, HEAD)
    keys = mine[:, :NV].reshape(-1, HEAD)
    vals = mine[:, NV : 2 * NV].reshape(-1, HEAD)
    lane = iota((rows, HEAD), 1)
    for b in range(size // rows):
        cut = slice(b * rows, (b + 1) * rows)
        s = jnp.where(pos <= qpos[cut], dot_t(q[cut], keys), -jnp.inf)
        top = jnp.maximum(jnp.max(s, axis=1, keepdims=True), LOW)
        p = jnp.exp2((s - top) * FACTOR)
        total = jnp.sum(p, axis=1, keepdims=True)
        out[cut, :HEAD] = jnp.dot(p.astype(BF16), vals, preferred_element_type=F32)
        out[cut, HEAD:] = jnp.where(lane == 0, top, total)


def finish_kernel(ints, recv, mine, other, half, weight_in, out, weight, sem):
    move = pltpu.make_async_copy(weight_in, weight, sem)
    move.start()
    count = recv.shape[0]
    size = 8 * count
    rows = out.shape[1]
    heads = size // rows
    core = ints[CORE : CORE + 1, :1]
    first = core == 0
    pos = key_positions(ints, 1 - core, mine.shape[0])
    qpos = row_positions(recv, rows)

    def by_owner(cut):
        a, b = cut(mine), cut(other)
        return jnp.concatenate([jnp.where(first, a, b), jnp.where(first, b, a)], axis=1)

    base = 2 * NV

    def slash_rows(ref):
        return jnp.where(
            first, ref[:, base : base + 8].astype(F32), ref[:, base + 8 : base + 16].astype(F32)
        )

    def sums_row(ref):
        tail = ref[:, base + 16 :].astype(F32)
        which = iota(tail.shape, 1)
        row = jnp.sum(jnp.where(which == core, tail, 0.0), axis=1, keepdims=True)
        return jnp.broadcast_to(row, tail.shape)

    slash = by_owner(slash_rows).reshape(size, HEAD)
    sums = by_owner(sums_row).reshape(size, HEAD)
    lane = iota((size, HEAD), 1)
    own = lane // 8 == iota((size, HEAD), 0) % 8
    top_b = jnp.sum(jnp.where(own & (lane % 8 < 3), sums, 0.0), axis=1, keepdims=True)
    total_b = jnp.sum(jnp.where(own & (lane % 8 >= 3), sums, 0.0), axis=1, keepdims=True)

    q = recv[:, :8].reshape(size, HEAD)
    keys = other[:, :NV].reshape(-1, HEAD)
    vals = other[:, NV : 2 * NV].reshape(-1, HEAD)
    done = []
    for b in range(heads):
        cut = slice(b * rows, (b + 1) * rows)
        s = jnp.where(pos <= qpos[cut], dot_t(q[cut], keys), -jnp.inf)
        top_a = half[cut, HEAD : HEAD + 1]
        top = jnp.maximum(jnp.max(s, axis=1, keepdims=True), jnp.maximum(top_a, top_b[cut]))
        p = jnp.exp2((s - top) * FACTOR)
        share_a = jnp.exp2((top_a - top) * FACTOR)
        share_b = total_b[cut] * jnp.exp2((top_b[cut] - top) * FACTOR)
        total = jnp.sum(p, axis=1, keepdims=True) + share_a * half[cut, HEAD + 1 : HEAD + 2] + share_b
        o = jnp.dot(p.astype(BF16), vals, preferred_element_type=F32)
        o += share_a * half[cut, :HEAD] + share_b * slash[cut]
        done.append((o / total).astype(BF16))
    attended = jnp.concatenate(done, axis=0)
    row = iota((rows, 1), 0)
    cols = iota((rows, size), 1)
    full = jnp.concatenate(
        [pick(cols == (row // 2) * 8 + h * 2 + row % 2, attended) for h in range(heads)], axis=1
    )
    width = out.shape[2]
    move.wait()
    for j in range(out.shape[0]):
        out[j] = jnp.dot(
            full, weight[:, j * width : (j + 1) * width], preferred_element_type=F32
        ).astype(BF16)


def local(queries, keys, values, vertical, offsets, send_order, out_weight):
    z_n, x_n, c_n, y_n = (lax.axis_size(a) for a in ("z", "x", "c", "y"))
    rows = queries.shape[0]
    n_ctx = z_n * x_n * c_n
    chips = z_n * x_n
    large = pltpu.CompilerParams(vmem_limit_bytes=60 * MIB)
    small = pltpu.CompilerParams(vmem_limit_bytes=16 * MIB)
    place = jnp.stack([lax.axis_index(CTX), lax.axis_index("c")]).astype(jnp.int32)
    held = [pltpu.VMEM(a.shape, a.dtype) for a in (queries, keys, values, send_order)]

    packed, kv = pl.pallas_call(
        pack_kernel,
        out_shape=[
            jax.ShapeDtypeStruct((n_ctx, 16, HEAD), BF16),
            jax.ShapeDtypeStruct((rows, 2 * HEAD), BF16),
        ],
        in_specs=[HBM] * 4,
        out_specs=[VMEM, VMEM],
        scratch_shapes=held + [pltpu.SemaphoreType.DMA((4,))],
        name="pack",
        compiler_params=large,
    )(queries, keys, values, send_order)
    recv = lax.all_to_all(packed, CTX, 0, 0, tiled=True)
    prev = lax.ppermute(kv, CTX, [(i, i + 1) for i in range(n_ctx - 1)])
    slash, ints = pl.pallas_call(
        band_kernel,
        out_shape=[
            jax.ShapeDtypeStruct((chips, 24, HEAD), BF16),
            jax.ShapeDtypeStruct((8, HEAD), jnp.int32),
        ],
        in_specs=[SMEM] + [HBM] * 7,
        out_specs=[VMEM, VMEM],
        scratch_shapes=held
        + [pltpu.VMEM(a.shape, a.dtype) for a in (offsets, vertical, prev)]
        + [pltpu.SemaphoreType.DMA((7,))],
        name="slash",
        compiler_params=large,
    )(place, queries, keys, values, send_order, offsets, vertical, prev)
    parts, ints = pl.pallas_call(
        select_kernel,
        out_shape=[
            jax.ShapeDtypeStruct((chips, 2 * NV + 24, HEAD), BF16),
            jax.ShapeDtypeStruct(ints.shape, jnp.int32),
        ],
        in_specs=[VMEM] * 3,
        out_specs=[VMEM, VMEM],
        name="select",
        compiler_params=small,
    )(ints, recv, slash)
    mine = lax.all_to_all(parts, ("z", "x"), 0, 0, tiled=True)
    other = lax.ppermute(mine, "c", [(0, 1), (1, 0)])
    half = pl.pallas_call(
        half_kernel,
        out_shape=jax.ShapeDtypeStruct((8 * n_ctx, 2 * HEAD), F32),
        in_specs=[VMEM] * 3,
        out_specs=VMEM,
        name="half",
        compiler_params=pltpu.CompilerParams(vmem_limit_bytes=32 * MIB),
        cost_estimate=pl.CostEstimate(flops=300000000, bytes_accessed=2000000, transcendentals=500000),
    )(ints, recv, mine)
    width = out_weight.shape[1] // y_n
    partial = pl.pallas_call(
        finish_kernel,
        out_shape=jax.ShapeDtypeStruct((y_n, rows, width), BF16),
        in_specs=[VMEM] * 5 + [HBM],
        out_specs=VMEM,
        scratch_shapes=[pltpu.VMEM(out_weight.shape, BF16), pltpu.SemaphoreType.DMA],
        name="finish",
        compiler_params=pltpu.CompilerParams(vmem_limit_bytes=50 * MIB),
    )(ints, recv, mine, other, half, out_weight)
    sums = lax.all_to_all(partial, "y", 0, 0, tiled=True)
    return jnp.sum(sums.astype(F32), axis=0).astype(BF16)


def solution(mesh):
    cut = Mesh(mesh.devices.reshape(8, 4, 2, 8), ("z", "x", "c", "y"))
    placed = (
        P(CTX, "y"),
        P(CTX, "y"),
        P(CTX, "y"),
        P("y", None),
        P("y", None),
        P(CTX, None),
        P("y", None),
    )
    return jax.shard_map(
        local, mesh=cut, in_specs=placed, out_specs=P(CTX, "y"), check_vma=False
    )
```

```python
import math

import jax
import jax.numpy as jnp
from jax import lax
from jax.experimental import pallas as pl
from jax.experimental.pallas import tpu as pltpu
from jax.sharding import Mesh, PartitionSpec as P

HEAD = 128
BLK = 64
NV = 32
CTX = ("z", "x", "c")
Y = ("yh", "yl")
VMEM = pl.BlockSpec(memory_space=pltpu.VMEM)
HBM = pl.BlockSpec(memory_space=pltpu.HBM)
F32 = jnp.float32
BF16 = jnp.bfloat16
LOW = -1e30
FACTOR = math.log2(math.e) / math.sqrt(HEAD)
MIB = 1024 * 1024
VERT, WANT, CORE = 0, 1, 2


def iota(shape, dim):
    return lax.broadcasted_iota(jnp.int32, shape, dim)


def bits(mask):
    return jnp.where(mask, 1.0, 0.0).astype(BF16)


def pick(mask, rows):
    return jnp.dot(bits(mask), rows, preferred_element_type=F32).astype(BF16)


def pick_t(mask, rows):
    return lax.dot_general(
        bits(mask), rows, (((0,), (0,)), ((), ())), preferred_element_type=F32
    ).astype(BF16)


def dot_t(a, b):
    return lax.dot_general(a, b, (((1,), (1,)), ((), ())), preferred_element_type=F32)


def by_destination(order, rows, heads):
    lanes = rows * heads
    count = rows // 2
    spread = bits(iota((count, lanes), 0) == iota((count, lanes), 1) // (2 * heads))
    piece = jnp.dot(order.astype(F32).astype(BF16), spread, preferred_element_type=F32)
    at = iota((1, lanes), 1)
    target = piece.astype(jnp.int32) * 2 + at % 2 + (at // 2 % heads) * rows
    return iota((lanes, lanes), 0) == target


def head_rows(ref, heads):
    return jnp.concatenate([ref[:, h * HEAD : (h + 1) * HEAD] for h in range(heads)], axis=0)


def load(pairs, sems):
    moves = [pltpu.make_async_copy(a, b, sems.at[i]) for i, (a, b) in enumerate(pairs)]
    for move in moves:
        move.start()
    for move in moves:
        move.wait()


def columns(ref, j, parity):
    width = ref.shape[1] // 8
    start = pl.multiple_of((2 * j + parity) * width, width)
    return ref.at[:, pl.ds(start, width)]


def pack_kernel(
    q_in, keys_in, values_in, order_in, weight_in, out, kv, sent, q, keys, values, order, sems, wsems
):
    load([(q_in, q), (keys_in, keys), (values_in, values), (order_in, order)], sems)
    parity = lax.axis_index("yl")
    moves = [
        pltpu.make_async_copy(columns(weight_in, j, 1 - parity), sent.at[j], wsems.at[j])
        for j in range(sent.shape[0])
    ]
    for move in moves:
        move.start()
    rows = q.shape[0]
    heads = q.shape[1] // HEAD
    count = rows // 2
    kv[:, :HEAD] = keys[...]
    kv[:, HEAD:] = values[...]
    moved = pick_t(by_destination(order[...], rows, heads), head_rows(q, heads))
    out[:, :8] = moved.reshape(count, 8, HEAD)
    new = iota((8 * count, 1), 0)
    slot = new % 8
    source = jnp.where(slot < 4, (slot % 2) * rows + (slot // 2) * BLK + new // 8, -1)
    kv_rows = jnp.dot(
        bits(iota((8 * count, 2 * rows), 1) == source),
        jnp.concatenate([keys[...], values[...]], axis=0),
        preferred_element_type=F32,
    )
    diagonal = iota((count, count), 0) == iota((count, count), 1)
    number = jnp.sum(jnp.where(diagonal, order[...].astype(F32), 0.0), axis=1, keepdims=True)
    number = jnp.broadcast_to(number, (count, HEAD)).astype(BF16)
    owner = jnp.where(slot == 4, new // 8, -1)
    numbers = jnp.dot(
        bits(iota((8 * count, count), 1) == owner), number, preferred_element_type=F32
    )
    out[:, 8:] = (kv_rows + numbers).astype(BF16).reshape(count, 8, HEAD)
    for move in moves:
        move.wait()


def split3(x):
    high = x.astype(BF16).astype(F32)
    middle = (x - high).astype(BF16).astype(F32)
    return high, middle, x - high - middle


def band_kernel(
    q_in, keys_in, values_in, order_in, offsets_in, vert_in, prev_in, out, ints,
    q, keys, values, order, offsets, vertical, prev, sems,
):
    load(
        [(q_in, q), (keys_in, keys), (values_in, values), (order_in, order), (offsets_in, offsets), (vert_in, vertical), (prev_in, prev)],
        sems,
    )
    rows = q.shape[0]
    heads = q.shape[1] // HEAD
    count = rows // 2
    chips = out.shape[0]
    band = 2 * rows
    ctx, core = lax.axis_index(CTX), lax.axis_index("c")
    spread = bits(iota((NV, HEAD), 0) == iota((NV, HEAD), 1) % NV)
    vert = jnp.dot(
        vertical[...].astype(F32).astype(BF16), spread, preferred_element_type=F32
    ).astype(jnp.int32)
    table_row = iota(ints.shape, 0)
    want = (vert // 2) * 8 + (vert % 2) * 2 + iota((1, HEAD), 1) // NV
    ints[...] = jnp.where(
        table_row == VERT, vert, jnp.where(table_row == WANT, want, jnp.where(table_row == CORE, core, 0))
    )
    closed = jnp.zeros((1, band), F32)
    part = iota((1, band), 1) // BLK
    for j in range(band // BLK):
        number = ctx * (rows // BLK) + (j - rows // BLK)
        hit = jnp.max(jnp.where(vert == number, 1.0, 0.0), axis=1, keepdims=True)
        hit = jnp.where(number < 0, 1.0, hit)
        closed = jnp.where(part == j, hit, closed)
    lag = rows - iota((heads, band), 1)
    table = jnp.zeros((heads, band), F32)
    offs = offsets[...]
    for k in range(offs.shape[1]):
        table = jnp.where(offs[:, k : k + 1] == lag, 1.0, table)
    kb = jnp.concatenate([prev[:, :HEAD], keys[...]], axis=0)
    vb = jnp.concatenate([prev[:, HEAD:], values[...]], axis=0)
    lanes = iota((rows, HEAD), 1) % 8
    done = []
    for h in range(heads):
        spread = jnp.broadcast_to(table[h : h + 1], (rows, band))
        slash = pltpu.roll(spread, 0, 1, stride=1, stride_axis=0)
        mask = (slash > 0.5) & (closed < 0.5)
        s = jnp.where(mask, dot_t(q[:, h * HEAD : (h + 1) * HEAD], kb), LOW)
        top = jnp.max(s, axis=1, keepdims=True)
        p = jnp.where(mask, jnp.exp2((s - top) * FACTOR), 0.0)
        total = jnp.sum(p, axis=1, keepdims=True)
        o = jnp.dot(p.astype(BF16), vb, preferred_element_type=F32)
        o = o / jnp.where(total > 0.0, total, 1.0)
        sums = jnp.zeros((rows, HEAD), F32)
        for j, term in enumerate(split3(top) + split3(total)):
            sums = jnp.where(lanes == j, term, sums)
        done.append(jnp.concatenate([o.astype(BF16), sums.astype(BF16)], axis=1))
    moved = pick_t(by_destination(order[...], rows, heads), jnp.concatenate(done, axis=0))
    size = 8 * count
    own = iota((size, HEAD), 1) // 8 == iota((size, HEAD), 0) % 8
    sums = jnp.where(own, moved[:, HEAD:].astype(F32), 0.0).astype(BF16)
    new = iota((8 * chips, 1), 0)
    owner = jnp.where(new % 8 < 2, (new // 8) * 2 + new % 8, -1)
    sums = pick(iota((8 * chips, size), 1) // 8 == owner, sums)
    out[:, :16] = moved[:, :HEAD].reshape(chips, 16, HEAD)
    out[:, 16:] = sums.reshape(chips, 8, HEAD)


def select_kernel(ints, recv, slash, out, kept):
    kept[...] = ints[...]
    want = ints[WANT : WANT + 1, : 2 * NV]
    held = recv[:, 8:].reshape(-1, HEAD)
    picked = pick_t(iota((held.shape[0], 2 * NV), 0) == want, held)
    out[:, 2 * NV :] = slash[...]
    for chip in range(out.shape[0]):
        out[chip, : 2 * NV] = picked


def key_positions(ints, core, chips):
    vpos = ints[VERT : VERT + 1, :] * BLK + (iota((1, HEAD), 1) // NV) * 2 + core
    step = 2 * HEAD // NV
    return jnp.concatenate([vpos + m * step for m in range(chips * NV // HEAD)], axis=1)


def row_positions(recv, rows):
    tail = recv[:, 8:].astype(F32)
    size = 8 * tail.shape[0]
    number = jnp.sum(jnp.where(iota(tail.shape, 1) == 4, tail, 0.0), axis=1, keepdims=True)
    number = jnp.broadcast_to(number, tail.shape).reshape(size, HEAD)[:, :1]
    at = iota((size, 1), 0)
    return (at // 8) * rows + number.astype(jnp.int32) * 2 + at % 2


def half_kernel(ints, recv, mine, out):
    core = ints[CORE : CORE + 1, :1]
    size = out.shape[0]
    rows = 2 * recv.shape[0]
    pos = key_positions(ints, core, mine.shape[0])
    qpos = row_positions(recv, rows)
    q = recv[:, :8].reshape(size, HEAD)
    keys = mine[:, :NV].reshape(-1, HEAD)
    vals = mine[:, NV : 2 * NV].reshape(-1, HEAD)
    lane = iota((rows, HEAD), 1)
    for b in range(size // rows):
        cut = slice(b * rows, (b + 1) * rows)
        s = jnp.where(pos <= qpos[cut], dot_t(q[cut], keys), -jnp.inf)
        top = jnp.maximum(jnp.max(s, axis=1, keepdims=True), LOW)
        p = jnp.exp2((s - top) * FACTOR)
        total = jnp.sum(p, axis=1, keepdims=True)
        out[cut, :HEAD] = jnp.dot(p.astype(BF16), vals, preferred_element_type=F32)
        out[cut, HEAD:] = jnp.where(lane == 0, top, total)


def finish_kernel(ints, recv, mine, other, half, out):
    count = recv.shape[0]
    size = 8 * count
    rows = out.shape[0]
    heads = size // rows
    core = ints[CORE : CORE + 1, :1]
    first = core == 0
    pos = key_positions(ints, 1 - core, mine.shape[0])
    qpos = row_positions(recv, rows)

    def by_owner(cut):
        a, b = cut(mine), cut(other)
        return jnp.concatenate([jnp.where(first, a, b), jnp.where(first, b, a)], axis=1)

    base = 2 * NV

    def slash_rows(ref):
        return jnp.where(
            first, ref[:, base : base + 8].astype(F32), ref[:, base + 8 : base + 16].astype(F32)
        )

    def sums_row(ref):
        tail = ref[:, base + 16 :].astype(F32)
        which = iota(tail.shape, 1)
        row = jnp.sum(jnp.where(which == core, tail, 0.0), axis=1, keepdims=True)
        return jnp.broadcast_to(row, tail.shape)

    slash = by_owner(slash_rows).reshape(size, HEAD)
    sums = by_owner(sums_row).reshape(size, HEAD)
    lane = iota((size, HEAD), 1)
    own = lane // 8 == iota((size, HEAD), 0) % 8
    top_b = jnp.sum(jnp.where(own & (lane % 8 < 3), sums, 0.0), axis=1, keepdims=True)
    total_b = jnp.sum(jnp.where(own & (lane % 8 >= 3), sums, 0.0), axis=1, keepdims=True)

    q = recv[:, :8].reshape(size, HEAD)
    keys = other[:, :NV].reshape(-1, HEAD)
    vals = other[:, NV : 2 * NV].reshape(-1, HEAD)
    done = []
    for b in range(heads):
        cut = slice(b * rows, (b + 1) * rows)
        s = jnp.where(pos <= qpos[cut], dot_t(q[cut], keys), -jnp.inf)
        top_a = half[cut, HEAD : HEAD + 1]
        top = jnp.maximum(jnp.max(s, axis=1, keepdims=True), jnp.maximum(top_a, top_b[cut]))
        p = jnp.exp2((s - top) * FACTOR)
        share_a = jnp.exp2((top_a - top) * FACTOR)
        share_b = total_b[cut] * jnp.exp2((top_b[cut] - top) * FACTOR)
        total = jnp.sum(p, axis=1, keepdims=True) + share_a * half[cut, HEAD + 1 : HEAD + 2] + share_b
        o = jnp.dot(p.astype(BF16), vals, preferred_element_type=F32)
        o += share_a * half[cut, :HEAD] + share_b * slash[cut]
        done.append((o / total).astype(BF16))
    attended = jnp.concatenate(done, axis=0)
    row = iota((rows, 1), 0)
    cols = iota((rows, size), 1)
    for h in range(heads):
        rows_h = pick(cols == (row // 2) * 8 + h * 2 + row % 2, attended)
        out[:, h * HEAD : (h + 1) * HEAD] = rows_h


def own_kernel(full, weight_in, theirs_in, out, theirs, weight, sems):
    n = out.shape[0]
    parity = lax.axis_index("yl")
    moves = [
        pltpu.make_async_copy(columns(weight_in, j, parity), weight.at[j], sems.at[j])
        for j in range(n)
    ]
    late = pltpu.make_async_copy(theirs_in, theirs, sems.at[n])
    for move in moves:
        move.start()
    late.start()
    for j in range(n):
        moves[j].wait()
        out[j] = jnp.dot(full[...], weight[j], preferred_element_type=F32)
    late.wait()


def both_kernel(own, full, weight, out):
    for j in range(out.shape[0]):
        part = own[j] + jnp.dot(full[...], weight[j], preferred_element_type=F32)
        out[j] = part.astype(BF16)


def local(queries, keys, values, vertical, offsets, send_order, out_weight):
    z_n, x_n, c_n, pairs = (lax.axis_size(a) for a in ("z", "x", "c", "yh"))
    rows = queries.shape[0]
    n_ctx = z_n * x_n * c_n
    chips = z_n * x_n
    large = pltpu.CompilerParams(vmem_limit_bytes=60 * MIB)
    small = pltpu.CompilerParams(vmem_limit_bytes=16 * MIB)
    width = out_weight.shape[1] // (2 * pairs)
    quarter = (pairs, out_weight.shape[0], width)
    held = [pltpu.VMEM(a.shape, a.dtype) for a in (queries, keys, values, send_order)]

    packed, kv, sent = pl.pallas_call(
        pack_kernel,
        out_shape=[
            jax.ShapeDtypeStruct((n_ctx, 16, HEAD), BF16),
            jax.ShapeDtypeStruct((rows, 2 * HEAD), BF16),
            jax.ShapeDtypeStruct(quarter, BF16),
        ],
        in_specs=[HBM] * 5,
        out_specs=[VMEM, VMEM, HBM],
        scratch_shapes=held + [pltpu.SemaphoreType.DMA((4,)), pltpu.SemaphoreType.DMA((pairs,))],
        name="pack",
        compiler_params=large,
    )(queries, keys, values, send_order, out_weight)
    recv = lax.all_to_all(packed, CTX, 0, 0, tiled=True)
    prev = lax.ppermute(kv, CTX, [(i, i + 1) for i in range(n_ctx - 1)])
    theirs = lax.ppermute(sent, "yl", [(0, 1), (1, 0)])
    slash, ints = pl.pallas_call(
        band_kernel,
        out_shape=[
            jax.ShapeDtypeStruct((chips, 24, HEAD), BF16),
            jax.ShapeDtypeStruct((8, HEAD), jnp.int32),
        ],
        in_specs=[HBM] * 7,
        out_specs=[VMEM, VMEM],
        scratch_shapes=held
        + [pltpu.VMEM(a.shape, a.dtype) for a in (offsets, vertical, prev)]
        + [pltpu.SemaphoreType.DMA((7,))],
        name="slash",
        compiler_params=large,
    )(queries, keys, values, send_order, offsets, vertical, prev)
    parts, ints = pl.pallas_call(
        select_kernel,
        out_shape=[
            jax.ShapeDtypeStruct((chips, 2 * NV + 24, HEAD), BF16),
            jax.ShapeDtypeStruct(ints.shape, jnp.int32),
        ],
        in_specs=[VMEM] * 3,
        out_specs=[VMEM, VMEM],
        name="select",
        compiler_params=small,
    )(ints, recv, slash)
    mine = lax.all_to_all(parts, ("z", "x"), 0, 0, tiled=True)
    other = lax.ppermute(mine, "c", [(0, 1), (1, 0)])
    half = pl.pallas_call(
        half_kernel,
        out_shape=jax.ShapeDtypeStruct((8 * n_ctx, 2 * HEAD), F32),
        in_specs=[VMEM] * 3,
        out_specs=VMEM,
        name="half",
        compiler_params=pltpu.CompilerParams(vmem_limit_bytes=32 * MIB),
        cost_estimate=pl.CostEstimate(flops=300000000, bytes_accessed=2000000, transcendentals=500000),
    )(ints, recv, mine)
    full = pl.pallas_call(
        finish_kernel,
        out_shape=jax.ShapeDtypeStruct(queries.shape, BF16),
        in_specs=[VMEM] * 5,
        out_specs=VMEM,
        name="finish",
        compiler_params=pltpu.CompilerParams(vmem_limit_bytes=32 * MIB),
    )(ints, recv, mine, other, half)
    theirs_full = lax.ppermute(full, "yl", [(0, 1), (1, 0)])
    own, weight = pl.pallas_call(
        own_kernel,
        out_shape=[
            jax.ShapeDtypeStruct((pairs, rows, width), F32),
            jax.ShapeDtypeStruct(quarter, BF16),
        ],
        in_specs=[VMEM, HBM, HBM],
        out_specs=[VMEM, VMEM],
        scratch_shapes=[pltpu.VMEM(quarter, BF16), pltpu.SemaphoreType.DMA((pairs + 1,))],
        name="project_own",
        compiler_params=pltpu.CompilerParams(vmem_limit_bytes=48 * MIB),
        cost_estimate=pl.CostEstimate(flops=300000000, bytes_accessed=8000000, transcendentals=0),
    )(full, out_weight, theirs)
    partial = pl.pallas_call(
        both_kernel,
        out_shape=jax.ShapeDtypeStruct((pairs, rows, width), BF16),
        in_specs=[VMEM] * 3,
        out_specs=VMEM,
        name="project_both",
        compiler_params=pltpu.CompilerParams(vmem_limit_bytes=32 * MIB),
    )(own, theirs_full, weight)
    sums = lax.all_to_all(partial, "yh", 0, 0, tiled=True)
    return jnp.sum(sums.astype(F32), axis=0).astype(BF16)


def solution(mesh):
    cut = Mesh(mesh.devices.reshape(8, 4, 2, 4, 2), CTX + Y)
    placed = (
        P(CTX, Y),
        P(CTX, Y),
        P(CTX, Y),
        P(Y, None),
        P(Y, None),
        P(CTX, None),
        P(Y, None),
    )
    return jax.shard_map(
        local, mesh=cut, in_specs=placed, out_specs=P(CTX, Y), check_vma=False
    )
```

```python
import math

import jax
import jax.numpy as jnp
from jax import lax
from jax.experimental import pallas as pl
from jax.experimental.pallas import tpu as pltpu
from jax.sharding import Mesh, PartitionSpec as P

HEAD = 128
BLK = 64
NV = 32
CTX = ("z", "x", "c")
Y = ("yh", "yl")
VMEM = pl.BlockSpec(memory_space=pltpu.VMEM)
HBM = pl.BlockSpec(memory_space=pltpu.HBM)
F32 = jnp.float32
BF16 = jnp.bfloat16
LOW = -1e30
FACTOR = math.log2(math.e) / math.sqrt(HEAD)
MIB = 1024 * 1024
VERT, WANT, CORE = 0, 1, 2


def iota(shape, dim):
    return lax.broadcasted_iota(jnp.int32, shape, dim)


def bits(mask):
    return jnp.where(mask, 1.0, 0.0).astype(BF16)


def pick(mask, rows):
    return jnp.dot(bits(mask), rows, preferred_element_type=F32).astype(BF16)


def pick_t(mask, rows):
    return lax.dot_general(
        bits(mask), rows, (((0,), (0,)), ((), ())), preferred_element_type=F32
    ).astype(BF16)


def dot_t(a, b):
    return lax.dot_general(a, b, (((1,), (1,)), ((), ())), preferred_element_type=F32)


def by_destination(order, rows, heads):
    lanes = rows * heads
    count = rows // 2
    spread = bits(iota((count, lanes), 0) == iota((count, lanes), 1) // (2 * heads))
    piece = jnp.dot(order.astype(F32).astype(BF16), spread, preferred_element_type=F32)
    at = iota((1, lanes), 1)
    target = piece.astype(jnp.int32) * 2 + at % 2 + (at // 2 % heads) * rows
    return iota((lanes, lanes), 0) == target


def head_rows(ref, heads):
    return jnp.concatenate([ref[:, h * HEAD : (h + 1) * HEAD] for h in range(heads)], axis=0)


def load(pairs, sems):
    moves = [pltpu.make_async_copy(a, b, sems.at[i]) for i, (a, b) in enumerate(pairs)]
    for move in moves:
        move.start()
    for move in moves:
        move.wait()


def columns(ref, j, parity):
    width = ref.shape[1] // 8
    start = pl.multiple_of((2 * j + parity) * width, width)
    return ref.at[:, pl.ds(start, width)]


def pack_kernel(
    q_in, keys_in, values_in, order_in, weight_in, out, kv, sent, q, keys, values, order, sems, wsems
):
    parity, core = lax.axis_index("yl"), lax.axis_index("c")
    share = sent.shape[0]
    moves = [
        pltpu.make_async_copy(
            columns(weight_in, core * share + j, 1 - parity), sent.at[j], wsems.at[j]
        )
        for j in range(share)
    ]
    for move in moves:
        move.start()
    load([(q_in, q), (keys_in, keys), (values_in, values), (order_in, order)], sems)
    rows = q.shape[0]
    heads = q.shape[1] // HEAD
    count = rows // 2
    kv[:, :HEAD] = keys[...]
    kv[:, HEAD:] = values[...]
    moved = pick_t(by_destination(order[...], rows, heads), head_rows(q, heads))
    out[:, :8] = moved.reshape(count, 8, HEAD)
    new = iota((8 * count, 1), 0)
    slot = new % 8
    source = jnp.where(slot < 4, (slot % 2) * rows + (slot // 2) * BLK + new // 8, -1)
    kv_rows = jnp.dot(
        bits(iota((8 * count, 2 * rows), 1) == source),
        jnp.concatenate([keys[...], values[...]], axis=0),
        preferred_element_type=F32,
    )
    diagonal = iota((count, count), 0) == iota((count, count), 1)
    number = jnp.sum(jnp.where(diagonal, order[...].astype(F32), 0.0), axis=1, keepdims=True)
    number = jnp.broadcast_to(number, (count, HEAD)).astype(BF16)
    owner = jnp.where(slot == 4, new // 8, -1)
    numbers = jnp.dot(
        bits(iota((8 * count, count), 1) == owner), number, preferred_element_type=F32
    )
    out[:, 8:] = (kv_rows + numbers).astype(BF16).reshape(count, 8, HEAD)
    for move in moves:
        move.wait()


def split3(x):
    high = x.astype(BF16).astype(F32)
    middle = (x - high).astype(BF16).astype(F32)
    return high, middle, x - high - middle


def band_kernel(
    q_in, keys_in, values_in, order_in, offsets_in, vert_in, prev_in, out, ints,
    q, keys, values, order, offsets, vertical, prev, sems,
):
    load(
        [(q_in, q), (keys_in, keys), (values_in, values), (order_in, order), (offsets_in, offsets), (vert_in, vertical), (prev_in, prev)],
        sems,
    )
    rows = q.shape[0]
    heads = q.shape[1] // HEAD
    count = rows // 2
    chips = out.shape[0]
    band = 2 * rows
    ctx, core = lax.axis_index(CTX), lax.axis_index("c")
    spread = bits(iota((NV, HEAD), 0) == iota((NV, HEAD), 1) % NV)
    vert = jnp.dot(
        vertical[...].astype(F32).astype(BF16), spread, preferred_element_type=F32
    ).astype(jnp.int32)
    table_row = iota(ints.shape, 0)
    want = (vert // 2) * 8 + (vert % 2) * 2 + iota((1, HEAD), 1) // NV
    ints[...] = jnp.where(
        table_row == VERT, vert, jnp.where(table_row == WANT, want, jnp.where(table_row == CORE, core, 0))
    )
    closed = jnp.zeros((1, band), F32)
    part = iota((1, band), 1) // BLK
    for j in range(band // BLK):
        number = ctx * (rows // BLK) + (j - rows // BLK)
        hit = jnp.max(jnp.where(vert == number, 1.0, 0.0), axis=1, keepdims=True)
        hit = jnp.where(number < 0, 1.0, hit)
        closed = jnp.where(part == j, hit, closed)
    lag = rows - iota((heads, band), 1)
    table = jnp.zeros((heads, band), F32)
    offs = offsets[...]
    for k in range(offs.shape[1]):
        table = jnp.where(offs[:, k : k + 1] == lag, 1.0, table)
    kb = jnp.concatenate([prev[:, :HEAD], keys[...]], axis=0)
    vb = jnp.concatenate([prev[:, HEAD:], values[...]], axis=0)
    lanes = iota((rows, HEAD), 1) % 8
    done = []
    for h in range(heads):
        spread = jnp.broadcast_to(table[h : h + 1], (rows, band))
        slash = pltpu.roll(spread, 0, 1, stride=1, stride_axis=0)
        mask = (slash > 0.5) & (closed < 0.5)
        s = jnp.where(mask, dot_t(q[:, h * HEAD : (h + 1) * HEAD], kb), LOW)
        top = jnp.max(s, axis=1, keepdims=True)
        p = jnp.where(mask, jnp.exp2((s - top) * FACTOR), 0.0)
        total = jnp.sum(p, axis=1, keepdims=True)
        o = jnp.dot(p.astype(BF16), vb, preferred_element_type=F32)
        o = o / jnp.where(total > 0.0, total, 1.0)
        sums = jnp.zeros((rows, HEAD), F32)
        for j, term in enumerate(split3(top) + split3(total)):
            sums = jnp.where(lanes == j, term, sums)
        done.append(jnp.concatenate([o.astype(BF16), sums.astype(BF16)], axis=1))
    moved = pick_t(by_destination(order[...], rows, heads), jnp.concatenate(done, axis=0))
    size = 8 * count
    own = iota((size, HEAD), 1) // 8 == iota((size, HEAD), 0) % 8
    sums = jnp.where(own, moved[:, HEAD:].astype(F32), 0.0).astype(BF16)
    new = iota((8 * chips, 1), 0)
    owner = jnp.where(new % 8 < 2, (new // 8) * 2 + new % 8, -1)
    sums = pick(iota((8 * chips, size), 1) // 8 == owner, sums)
    out[:, :16] = moved[:, :HEAD].reshape(chips, 16, HEAD)
    out[:, 16:] = sums.reshape(chips, 8, HEAD)


def select_kernel(ints, recv, slash, out, kept):
    kept[...] = ints[...]
    want = ints[WANT : WANT + 1, : 2 * NV]
    held = recv[:, 8:].reshape(-1, HEAD)
    picked = pick_t(iota((held.shape[0], 2 * NV), 0) == want, held)
    out[:, 2 * NV :] = slash[...]
    for chip in range(out.shape[0]):
        out[chip, : 2 * NV] = picked


def key_positions(ints, core, chips):
    vpos = ints[VERT : VERT + 1, :] * BLK + (iota((1, HEAD), 1) // NV) * 2 + core
    step = 2 * HEAD // NV
    return jnp.concatenate([vpos + m * step for m in range(chips * NV // HEAD)], axis=1)


def row_positions(recv, rows):
    tail = recv[:, 8:].astype(F32)
    size = 8 * tail.shape[0]
    number = jnp.sum(jnp.where(iota(tail.shape, 1) == 4, tail, 0.0), axis=1, keepdims=True)
    number = jnp.broadcast_to(number, tail.shape).reshape(size, HEAD)[:, :1]
    at = iota((size, 1), 0)
    return (at // 8) * rows + number.astype(jnp.int32) * 2 + at % 2


def half_kernel(ints, recv, mine, out):
    core = ints[CORE : CORE + 1, :1]
    size = out.shape[0]
    rows = 2 * recv.shape[0]
    pos = key_positions(ints, core, mine.shape[0])
    qpos = row_positions(recv, rows)
    q = recv[:, :8].reshape(size, HEAD)
    keys = mine[:, :NV].reshape(-1, HEAD)
    vals = mine[:, NV : 2 * NV].reshape(-1, HEAD)
    lane = iota((rows, HEAD), 1)
    for b in range(size // rows):
        cut = slice(b * rows, (b + 1) * rows)
        s = jnp.where(pos <= qpos[cut], dot_t(q[cut], keys), -jnp.inf)
        top = jnp.maximum(jnp.max(s, axis=1, keepdims=True), LOW)
        p = jnp.exp2((s - top) * FACTOR)
        total = jnp.sum(p, axis=1, keepdims=True)
        out[cut, :HEAD] = jnp.dot(p.astype(BF16), vals, preferred_element_type=F32)
        out[cut, HEAD:] = jnp.where(lane == 0, top, total)


def finish_kernel(ints, recv, mine, other, half, out):
    count = recv.shape[0]
    size = 8 * count
    rows = out.shape[0]
    heads = size // rows
    core = ints[CORE : CORE + 1, :1]
    first = core == 0
    pos = key_positions(ints, 1 - core, mine.shape[0])
    qpos = row_positions(recv, rows)

    def by_owner(cut):
        a, b = cut(mine), cut(other)
        return jnp.concatenate([jnp.where(first, a, b), jnp.where(first, b, a)], axis=1)

    base = 2 * NV

    def slash_rows(ref):
        return jnp.where(
            first, ref[:, base : base + 8].astype(F32), ref[:, base + 8 : base + 16].astype(F32)
        )

    def sums_row(ref):
        tail = ref[:, base + 16 :].astype(F32)
        which = iota(tail.shape, 1)
        row = jnp.sum(jnp.where(which == core, tail, 0.0), axis=1, keepdims=True)
        return jnp.broadcast_to(row, tail.shape)

    slash = by_owner(slash_rows).reshape(size, HEAD)
    sums = by_owner(sums_row).reshape(size, HEAD)
    lane = iota((size, HEAD), 1)
    own = lane // 8 == iota((size, HEAD), 0) % 8
    top_b = jnp.sum(jnp.where(own & (lane % 8 < 3), sums, 0.0), axis=1, keepdims=True)
    total_b = jnp.sum(jnp.where(own & (lane % 8 >= 3), sums, 0.0), axis=1, keepdims=True)

    q = recv[:, :8].reshape(size, HEAD)
    keys = other[:, :NV].reshape(-1, HEAD)
    vals = other[:, NV : 2 * NV].reshape(-1, HEAD)
    done = []
    for b in range(heads):
        cut = slice(b * rows, (b + 1) * rows)
        s = jnp.where(pos <= qpos[cut], dot_t(q[cut], keys), -jnp.inf)
        top_a = half[cut, HEAD : HEAD + 1]
        top = jnp.maximum(jnp.max(s, axis=1, keepdims=True), jnp.maximum(top_a, top_b[cut]))
        p = jnp.exp2((s - top) * FACTOR)
        share_a = jnp.exp2((top_a - top) * FACTOR)
        share_b = total_b[cut] * jnp.exp2((top_b[cut] - top) * FACTOR)
        total = jnp.sum(p, axis=1, keepdims=True) + share_a * half[cut, HEAD + 1 : HEAD + 2] + share_b
        o = jnp.dot(p.astype(BF16), vals, preferred_element_type=F32)
        o += share_a * half[cut, :HEAD] + share_b * slash[cut]
        done.append((o / total).astype(BF16))
    attended = jnp.concatenate(done, axis=0)
    row = iota((rows, 1), 0)
    cols = iota((rows, size), 1)
    for h in range(heads):
        rows_h = pick(cols == (row // 2) * 8 + h * 2 + row % 2, attended)
        out[:, h * HEAD : (h + 1) * HEAD] = rows_h


def own_kernel(full, weight_in, out, weight, sems):
    parity = lax.axis_index("yl")
    moves = [
        pltpu.make_async_copy(columns(weight_in, j, parity), weight.at[j], sems.at[j])
        for j in range(out.shape[0])
    ]
    for move in moves:
        move.start()
    for j, move in enumerate(moves):
        move.wait()
        out[j] = jnp.dot(full[...], weight[j], preferred_element_type=F32)


def both_kernel(own, full, near, far, out):
    core = lax.axis_index("c")
    share = near.shape[0]
    for weight, first in ((near, core * share), (far, (1 - core) * share)):
        for i in range(share):
            part = own[first + i] + jnp.dot(full[...], weight[i], preferred_element_type=F32)
            out[first + i] = part.astype(BF16)


def local(queries, keys, values, vertical, offsets, send_order, out_weight):
    z_n, x_n, c_n, pairs = (lax.axis_size(a) for a in ("z", "x", "c", "yh"))
    rows = queries.shape[0]
    n_ctx = z_n * x_n * c_n
    chips = z_n * x_n
    large = pltpu.CompilerParams(vmem_limit_bytes=60 * MIB)
    small = pltpu.CompilerParams(vmem_limit_bytes=16 * MIB)
    width = out_weight.shape[1] // (2 * pairs)
    columns_half = (pairs // c_n, out_weight.shape[0], width)
    held = [pltpu.VMEM(a.shape, a.dtype) for a in (queries, keys, values, send_order)]

    packed, kv, sent = pl.pallas_call(
        pack_kernel,
        out_shape=[
            jax.ShapeDtypeStruct((n_ctx, 16, HEAD), BF16),
            jax.ShapeDtypeStruct((rows, 2 * HEAD), BF16),
            jax.ShapeDtypeStruct(columns_half, BF16),
        ],
        in_specs=[HBM] * 5,
        out_specs=[VMEM, VMEM, VMEM],
        scratch_shapes=held + [pltpu.SemaphoreType.DMA((4,)), pltpu.SemaphoreType.DMA((pairs // c_n,))],
        name="pack",
        compiler_params=large,
    )(queries, keys, values, send_order, out_weight)
    recv = lax.all_to_all(packed, CTX, 0, 0, tiled=True)
    prev = lax.ppermute(kv, CTX, [(i, i + 1) for i in range(n_ctx - 1)])
    swap = [(0, 1), (1, 0)]
    near = lax.ppermute(sent, "yl", swap)
    slash, ints = pl.pallas_call(
        band_kernel,
        out_shape=[
            jax.ShapeDtypeStruct((chips, 24, HEAD), BF16),
            jax.ShapeDtypeStruct((8, HEAD), jnp.int32),
        ],
        in_specs=[HBM] * 7,
        out_specs=[VMEM, VMEM],
        scratch_shapes=held
        + [pltpu.VMEM(a.shape, a.dtype) for a in (offsets, vertical, prev)]
        + [pltpu.SemaphoreType.DMA((7,))],
        name="slash",
        compiler_params=large,
    )(queries, keys, values, send_order, offsets, vertical, prev)
    parts, ints = pl.pallas_call(
        select_kernel,
        out_shape=[
            jax.ShapeDtypeStruct((chips, 2 * NV + 24, HEAD), BF16),
            jax.ShapeDtypeStruct(ints.shape, jnp.int32),
        ],
        in_specs=[VMEM] * 3,
        out_specs=[VMEM, VMEM],
        name="select",
        compiler_params=small,
    )(ints, recv, slash)
    parts, near = lax.optimization_barrier((parts, near))
    far = lax.ppermute(near, "c", swap)
    mine = lax.all_to_all(parts, ("z", "x"), 0, 0, tiled=True)
    mine, far = lax.optimization_barrier((mine, far))
    other = lax.ppermute(mine, "c", swap)
    half = pl.pallas_call(
        half_kernel,
        out_shape=jax.ShapeDtypeStruct((8 * n_ctx, 2 * HEAD), F32),
        in_specs=[VMEM] * 3,
        out_specs=VMEM,
        name="half",
        compiler_params=pltpu.CompilerParams(vmem_limit_bytes=32 * MIB),
        cost_estimate=pl.CostEstimate(flops=300000000, bytes_accessed=2000000, transcendentals=500000),
    )(ints, recv, mine)
    full = pl.pallas_call(
        finish_kernel,
        out_shape=jax.ShapeDtypeStruct(queries.shape, BF16),
        in_specs=[VMEM] * 5,
        out_specs=VMEM,
        name="finish",
        compiler_params=pltpu.CompilerParams(vmem_limit_bytes=32 * MIB),
    )(ints, recv, mine, other, half)
    theirs_full = lax.ppermute(full, "yl", swap)
    own = pl.pallas_call(
        own_kernel,
        out_shape=jax.ShapeDtypeStruct((pairs, rows, width), F32),
        in_specs=[VMEM, HBM],
        out_specs=VMEM,
        scratch_shapes=[
            pltpu.VMEM((pairs, out_weight.shape[0], width), BF16),
            pltpu.SemaphoreType.DMA((pairs,)),
        ],
        name="project_own",
        compiler_params=pltpu.CompilerParams(vmem_limit_bytes=52 * MIB),
        cost_estimate=pl.CostEstimate(flops=300000000, bytes_accessed=8000000, transcendentals=0),
    )(full, out_weight)
    partial = pl.pallas_call(
        both_kernel,
        out_shape=jax.ShapeDtypeStruct((pairs, rows, width), BF16),
        in_specs=[VMEM] * 4,
        out_specs=VMEM,
        name="project_both",
        compiler_params=pltpu.CompilerParams(vmem_limit_bytes=32 * MIB),
    )(own, theirs_full, near, far)
    sums = lax.all_to_all(partial, "yh", 0, 0, tiled=True)
    return jnp.sum(sums.astype(F32), axis=0).astype(BF16)


def solution(mesh):
    cut = Mesh(mesh.devices.reshape(8, 4, 2, 4, 2), CTX + Y)
    placed = (
        P(CTX, Y),
        P(CTX, Y),
        P(CTX, Y),
        P(Y, None),
        P(Y, None),
        P(CTX, None),
        P(Y, None),
    )
    return jax.shard_map(
        local, mesh=cut, in_specs=placed, out_specs=P(CTX, Y), check_vma=False
    )
```

```python
import math

import jax
import jax.numpy as jnp
from jax import lax
from jax.experimental import pallas as pl
from jax.experimental.pallas import tpu as pltpu
from jax.sharding import Mesh, PartitionSpec as P

HEAD = 128
BLK = 64
NV = 32
CTX = ("z", "x", "c")
Y = ("yh", "yl")
VMEM = pl.BlockSpec(memory_space=pltpu.VMEM)
HBM = pl.BlockSpec(memory_space=pltpu.HBM)
F32 = jnp.float32
BF16 = jnp.bfloat16
LOW = -1e30
FACTOR = math.log2(math.e) / math.sqrt(HEAD)
MIB = 1024 * 1024
NUMBER, VERT = 4, 5


def iota(shape, dim):
    return lax.broadcasted_iota(jnp.int32, shape, dim)


def bits(mask):
    return jnp.where(mask, 1.0, 0.0).astype(BF16)


def pick(mask, rows):
    return jnp.dot(bits(mask), rows, preferred_element_type=F32).astype(BF16)


def pick_t(mask, rows):
    return lax.dot_general(
        bits(mask), rows, (((0,), (0,)), ((), ())), preferred_element_type=F32
    ).astype(BF16)


def dot_t(a, b):
    return lax.dot_general(a, b, (((1,), (1,)), ((), ())), preferred_element_type=F32)


def by_destination(order, rows, heads):
    lanes = rows * heads
    count = rows // 2
    spread = bits(iota((count, lanes), 0) == iota((count, lanes), 1) // (2 * heads))
    piece = jnp.dot(order.astype(F32).astype(BF16), spread, preferred_element_type=F32)
    at = iota((1, lanes), 1)
    target = piece.astype(jnp.int32) * 2 + at % 2 + (at // 2 % heads) * rows
    return iota((lanes, lanes), 0) == target


def head_rows(ref, heads):
    return jnp.concatenate([ref[:, h * HEAD : (h + 1) * HEAD] for h in range(heads)], axis=0)


def load(pairs, sems):
    moves = [pltpu.make_async_copy(a, b, sems.at[i]) for i, (a, b) in enumerate(pairs)]
    for move in moves:
        move.start()
    for move in moves:
        move.wait()


def columns(ref, j, parity):
    width = ref.shape[1] // 8
    start = pl.multiple_of((2 * j + parity) * width, width)
    return ref.at[:, pl.ds(start, width)]


def tiled_vertical(vertical):
    spread = bits(iota((NV, HEAD), 0) == iota((NV, HEAD), 1) % NV)
    return jnp.dot(vertical[...].astype(F32).astype(BF16), spread, preferred_element_type=F32)


def vertical_of(recv):
    tail = recv[0, 8:].astype(F32)
    here = iota(tail.shape, 0) == VERT
    return jnp.sum(jnp.where(here, tail, 0.0), axis=0, keepdims=True).astype(jnp.int32)


def pack_kernel(
    q_in, keys_in, values_in, order_in, vert_in, weight_in, out, kv, sent,
    q, keys, values, order, vertical, sems, wsems,
):
    parity, core = lax.axis_index("yl"), lax.axis_index("c")
    share = sent.shape[0]
    moves = [
        pltpu.make_async_copy(
            columns(weight_in, core * share + j, 1 - parity), sent.at[j], wsems.at[j]
        )
        for j in range(share)
    ]
    for move in moves:
        move.start()
    load(
        [(q_in, q), (keys_in, keys), (values_in, values), (order_in, order), (vert_in, vertical)],
        sems,
    )
    rows = q.shape[0]
    heads = q.shape[1] // HEAD
    count = rows // 2
    kv[:, :HEAD] = keys[...]
    kv[:, HEAD:] = values[...]
    moved = pick_t(by_destination(order[...], rows, heads), head_rows(q, heads))
    out[:, :8] = moved.reshape(count, 8, HEAD)
    new = iota((8 * count, 1), 0)
    slot = new % 8
    source = jnp.where(slot < 4, (slot % 2) * rows + (slot // 2) * BLK + new // 8, -1)
    kv_rows = jnp.dot(
        bits(iota((8 * count, 2 * rows), 1) == source),
        jnp.concatenate([keys[...], values[...]], axis=0),
        preferred_element_type=F32,
    )
    diagonal = iota((count, count), 0) == iota((count, count), 1)
    number = jnp.sum(jnp.where(diagonal, order[...].astype(F32), 0.0), axis=1, keepdims=True)
    number = jnp.broadcast_to(number, (count, HEAD)).astype(BF16)
    owner = jnp.where(slot == NUMBER, new // 8, -1)
    numbers = jnp.dot(
        bits(iota((8 * count, count), 1) == owner), number, preferred_element_type=F32
    )
    numbers += jnp.where(slot == VERT, tiled_vertical(vertical), 0.0)
    out[:, 8:] = (kv_rows + numbers).astype(BF16).reshape(count, 8, HEAD)
    for move in moves:
        move.wait()


def split3(x):
    high = x.astype(BF16).astype(F32)
    middle = (x - high).astype(BF16).astype(F32)
    return high, middle, x - high - middle


def band_kernel(
    q_in, keys_in, values_in, order_in, offsets_in, vert_in, prev_in, out,
    q, keys, values, order, offsets, vertical, prev, sems,
):
    load(
        [(q_in, q), (keys_in, keys), (values_in, values), (order_in, order), (offsets_in, offsets), (vert_in, vertical), (prev_in, prev)],
        sems,
    )
    rows = q.shape[0]
    heads = q.shape[1] // HEAD
    count = rows // 2
    chips = out.shape[0]
    band = 2 * rows
    ctx = lax.axis_index(CTX)
    vert = tiled_vertical(vertical).astype(jnp.int32)
    closed = jnp.zeros((1, band), F32)
    part = iota((1, band), 1) // BLK
    for j in range(band // BLK):
        number = ctx * (rows // BLK) + (j - rows // BLK)
        hit = jnp.max(jnp.where(vert == number, 1.0, 0.0), axis=1, keepdims=True)
        hit = jnp.where(number < 0, 1.0, hit)
        closed = jnp.where(part == j, hit, closed)
    lag = rows - iota((heads, band), 1)
    table = jnp.zeros((heads, band), F32)
    offs = offsets[...]
    for k in range(offs.shape[1]):
        table = jnp.where(offs[:, k : k + 1] == lag, 1.0, table)
    kb = jnp.concatenate([prev[:, :HEAD], keys[...]], axis=0)
    vb = jnp.concatenate([prev[:, HEAD:], values[...]], axis=0)
    lanes = iota((rows, HEAD), 1) % 8
    done = []
    for h in range(heads):
        spread = jnp.broadcast_to(table[h : h + 1], (rows, band))
        slash = pltpu.roll(spread, 0, 1, stride=1, stride_axis=0)
        mask = (slash > 0.5) & (closed < 0.5)
        s = jnp.where(mask, dot_t(q[:, h * HEAD : (h + 1) * HEAD], kb), LOW)
        top = jnp.max(s, axis=1, keepdims=True)
        p = jnp.where(mask, jnp.exp2((s - top) * FACTOR), 0.0)
        total = jnp.sum(p, axis=1, keepdims=True)
        o = jnp.dot(p.astype(BF16), vb, preferred_element_type=F32)
        o = o / jnp.where(total > 0.0, total, 1.0)
        sums = jnp.zeros((rows, HEAD), F32)
        for j, term in enumerate(split3(top) + split3(total)):
            sums = jnp.where(lanes == j, term, sums)
        done.append(jnp.concatenate([o.astype(BF16), sums.astype(BF16)], axis=1))
    moved = pick_t(by_destination(order[...], rows, heads), jnp.concatenate(done, axis=0))
    size = 8 * count
    own = iota((size, HEAD), 1) // 8 == iota((size, HEAD), 0) % 8
    sums = jnp.where(own, moved[:, HEAD:].astype(F32), 0.0).astype(BF16)
    new = iota((8 * chips, 1), 0)
    owner = jnp.where(new % 8 < 2, (new // 8) * 2 + new % 8, -1)
    sums = pick(iota((8 * chips, size), 1) // 8 == owner, sums)
    out[:, :16] = moved[:, :HEAD].reshape(chips, 16, HEAD)
    out[:, 16:] = sums.reshape(chips, 8, HEAD)


def select_kernel(recv, slash, out):
    vert = vertical_of(recv)
    want = ((vert // 2) * 8 + (vert % 2) * 2 + iota((1, HEAD), 1) // NV)[:, : 2 * NV]
    held = recv[:, 8:].reshape(-1, HEAD)
    picked = pick_t(iota((held.shape[0], 2 * NV), 0) == want, held)
    out[:, 2 * NV :] = slash[...]
    for chip in range(out.shape[0]):
        out[chip, : 2 * NV] = picked


def key_positions(vert, core, chips):
    vpos = vert * BLK + (iota((1, HEAD), 1) // NV) * 2 + core
    step = 2 * HEAD // NV
    return jnp.concatenate([vpos + m * step for m in range(chips * NV // HEAD)], axis=1)


def row_positions(recv, rows):
    tail = recv[:, 8:].astype(F32)
    size = 8 * tail.shape[0]
    number = jnp.sum(jnp.where(iota(tail.shape, 1) == NUMBER, tail, 0.0), axis=1, keepdims=True)
    number = jnp.broadcast_to(number, tail.shape).reshape(size, HEAD)[:, :1]
    at = iota((size, 1), 0)
    return (at // 8) * rows + number.astype(jnp.int32) * 2 + at % 2


def half_kernel(recv, mine, out):
    core = lax.axis_index("c")
    size = out.shape[0]
    rows = 2 * recv.shape[0]
    pos = key_positions(vertical_of(recv), core, mine.shape[0])
    qpos = row_positions(recv, rows)
    q = recv[:, :8].reshape(size, HEAD)
    keys = mine[:, :NV].reshape(-1, HEAD)
    vals = mine[:, NV : 2 * NV].reshape(-1, HEAD)
    lane = iota((rows, HEAD), 1)
    for b in range(size // rows):
        cut = slice(b * rows, (b + 1) * rows)
        s = jnp.where(pos <= qpos[cut], dot_t(q[cut], keys), -jnp.inf)
        top = jnp.maximum(jnp.max(s, axis=1, keepdims=True), LOW)
        p = jnp.exp2((s - top) * FACTOR)
        total = jnp.sum(p, axis=1, keepdims=True)
        out[cut, :HEAD] = jnp.dot(p.astype(BF16), vals, preferred_element_type=F32)
        out[cut, HEAD:] = jnp.where(lane == 0, top, total)


def finish_kernel(recv, mine, other, half, out):
    count = recv.shape[0]
    size = 8 * count
    rows = out.shape[0]
    heads = size // rows
    core = lax.axis_index("c")
    first = core == 0
    pos = key_positions(vertical_of(recv), 1 - core, mine.shape[0])
    qpos = row_positions(recv, rows)

    def by_owner(cut):
        a, b = cut(mine), cut(other)
        return jnp.concatenate([jnp.where(first, a, b), jnp.where(first, b, a)], axis=1)

    base = 2 * NV

    def slash_rows(ref):
        return jnp.where(
            first, ref[:, base : base + 8].astype(F32), ref[:, base + 8 : base + 16].astype(F32)
        )

    def sums_row(ref):
        tail = ref[:, base + 16 :].astype(F32)
        which = iota(tail.shape, 1)
        row = jnp.sum(jnp.where(which == core, tail, 0.0), axis=1, keepdims=True)
        return jnp.broadcast_to(row, tail.shape)

    slash = by_owner(slash_rows).reshape(size, HEAD)
    sums = by_owner(sums_row).reshape(size, HEAD)
    lane = iota((size, HEAD), 1)
    own = lane // 8 == iota((size, HEAD), 0) % 8
    top_b = jnp.sum(jnp.where(own & (lane % 8 < 3), sums, 0.0), axis=1, keepdims=True)
    total_b = jnp.sum(jnp.where(own & (lane % 8 >= 3), sums, 0.0), axis=1, keepdims=True)

    q = recv[:, :8].reshape(size, HEAD)
    keys = other[:, :NV].reshape(-1, HEAD)
    vals = other[:, NV : 2 * NV].reshape(-1, HEAD)
    done = []
    for b in range(heads):
        cut = slice(b * rows, (b + 1) * rows)
        s = jnp.where(pos <= qpos[cut], dot_t(q[cut], keys), -jnp.inf)
        top_a = half[cut, HEAD : HEAD + 1]
        top = jnp.maximum(jnp.max(s, axis=1, keepdims=True), jnp.maximum(top_a, top_b[cut]))
        p = jnp.exp2((s - top) * FACTOR)
        share_a = jnp.exp2((top_a - top) * FACTOR)
        share_b = total_b[cut] * jnp.exp2((top_b[cut] - top) * FACTOR)
        total = jnp.sum(p, axis=1, keepdims=True) + share_a * half[cut, HEAD + 1 : HEAD + 2] + share_b
        o = jnp.dot(p.astype(BF16), vals, preferred_element_type=F32)
        o += share_a * half[cut, :HEAD] + share_b * slash[cut]
        done.append((o / total).astype(BF16))
    attended = jnp.concatenate(done, axis=0)
    row = iota((rows, 1), 0)
    cols = iota((rows, size), 1)
    for h in range(heads):
        rows_h = pick(cols == (row // 2) * 8 + h * 2 + row % 2, attended)
        out[:, h * HEAD : (h + 1) * HEAD] = rows_h


def own_kernel(full, weight_in, out, weight, sems):
    parity = lax.axis_index("yl")
    moves = [
        pltpu.make_async_copy(columns(weight_in, j, parity), weight.at[j], sems.at[j])
        for j in range(out.shape[0])
    ]
    for move in moves:
        move.start()
    for j, move in enumerate(moves):
        move.wait()
        out[j] = jnp.dot(full[...], weight[j], preferred_element_type=F32)


def arrange_kernel(near, far, out):
    core = lax.axis_index("c")
    share = near.shape[0]
    out[pl.ds(core * share, share)] = near[...]
    out[pl.ds((1 - core) * share, share)] = far[...]


def both_kernel(own, full, weight, out):
    for j in range(out.shape[0]):
        part = own[j] + jnp.dot(full[...], weight[j], preferred_element_type=F32)
        out[j] = part.astype(BF16)


def local(queries, keys, values, vertical, offsets, send_order, out_weight):
    z_n, x_n, c_n, pairs = (lax.axis_size(a) for a in ("z", "x", "c", "yh"))
    rows = queries.shape[0]
    n_ctx = z_n * x_n * c_n
    chips = z_n * x_n
    large = pltpu.CompilerParams(vmem_limit_bytes=60 * MIB)
    small = pltpu.CompilerParams(vmem_limit_bytes=16 * MIB)
    width = out_weight.shape[1] // (2 * pairs)
    columns_half = (pairs // c_n, out_weight.shape[0], width)
    held = [pltpu.VMEM(a.shape, a.dtype) for a in (queries, keys, values, send_order)]

    packed, kv, sent = pl.pallas_call(
        pack_kernel,
        out_shape=[
            jax.ShapeDtypeStruct((n_ctx, 16, HEAD), BF16),
            jax.ShapeDtypeStruct((rows, 2 * HEAD), BF16),
            jax.ShapeDtypeStruct(columns_half, BF16),
        ],
        in_specs=[HBM] * 6,
        out_specs=[VMEM, VMEM, VMEM],
        scratch_shapes=held + [pltpu.VMEM(vertical.shape, jnp.int32), pltpu.SemaphoreType.DMA((5,)), pltpu.SemaphoreType.DMA((pairs // c_n,))],
        name="pack",
        compiler_params=large,
    )(queries, keys, values, send_order, vertical, out_weight)
    recv = lax.all_to_all(packed, CTX, 0, 0, tiled=True)
    prev = lax.ppermute(kv, CTX, [(i, i + 1) for i in range(n_ctx - 1)])
    swap = [(0, 1), (1, 0)]
    sent, prev = lax.optimization_barrier((sent, prev))
    near = lax.ppermute(sent, "yl", swap)
    slash = pl.pallas_call(
        band_kernel,
        out_shape=jax.ShapeDtypeStruct((chips, 24, HEAD), BF16),
        in_specs=[HBM] * 7,
        out_specs=VMEM,
        scratch_shapes=held
        + [pltpu.VMEM(a.shape, a.dtype) for a in (offsets, vertical, prev)]
        + [pltpu.SemaphoreType.DMA((7,))],
        name="slash",
        compiler_params=large,
        cost_estimate=pl.CostEstimate(flops=20000000000, bytes_accessed=1000000, transcendentals=0),
    )(queries, keys, values, send_order, offsets, vertical, prev)
    parts = pl.pallas_call(
        select_kernel,
        out_shape=jax.ShapeDtypeStruct((chips, 2 * NV + 24, HEAD), BF16),
        in_specs=[VMEM] * 2,
        out_specs=VMEM,
        name="select",
        compiler_params=small,
    )(recv, slash)
    far = lax.ppermute(near, "c", swap)
    theirs = pl.pallas_call(
        arrange_kernel,
        out_shape=jax.ShapeDtypeStruct((pairs,) + near.shape[1:], BF16),
        in_specs=[VMEM] * 2,
        out_specs=VMEM,
        name="arrange",
        compiler_params=small,
        cost_estimate=pl.CostEstimate(flops=3000000000, bytes_accessed=4000000, transcendentals=0),
    )(near, far)
    mine = lax.all_to_all(parts, ("z", "x"), 0, 0, tiled=True)
    mine, theirs = lax.optimization_barrier((mine, theirs))
    other = lax.ppermute(mine, "c", swap)
    half = pl.pallas_call(
        half_kernel,
        out_shape=jax.ShapeDtypeStruct((8 * n_ctx, 2 * HEAD), F32),
        in_specs=[VMEM] * 2,
        out_specs=VMEM,
        name="half",
        compiler_params=pltpu.CompilerParams(vmem_limit_bytes=32 * MIB),
        cost_estimate=pl.CostEstimate(flops=300000000, bytes_accessed=2000000, transcendentals=500000),
    )(recv, mine)
    full = pl.pallas_call(
        finish_kernel,
        out_shape=jax.ShapeDtypeStruct(queries.shape, BF16),
        in_specs=[VMEM] * 4,
        out_specs=VMEM,
        name="finish",
        compiler_params=pltpu.CompilerParams(vmem_limit_bytes=32 * MIB),
    )(recv, mine, other, half)
    theirs_full = lax.ppermute(full, "yl", swap)
    own = pl.pallas_call(
        own_kernel,
        out_shape=jax.ShapeDtypeStruct((pairs, rows, width), F32),
        in_specs=[VMEM, HBM],
        out_specs=VMEM,
        scratch_shapes=[
            pltpu.VMEM((pairs, out_weight.shape[0], width), BF16),
            pltpu.SemaphoreType.DMA((pairs,)),
        ],
        name="project_own",
        compiler_params=pltpu.CompilerParams(vmem_limit_bytes=52 * MIB),
        cost_estimate=pl.CostEstimate(flops=300000000, bytes_accessed=8000000, transcendentals=0),
    )(full, out_weight)
    partial = pl.pallas_call(
        both_kernel,
        out_shape=jax.ShapeDtypeStruct((pairs, rows, width), BF16),
        in_specs=[VMEM] * 3,
        out_specs=VMEM,
        name="project_both",
        compiler_params=pltpu.CompilerParams(vmem_limit_bytes=32 * MIB),
    )(own, theirs_full, theirs)
    sums = lax.all_to_all(partial, "yh", 0, 0, tiled=True)
    return jnp.sum(sums.astype(F32), axis=0).astype(BF16)


def solution(mesh):
    cut = Mesh(mesh.devices.reshape(8, 4, 2, 4, 2), CTX + Y)
    placed = (
        P(CTX, Y),
        P(CTX, Y),
        P(CTX, Y),
        P(Y, None),
        P(Y, None),
        P(CTX, None),
        P(Y, None),
    )
    return jax.shard_map(
        local, mesh=cut, in_specs=placed, out_specs=P(CTX, Y), check_vma=False
    )
```

```python
import math

import jax
import jax.numpy as jnp
from jax import lax
from jax.experimental import pallas as pl
from jax.experimental.pallas import tpu as pltpu
from jax.sharding import Mesh, PartitionSpec as P

HEAD = 128
BLK = 64
NV = 32
CTX = ("z", "x", "c")
Y = ("yh", "yl")
VMEM = pl.BlockSpec(memory_space=pltpu.VMEM)
HBM = pl.BlockSpec(memory_space=pltpu.HBM)
F32 = jnp.float32
BF16 = jnp.bfloat16
LOW = -1e30
FACTOR = math.log2(math.e) / math.sqrt(HEAD)
MIB = 1024 * 1024
NUMBER, VERT = 4, 5


def iota(shape, dim):
    return lax.broadcasted_iota(jnp.int32, shape, dim)


def bits(mask):
    return jnp.where(mask, 1.0, 0.0).astype(BF16)


def pick(mask, rows):
    return jnp.dot(bits(mask), rows, preferred_element_type=F32).astype(BF16)


def pick_t(mask, rows):
    return lax.dot_general(
        bits(mask), rows, (((0,), (0,)), ((), ())), preferred_element_type=F32
    ).astype(BF16)


def dot_t(a, b):
    return lax.dot_general(a, b, (((1,), (1,)), ((), ())), preferred_element_type=F32)


def by_destination(order, rows, heads):
    lanes = rows * heads
    count = rows // 2
    spread = bits(iota((count, lanes), 0) == iota((count, lanes), 1) // (2 * heads))
    piece = jnp.dot(order.astype(F32).astype(BF16), spread, preferred_element_type=F32)
    at = iota((1, lanes), 1)
    target = piece.astype(jnp.int32) * 2 + at % 2 + (at // 2 % heads) * rows
    return iota((lanes, lanes), 0) == target


def head_rows(ref, heads):
    return jnp.concatenate([ref[:, h * HEAD : (h + 1) * HEAD] for h in range(heads)], axis=0)


def load(pairs, sems):
    moves = [pltpu.make_async_copy(a, b, sems.at[i]) for i, (a, b) in enumerate(pairs)]
    for move in moves:
        move.start()
    for move in moves:
        move.wait()


def columns(ref, j, parity):
    width = ref.shape[1] // 8
    start = pl.multiple_of((2 * j + parity) * width, width)
    return ref.at[:, pl.ds(start, width)]


def tiled_vertical(vertical):
    spread = bits(iota((NV, HEAD), 0) == iota((NV, HEAD), 1) % NV)
    return jnp.dot(vertical[...].astype(F32).astype(BF16), spread, preferred_element_type=F32)


def vertical_of(recv):
    tail = recv[0, 8:].astype(F32)
    here = iota(tail.shape, 0) == VERT
    return jnp.sum(jnp.where(here, tail, 0.0), axis=0, keepdims=True).astype(jnp.int32)


def pack_kernel(
    q_in, keys_in, values_in, order_in, vert_in, weight_in, out, kv, sent,
    q, keys, values, order, vertical, sems, wsems,
):
    parity, core = lax.axis_index("yl"), lax.axis_index("c")
    share = sent.shape[0]
    moves = [
        pltpu.make_async_copy(
            columns(weight_in, core * share + j, 1 - parity), sent.at[j], wsems.at[j]
        )
        for j in range(share)
    ]
    loads = [(order_in, order), (vert_in, vertical), (keys_in, keys), (values_in, values), (q_in, q)]
    loads = [pltpu.make_async_copy(a, b, sems.at[i]) for i, (a, b) in enumerate(loads)]
    for move in loads + moves:
        move.start()
    rows = q.shape[0]
    heads = q.shape[1] // HEAD
    count = rows // 2
    new = iota((8 * count, 1), 0)
    slot = new % 8
    source = jnp.where(slot < 4, (slot % 2) * rows + (slot // 2) * BLK + new // 8, -1)
    source = bits(iota((8 * count, 2 * rows), 1) == source)
    owner = bits(iota((8 * count, count), 1) == jnp.where(slot == NUMBER, new // 8, -1))
    diagonal = iota((count, count), 0) == iota((count, count), 1)
    for move in loads[:2]:
        move.wait()
    number = jnp.sum(jnp.where(diagonal, order[...].astype(F32), 0.0), axis=1, keepdims=True)
    number = jnp.broadcast_to(number, (count, HEAD)).astype(BF16)
    numbers = jnp.dot(owner, number, preferred_element_type=F32)
    numbers += jnp.where(slot == VERT, tiled_vertical(vertical), 0.0)
    target = bits(by_destination(order[...], rows, heads))
    for move in loads[2:]:
        move.wait()
    kv[:, :HEAD] = keys[...]
    kv[:, HEAD:] = values[...]
    kv_rows = jnp.dot(
        source, jnp.concatenate([keys[...], values[...]], axis=0), preferred_element_type=F32
    )
    out[:, 8:] = (kv_rows + numbers).astype(BF16).reshape(count, 8, HEAD)
    moved = lax.dot_general(
        target, head_rows(q, heads), (((0,), (0,)), ((), ())), preferred_element_type=F32
    )
    out[:, :8] = moved.astype(BF16).reshape(count, 8, HEAD)
    for move in moves:
        move.wait()


def split3(x):
    high = x.astype(BF16).astype(F32)
    middle = (x - high).astype(BF16).astype(F32)
    return high, middle, x - high - middle


def band_kernel(
    q_in, keys_in, values_in, order_in, offsets_in, vert_in, prev_in, out,
    q, keys, values, order, offsets, vertical, prev, sems,
):
    pairs = [(offsets_in, offsets), (vert_in, vertical), (keys_in, keys), (prev_in, prev)]
    pairs += [(values_in, values), (q_in, q), (order_in, order)]
    moves = [pltpu.make_async_copy(a, b, sems.at[i]) for i, (a, b) in enumerate(pairs)]
    for move in moves:
        move.start()
    for move in moves[:2]:
        move.wait()
    rows = q.shape[0]
    heads = q.shape[1] // HEAD
    count = rows // 2
    chips = out.shape[0]
    band = 2 * rows
    ctx = lax.axis_index(CTX)
    vert = tiled_vertical(vertical).astype(jnp.int32)
    closed = jnp.zeros((1, band), F32)
    part = iota((1, band), 1) // BLK
    for j in range(band // BLK):
        number = ctx * (rows // BLK) + (j - rows // BLK)
        hit = jnp.max(jnp.where(vert == number, 1.0, 0.0), axis=1, keepdims=True)
        hit = jnp.where(number < 0, 1.0, hit)
        closed = jnp.where(part == j, hit, closed)
    lag = rows - iota((heads, band), 1)
    table = jnp.zeros((heads, band), F32)
    offs = offsets[...]
    for k in range(offs.shape[1]):
        table = jnp.where(offs[:, k : k + 1] == lag, 1.0, table)
    for move in moves[2:]:
        move.wait()
    kb = jnp.concatenate([prev[:, :HEAD], keys[...]], axis=0)
    vb = jnp.concatenate([prev[:, HEAD:], values[...]], axis=0)
    lanes = iota((rows, HEAD), 1) % 8
    done = []
    for h in range(heads):
        spread = jnp.broadcast_to(table[h : h + 1], (rows, band))
        slash = pltpu.roll(spread, 0, 1, stride=1, stride_axis=0)
        mask = (slash > 0.5) & (closed < 0.5)
        s = jnp.where(mask, dot_t(q[:, h * HEAD : (h + 1) * HEAD], kb), LOW)
        top = jnp.max(s, axis=1, keepdims=True)
        p = jnp.where(mask, jnp.exp2((s - top) * FACTOR), 0.0)
        total = jnp.sum(p, axis=1, keepdims=True)
        o = jnp.dot(p.astype(BF16), vb, preferred_element_type=F32)
        o = o / jnp.where(total > 0.0, total, 1.0)
        sums = jnp.zeros((rows, HEAD), F32)
        for j, term in enumerate(split3(top) + split3(total)):
            sums = jnp.where(lanes == j, term, sums)
        done.append(jnp.concatenate([o.astype(BF16), sums.astype(BF16)], axis=1))
    moved = pick_t(by_destination(order[...], rows, heads), jnp.concatenate(done, axis=0))
    size = 8 * count
    own = iota((size, HEAD), 1) // 8 == iota((size, HEAD), 0) % 8
    sums = jnp.where(own, moved[:, HEAD:].astype(F32), 0.0).astype(BF16)
    new = iota((8 * chips, 1), 0)
    owner = jnp.where(new % 8 < 2, (new // 8) * 2 + new % 8, -1)
    sums = pick(iota((8 * chips, size), 1) // 8 == owner, sums)
    out[:, :16] = moved[:, :HEAD].astype(F32).reshape(chips, 16, HEAD)
    out[:, 16:] = sums.astype(F32).reshape(chips, 8, HEAD)


def select_kernel(recv, slash, out):
    vert = vertical_of(recv)
    want = ((vert // 2) * 8 + (vert % 2) * 2 + iota((1, HEAD), 1) // NV)[:, : 2 * NV]
    held = recv[:, 8:].reshape(-1, HEAD)
    picked = pick_t(iota((held.shape[0], 2 * NV), 0) == want, held)
    out[:, 2 * NV :] = slash[...]
    for chip in range(out.shape[0]):
        out[chip, : 2 * NV] = picked


def key_positions(vert, core, chips):
    vpos = vert * BLK + (iota((1, HEAD), 1) // NV) * 2 + core
    step = 2 * HEAD // NV
    return jnp.concatenate([vpos + m * step for m in range(chips * NV // HEAD)], axis=1)


def row_positions(recv, rows):
    tail = recv[:, 8:].astype(F32)
    size = 8 * tail.shape[0]
    number = jnp.sum(jnp.where(iota(tail.shape, 1) == NUMBER, tail, 0.0), axis=1, keepdims=True)
    number = jnp.broadcast_to(number, tail.shape).reshape(size, HEAD)[:, :1]
    at = iota((size, 1), 0)
    return (at // 8) * rows + number.astype(jnp.int32) * 2 + at % 2


def half_kernel(recv, mine, out):
    core = lax.axis_index("c")
    size = out.shape[0]
    rows = 2 * recv.shape[0]
    pos = key_positions(vertical_of(recv), core, mine.shape[0])
    qpos = row_positions(recv, rows)
    q = recv[:, :8].reshape(size, HEAD)
    keys = mine[:, :NV].reshape(-1, HEAD)
    vals = mine[:, NV : 2 * NV].reshape(-1, HEAD)
    lane = iota((rows, HEAD), 1)
    for b in range(size // rows):
        cut = slice(b * rows, (b + 1) * rows)
        s = jnp.where(pos <= qpos[cut], dot_t(q[cut], keys), -jnp.inf)
        top = jnp.maximum(jnp.max(s, axis=1, keepdims=True), LOW)
        p = jnp.exp2((s - top) * FACTOR)
        total = jnp.sum(p, axis=1, keepdims=True)
        out[cut, :HEAD] = jnp.dot(p.astype(BF16), vals, preferred_element_type=F32)
        out[cut, HEAD:] = jnp.where(lane == 0, top, total)


def finish_kernel(recv, mine, other, half, out):
    count = recv.shape[0]
    size = 8 * count
    rows = out.shape[0]
    heads = size // rows
    core = lax.axis_index("c")
    first = core == 0
    pos = key_positions(vertical_of(recv), 1 - core, mine.shape[0])
    qpos = row_positions(recv, rows)

    def by_owner(cut):
        a, b = cut(mine), cut(other)
        return jnp.concatenate([jnp.where(first, a, b), jnp.where(first, b, a)], axis=1)

    base = 2 * NV

    def slash_rows(ref):
        return jnp.where(
            first, ref[:, base : base + 8].astype(F32), ref[:, base + 8 : base + 16].astype(F32)
        )

    def sums_row(ref):
        tail = ref[:, base + 16 :].astype(F32)
        which = iota(tail.shape, 1)
        row = jnp.sum(jnp.where(which == core, tail, 0.0), axis=1, keepdims=True)
        return jnp.broadcast_to(row, tail.shape)

    slash = by_owner(slash_rows).reshape(size, HEAD)
    sums = by_owner(sums_row).reshape(size, HEAD)
    lane = iota((size, HEAD), 1)
    own = lane // 8 == iota((size, HEAD), 0) % 8
    top_b = jnp.sum(jnp.where(own & (lane % 8 < 3), sums, 0.0), axis=1, keepdims=True)
    total_b = jnp.sum(jnp.where(own & (lane % 8 >= 3), sums, 0.0), axis=1, keepdims=True)

    q = recv[:, :8].reshape(size, HEAD)
    keys = other[:, :NV].reshape(-1, HEAD)
    vals = other[:, NV : 2 * NV].reshape(-1, HEAD)
    done = []
    for b in range(heads):
        cut = slice(b * rows, (b + 1) * rows)
        s = jnp.where(pos <= qpos[cut], dot_t(q[cut], keys), -jnp.inf)
        top_a = half[cut, HEAD : HEAD + 1]
        top = jnp.maximum(jnp.max(s, axis=1, keepdims=True), jnp.maximum(top_a, top_b[cut]))
        p = jnp.exp2((s - top) * FACTOR)
        share_a = jnp.exp2((top_a - top) * FACTOR)
        share_b = total_b[cut] * jnp.exp2((top_b[cut] - top) * FACTOR)
        total = jnp.sum(p, axis=1, keepdims=True) + share_a * half[cut, HEAD + 1 : HEAD + 2] + share_b
        o = jnp.dot(p.astype(BF16), vals, preferred_element_type=F32)
        o += share_a * half[cut, :HEAD] + share_b * slash[cut]
        done.append((o / total).astype(BF16))
    attended = jnp.concatenate(done, axis=0)
    row = iota((rows, 1), 0)
    cols = iota((rows, size), 1)
    for h in range(heads):
        rows_h = pick(cols == (row // 2) * 8 + h * 2 + row % 2, attended)
        out[:, h * HEAD : (h + 1) * HEAD] = rows_h


def own_kernel(full, weight_in, out, weight, sems):
    parity = lax.axis_index("yl")
    moves = [
        pltpu.make_async_copy(columns(weight_in, j, parity), weight.at[j], sems.at[j])
        for j in range(out.shape[0])
    ]
    for move in moves:
        move.start()
    for j, move in enumerate(moves):
        move.wait()
        out[j] = jnp.dot(full[...], weight[j], preferred_element_type=F32)


def arrange_kernel(near, far, out):
    core = lax.axis_index("c")
    share = near.shape[0]
    out[pl.ds(core * share, share)] = near[...]
    out[pl.ds((1 - core) * share, share)] = far[...]


def both_kernel(own, full, weight, out):
    for j in range(out.shape[0]):
        part = own[j] + jnp.dot(full[...], weight[j], preferred_element_type=F32)
        out[j] = part.astype(BF16)


def local(queries, keys, values, vertical, offsets, send_order, out_weight):
    z_n, x_n, c_n, pairs = (lax.axis_size(a) for a in ("z", "x", "c", "yh"))
    rows = queries.shape[0]
    n_ctx = z_n * x_n * c_n
    chips = z_n * x_n
    large = pltpu.CompilerParams(vmem_limit_bytes=60 * MIB)
    small = pltpu.CompilerParams(vmem_limit_bytes=16 * MIB)
    width = out_weight.shape[1] // (2 * pairs)
    columns_half = (pairs // c_n, out_weight.shape[0], width)
    held = [pltpu.VMEM(a.shape, a.dtype) for a in (queries, keys, values, send_order)]

    packed, kv, sent = pl.pallas_call(
        pack_kernel,
        out_shape=[
            jax.ShapeDtypeStruct((n_ctx, 16, HEAD), BF16),
            jax.ShapeDtypeStruct((rows, 2 * HEAD), BF16),
            jax.ShapeDtypeStruct(columns_half, BF16),
        ],
        in_specs=[HBM] * 6,
        out_specs=[VMEM, VMEM, VMEM],
        scratch_shapes=held + [pltpu.VMEM(vertical.shape, jnp.int32), pltpu.SemaphoreType.DMA((5,)), pltpu.SemaphoreType.DMA((pairs // c_n,))],
        name="pack",
        compiler_params=large,
    )(queries, keys, values, send_order, vertical, out_weight)
    recv = lax.all_to_all(packed, CTX, 0, 0, tiled=True)
    prev = lax.ppermute(kv, CTX, [(i, i + 1) for i in range(n_ctx - 1)])
    swap = [(0, 1), (1, 0)]
    sent, prev = lax.optimization_barrier((sent, prev))
    near = lax.ppermute(sent, "yl", swap)
    slash = pl.pallas_call(
        band_kernel,
        out_shape=jax.ShapeDtypeStruct((chips, 24, HEAD), F32),
        in_specs=[HBM] * 7,
        out_specs=VMEM,
        scratch_shapes=held
        + [pltpu.VMEM(a.shape, a.dtype) for a in (offsets, vertical, prev)]
        + [pltpu.SemaphoreType.DMA((7,))],
        name="slash",
        compiler_params=large,
        cost_estimate=pl.CostEstimate(flops=20000000000, bytes_accessed=1000000, transcendentals=0),
    )(queries, keys, values, send_order, offsets, vertical, prev)
    parts = pl.pallas_call(
        select_kernel,
        out_shape=jax.ShapeDtypeStruct((chips, 2 * NV + 24, HEAD), BF16),
        in_specs=[VMEM] * 2,
        out_specs=VMEM,
        name="select",
        compiler_params=small,
    )(recv, slash.astype(BF16))
    far = lax.ppermute(near, "c", swap)
    theirs = pl.pallas_call(
        arrange_kernel,
        out_shape=jax.ShapeDtypeStruct((pairs,) + near.shape[1:], BF16),
        in_specs=[VMEM] * 2,
        out_specs=VMEM,
        name="arrange",
        compiler_params=small,
        cost_estimate=pl.CostEstimate(flops=3000000000, bytes_accessed=4000000, transcendentals=0),
    )(near, far)
    mine = lax.all_to_all(parts, ("z", "x"), 0, 0, tiled=True)
    mine, theirs = lax.optimization_barrier((mine, theirs))
    other = lax.ppermute(mine, "c", swap)
    half = pl.pallas_call(
        half_kernel,
        out_shape=jax.ShapeDtypeStruct((8 * n_ctx, 2 * HEAD), F32),
        in_specs=[VMEM] * 2,
        out_specs=VMEM,
        name="half",
        compiler_params=pltpu.CompilerParams(vmem_limit_bytes=32 * MIB),
        cost_estimate=pl.CostEstimate(flops=300000000, bytes_accessed=2000000, transcendentals=500000),
    )(recv, mine)
    full = pl.pallas_call(
        finish_kernel,
        out_shape=jax.ShapeDtypeStruct(queries.shape, BF16),
        in_specs=[VMEM] * 4,
        out_specs=VMEM,
        name="finish",
        compiler_params=pltpu.CompilerParams(vmem_limit_bytes=32 * MIB),
    )(recv, mine, other, half)
    theirs_full = lax.ppermute(full, "yl", swap)
    own = pl.pallas_call(
        own_kernel,
        out_shape=jax.ShapeDtypeStruct((pairs, rows, width), F32),
        in_specs=[VMEM, HBM],
        out_specs=VMEM,
        scratch_shapes=[
            pltpu.VMEM((pairs, out_weight.shape[0], width), BF16),
            pltpu.SemaphoreType.DMA((pairs,)),
        ],
        name="project_own",
        compiler_params=pltpu.CompilerParams(vmem_limit_bytes=52 * MIB),
        cost_estimate=pl.CostEstimate(flops=300000000, bytes_accessed=8000000, transcendentals=0),
    )(full, out_weight)
    partial = pl.pallas_call(
        both_kernel,
        out_shape=jax.ShapeDtypeStruct((pairs, rows, width), BF16),
        in_specs=[VMEM] * 3,
        out_specs=VMEM,
        name="project_both",
        compiler_params=pltpu.CompilerParams(vmem_limit_bytes=32 * MIB),
    )(own, theirs_full, theirs)
    sums = lax.all_to_all(partial, "yh", 0, 0, tiled=True)
    return jnp.sum(sums.astype(F32), axis=0).astype(BF16)


def solution(mesh):
    cut = Mesh(mesh.devices.reshape(8, 4, 2, 4, 2), CTX + Y)
    placed = (
        P(CTX, Y),
        P(CTX, Y),
        P(CTX, Y),
        P(Y, None),
        P(Y, None),
        P(CTX, None),
        P(Y, None),
    )
    return jax.shard_map(
        local, mesh=cut, in_specs=placed, out_specs=P(CTX, Y), check_vma=False
    )
```

```python
import math

import jax
import jax.numpy as jnp
from jax import lax
from jax.experimental import pallas as pl
from jax.experimental.pallas import tpu as pltpu
from jax.sharding import Mesh, PartitionSpec as P

HEAD = 128
BLK = 64
NV = 32
CTX = ("z", "x", "c")
Y = ("yh", "yl")
VMEM = pl.BlockSpec(memory_space=pltpu.VMEM)
HBM = pl.BlockSpec(memory_space=pltpu.HBM)
F32 = jnp.float32
BF16 = jnp.bfloat16
LOW = -1e30
FACTOR = math.log2(math.e) / math.sqrt(HEAD)
MIB = 1024 * 1024
NUMBER, VERT = 4, 5


def iota(shape, dim):
    return lax.broadcasted_iota(jnp.int32, shape, dim)


def bits(mask):
    return jnp.where(mask, 1.0, 0.0).astype(BF16)


def pick(mask, rows):
    return jnp.dot(bits(mask), rows, preferred_element_type=F32).astype(BF16)


def pick_t(mask, rows):
    return lax.dot_general(
        bits(mask), rows, (((0,), (0,)), ((), ())), preferred_element_type=F32
    ).astype(BF16)


def dot_t(a, b):
    return lax.dot_general(a, b, (((1,), (1,)), ((), ())), preferred_element_type=F32)


def by_destination(order, rows, heads):
    lanes = rows * heads
    count = rows // 2
    spread = bits(iota((count, lanes), 0) == iota((count, lanes), 1) // (2 * heads))
    piece = jnp.dot(order.astype(F32).astype(BF16), spread, preferred_element_type=F32)
    at = iota((1, lanes), 1)
    target = piece.astype(jnp.int32) * 2 + at % 2 + (at // 2 % heads) * rows
    return iota((lanes, lanes), 0) == target


def head_rows(ref, heads):
    return jnp.concatenate([ref[:, h * HEAD : (h + 1) * HEAD] for h in range(heads)], axis=0)


def load(pairs, sems):
    moves = [pltpu.make_async_copy(a, b, sems.at[i]) for i, (a, b) in enumerate(pairs)]
    for move in moves:
        move.start()
    for move in moves:
        move.wait()


def columns(ref, j, parity):
    width = ref.shape[1] // 8
    start = pl.multiple_of((2 * j + parity) * width, width)
    return ref.at[:, pl.ds(start, width)]


def tiled_vertical(vertical):
    spread = bits(iota((NV, HEAD), 0) == iota((NV, HEAD), 1) % NV)
    return jnp.dot(vertical[...].astype(F32).astype(BF16), spread, preferred_element_type=F32)


def vertical_of(recv):
    tail = recv[0, 8:].astype(F32)
    here = iota(tail.shape, 0) == VERT
    return jnp.sum(jnp.where(here, tail, 0.0), axis=0, keepdims=True).astype(jnp.int32)


def pack_kernel(
    q_in, keys_in, values_in, order_in, vert_in, weight_in, out, kv, sent,
    q, keys, values, order, vertical, sems, wsems,
):
    parity, core = lax.axis_index("yl"), lax.axis_index("c")
    share = sent.shape[0]
    moves = [
        pltpu.make_async_copy(
            columns(weight_in, core * share + j, 1 - parity), sent.at[j], wsems.at[j]
        )
        for j in range(share)
    ]
    loads = [(order_in, order), (vert_in, vertical), (keys_in, keys), (values_in, values), (q_in, q)]
    loads = [pltpu.make_async_copy(a, b, sems.at[i]) for i, (a, b) in enumerate(loads)]
    for move in loads + moves:
        move.start()
    rows = q.shape[0]
    heads = q.shape[1] // HEAD
    count = rows // 2
    new = iota((8 * count, 1), 0)
    slot = new % 8
    source = jnp.where(slot < 4, (slot % 2) * rows + (slot // 2) * BLK + new // 8, -1)
    source = bits(iota((8 * count, 2 * rows), 1) == source)
    owner = bits(iota((8 * count, count), 1) == jnp.where(slot == NUMBER, new // 8, -1))
    diagonal = iota((count, count), 0) == iota((count, count), 1)
    for move in loads[:2]:
        move.wait()
    number = jnp.sum(jnp.where(diagonal, order[...].astype(F32), 0.0), axis=1, keepdims=True)
    number = jnp.broadcast_to(number, (count, HEAD)).astype(BF16)
    numbers = jnp.dot(owner, number, preferred_element_type=F32)
    numbers += jnp.where(slot == VERT, tiled_vertical(vertical), 0.0)
    target = bits(by_destination(order[...], rows, heads))
    for move in loads[2:]:
        move.wait()
    kv[:, :HEAD] = keys[...]
    kv[:, HEAD:] = values[...]
    kv_rows = jnp.dot(
        source, jnp.concatenate([keys[...], values[...]], axis=0), preferred_element_type=F32
    )
    out[:, 8:] = (kv_rows + numbers).astype(BF16).reshape(count, 8, HEAD)
    moved = lax.dot_general(
        target, head_rows(q, heads), (((0,), (0,)), ((), ())), preferred_element_type=F32
    )
    out[:, :8] = moved.astype(BF16).reshape(count, 8, HEAD)
    for move in moves:
        move.wait()


def split3(x):
    high = x.astype(BF16).astype(F32)
    middle = (x - high).astype(BF16).astype(F32)
    return high, middle, x - high - middle


def band_kernel(
    q_in, keys_in, values_in, order_in, offsets_in, vert_in, prev_in, out,
    q, keys, values, order, offsets, vertical, prev, sems,
):
    pairs = [(offsets_in, offsets), (vert_in, vertical), (keys_in, keys), (prev_in, prev)]
    pairs += [(values_in, values), (q_in, q), (order_in, order)]
    moves = [pltpu.make_async_copy(a, b, sems.at[i]) for i, (a, b) in enumerate(pairs)]
    for move in moves:
        move.start()
    for move in moves[:2]:
        move.wait()
    rows = q.shape[0]
    heads = q.shape[1] // HEAD
    count = rows // 2
    chips = out.shape[0]
    band = 2 * rows
    ctx = lax.axis_index(CTX)
    vert = tiled_vertical(vertical).astype(jnp.int32)
    closed = jnp.zeros((1, band), F32)
    part = iota((1, band), 1) // BLK
    for j in range(band // BLK):
        number = ctx * (rows // BLK) + (j - rows // BLK)
        hit = jnp.max(jnp.where(vert == number, 1.0, 0.0), axis=1, keepdims=True)
        hit = jnp.where(number < 0, 1.0, hit)
        closed = jnp.where(part == j, hit, closed)
    lag = rows - iota((heads, band), 1)
    table = jnp.zeros((heads, band), F32)
    offs = offsets[...]
    for k in range(offs.shape[1]):
        table = jnp.where(offs[:, k : k + 1] == lag, 1.0, table)
    for move in moves[2:]:
        move.wait()
    kb = jnp.concatenate([prev[:, :HEAD], keys[...]], axis=0)
    vb = jnp.concatenate([prev[:, HEAD:], values[...]], axis=0)
    lanes = iota((rows, HEAD), 1) % 8
    done = []
    for h in range(heads):
        spread = jnp.broadcast_to(table[h : h + 1], (rows, band))
        slash = pltpu.roll(spread, 0, 1, stride=1, stride_axis=0)
        mask = (slash > 0.5) & (closed < 0.5)
        s = jnp.where(mask, dot_t(q[:, h * HEAD : (h + 1) * HEAD], kb), LOW)
        top = jnp.max(s, axis=1, keepdims=True)
        p = jnp.where(mask, jnp.exp2((s - top) * FACTOR), 0.0)
        total = jnp.sum(p, axis=1, keepdims=True)
        o = jnp.dot(p.astype(BF16), vb, preferred_element_type=F32)
        o = o / jnp.where(total > 0.0, total, 1.0)
        sums = jnp.zeros((rows, HEAD), F32)
        for j, term in enumerate(split3(top) + split3(total)):
            sums = jnp.where(lanes == j, term, sums)
        done.append(jnp.concatenate([o.astype(BF16), sums.astype(BF16)], axis=1))
    moved = pick_t(by_destination(order[...], rows, heads), jnp.concatenate(done, axis=0))
    size = 8 * count
    own = iota((size, HEAD), 1) // 8 == iota((size, HEAD), 0) % 8
    sums = jnp.where(own, moved[:, HEAD:].astype(F32), 0.0).astype(BF16)
    new = iota((8 * chips, 1), 0)
    owner = jnp.where(new % 8 < 2, (new // 8) * 2 + new % 8, -1)
    sums = pick(iota((8 * chips, size), 1) // 8 == owner, sums)
    out[:, :16] = moved[:, :HEAD].astype(F32).reshape(chips, 16, HEAD)
    out[:, 16:] = sums.astype(F32).reshape(chips, 8, HEAD)


def select_kernel(recv, slash, out):
    vert = vertical_of(recv)
    want = ((vert // 2) * 8 + (vert % 2) * 2 + iota((1, HEAD), 1) // NV)[:, : 2 * NV]
    held = recv[:, 8:].reshape(-1, HEAD)
    picked = pick_t(iota((held.shape[0], 2 * NV), 0) == want, held)
    out[:, 2 * NV :] = slash[...]
    for chip in range(out.shape[0]):
        out[chip, : 2 * NV] = picked


def key_positions(vert, core, chips):
    vpos = vert * BLK + (iota((1, HEAD), 1) // NV) * 2 + core
    step = 2 * HEAD // NV
    return jnp.concatenate([vpos + m * step for m in range(chips * NV // HEAD)], axis=1)


def row_positions(recv, rows):
    tail = recv[:, 8:].astype(F32)
    size = 8 * tail.shape[0]
    number = jnp.sum(jnp.where(iota(tail.shape, 1) == NUMBER, tail, 0.0), axis=1, keepdims=True)
    number = jnp.broadcast_to(number, tail.shape).reshape(size, HEAD)[:, :1]
    at = iota((size, 1), 0)
    return (at // 8) * rows + number.astype(jnp.int32) * 2 + at % 2


def half_kernel(recv, mine, out):
    core = lax.axis_index("c")
    size = out.shape[0]
    rows = 2 * recv.shape[0]
    pos = key_positions(vertical_of(recv), core, mine.shape[0])
    qpos = row_positions(recv, rows)
    q = recv[:, :8].reshape(size, HEAD)
    keys = mine[:, :NV].reshape(-1, HEAD)
    vals = mine[:, NV : 2 * NV].reshape(-1, HEAD)
    lane = iota((rows, HEAD), 1)
    for b in range(size // rows):
        cut = slice(b * rows, (b + 1) * rows)
        s = jnp.where(pos <= qpos[cut], dot_t(q[cut], keys), -jnp.inf)
        top = jnp.maximum(jnp.max(s, axis=1, keepdims=True), LOW)
        p = jnp.exp2((s - top) * FACTOR)
        total = jnp.sum(p, axis=1, keepdims=True)
        out[cut, :HEAD] = jnp.dot(p.astype(BF16), vals, preferred_element_type=F32)
        out[cut, HEAD:] = jnp.where(lane == 0, top, total)


def finish_kernel(recv, mine, other, half, out):
    count = recv.shape[0]
    size = 8 * count
    rows = out.shape[0]
    heads = size // rows
    core = lax.axis_index("c")
    first = core == 0
    pos = key_positions(vertical_of(recv), 1 - core, mine.shape[0])
    qpos = row_positions(recv, rows)

    def by_owner(cut):
        a, b = cut(mine), cut(other)
        return jnp.concatenate([jnp.where(first, a, b), jnp.where(first, b, a)], axis=1)

    base = 2 * NV

    def slash_rows(ref):
        return jnp.where(
            first, ref[:, base : base + 8].astype(F32), ref[:, base + 8 : base + 16].astype(F32)
        )

    def sums_row(ref):
        tail = ref[:, base + 16 :].astype(F32)
        which = iota(tail.shape, 1)
        row = jnp.sum(jnp.where(which == core, tail, 0.0), axis=1, keepdims=True)
        return jnp.broadcast_to(row, tail.shape)

    slash = by_owner(slash_rows).reshape(size, HEAD)
    sums = by_owner(sums_row).reshape(size, HEAD)
    lane = iota((size, HEAD), 1)
    own = lane // 8 == iota((size, HEAD), 0) % 8
    top_b = jnp.sum(jnp.where(own & (lane % 8 < 3), sums, 0.0), axis=1, keepdims=True)
    total_b = jnp.sum(jnp.where(own & (lane % 8 >= 3), sums, 0.0), axis=1, keepdims=True)

    q = recv[:, :8].reshape(size, HEAD)
    keys = other[:, :NV].reshape(-1, HEAD)
    vals = other[:, NV : 2 * NV].reshape(-1, HEAD)
    done = []
    for b in range(heads):
        cut = slice(b * rows, (b + 1) * rows)
        s = jnp.where(pos <= qpos[cut], dot_t(q[cut], keys), -jnp.inf)
        top_a = half[cut, HEAD : HEAD + 1]
        top = jnp.maximum(jnp.max(s, axis=1, keepdims=True), jnp.maximum(top_a, top_b[cut]))
        p = jnp.exp2((s - top) * FACTOR)
        share_a = jnp.exp2((top_a - top) * FACTOR)
        share_b = total_b[cut] * jnp.exp2((top_b[cut] - top) * FACTOR)
        total = jnp.sum(p, axis=1, keepdims=True) + share_a * half[cut, HEAD + 1 : HEAD + 2] + share_b
        o = jnp.dot(p.astype(BF16), vals, preferred_element_type=F32)
        o += share_a * half[cut, :HEAD] + share_b * slash[cut]
        done.append((o / total).astype(BF16))
    attended = jnp.concatenate(done, axis=0)
    row = iota((rows, 1), 0)
    cols = iota((rows, size), 1)
    for h in range(heads):
        rows_h = pick(cols == (row // 2) * 8 + h * 2 + row % 2, attended)
        out[:, h * HEAD : (h + 1) * HEAD] = rows_h


def own_kernel(full, weight_in, near, far, out, theirs, weight, sems, tsems):
    parity, core = lax.axis_index("yl"), lax.axis_index("c")
    share = near.shape[0]
    moves = [
        pltpu.make_async_copy(columns(weight_in, j, parity), weight.at[j], sems.at[j])
        for j in range(out.shape[0])
    ]
    late = [
        pltpu.make_async_copy(part, theirs.at[pl.ds(first, share)], tsems.at[i])
        for i, (part, first) in enumerate(((near, core * share), (far, (1 - core) * share)))
    ]
    for move in moves + late:
        move.start()
    for j, move in enumerate(moves):
        move.wait()
        out[j] = jnp.dot(full[...], weight[j], preferred_element_type=F32)
    for move in late:
        move.wait()


def both_kernel(own, full, weight, out):
    for j in range(out.shape[0]):
        part = own[j] + jnp.dot(full[...], weight[j], preferred_element_type=F32)
        out[j] = part.astype(BF16)


def local(queries, keys, values, vertical, offsets, send_order, out_weight):
    z_n, x_n, c_n, pairs = (lax.axis_size(a) for a in ("z", "x", "c", "yh"))
    rows = queries.shape[0]
    n_ctx = z_n * x_n * c_n
    chips = z_n * x_n
    large = pltpu.CompilerParams(vmem_limit_bytes=60 * MIB)
    small = pltpu.CompilerParams(vmem_limit_bytes=16 * MIB)
    width = out_weight.shape[1] // (2 * pairs)
    columns_half = (pairs // c_n, out_weight.shape[0], width)
    held = [pltpu.VMEM(a.shape, a.dtype) for a in (queries, keys, values, send_order)]

    packed, kv, sent = pl.pallas_call(
        pack_kernel,
        out_shape=[
            jax.ShapeDtypeStruct((n_ctx, 16, HEAD), BF16),
            jax.ShapeDtypeStruct((rows, 2 * HEAD), BF16),
            jax.ShapeDtypeStruct(columns_half, BF16),
        ],
        in_specs=[HBM] * 6,
        out_specs=[VMEM, VMEM, VMEM],
        scratch_shapes=held + [pltpu.VMEM(vertical.shape, jnp.int32), pltpu.SemaphoreType.DMA((5,)), pltpu.SemaphoreType.DMA((pairs // c_n,))],
        name="pack",
        compiler_params=large,
    )(queries, keys, values, send_order, vertical, out_weight)
    recv = lax.all_to_all(packed, CTX, 0, 0, tiled=True)
    prev = lax.ppermute(kv, CTX, [(i, i + 1) for i in range(n_ctx - 1)])
    swap = [(0, 1), (1, 0)]
    sent, prev = lax.optimization_barrier((sent, prev))
    near = lax.ppermute(sent, "yl", swap)
    slash = pl.pallas_call(
        band_kernel,
        out_shape=jax.ShapeDtypeStruct((chips, 24, HEAD), F32),
        in_specs=[HBM] * 7,
        out_specs=VMEM,
        scratch_shapes=held
        + [pltpu.VMEM(a.shape, a.dtype) for a in (offsets, vertical, prev)]
        + [pltpu.SemaphoreType.DMA((7,))],
        name="slash",
        compiler_params=large,
        cost_estimate=pl.CostEstimate(flops=20000000000, bytes_accessed=1000000, transcendentals=0),
    )(queries, keys, values, send_order, offsets, vertical, prev)
    parts = pl.pallas_call(
        select_kernel,
        out_shape=jax.ShapeDtypeStruct((chips, 2 * NV + 24, HEAD), BF16),
        in_specs=[VMEM] * 2,
        out_specs=VMEM,
        name="select",
        compiler_params=small,
    )(recv, slash.astype(BF16))
    far = lax.ppermute(near, "c", swap)
    mine = lax.all_to_all(parts, ("z", "x"), 0, 0, tiled=True)
    mine, far = lax.optimization_barrier((mine, far))
    other = lax.ppermute(mine, "c", swap)
    half = pl.pallas_call(
        half_kernel,
        out_shape=jax.ShapeDtypeStruct((8 * n_ctx, 2 * HEAD), F32),
        in_specs=[VMEM] * 2,
        out_specs=VMEM,
        name="half",
        compiler_params=pltpu.CompilerParams(vmem_limit_bytes=32 * MIB),
        cost_estimate=pl.CostEstimate(flops=300000000, bytes_accessed=2000000, transcendentals=500000),
    )(recv, mine)
    full = pl.pallas_call(
        finish_kernel,
        out_shape=jax.ShapeDtypeStruct(queries.shape, BF16),
        in_specs=[VMEM] * 4,
        out_specs=VMEM,
        name="finish",
        compiler_params=pltpu.CompilerParams(vmem_limit_bytes=32 * MIB),
    )(recv, mine, other, half)
    theirs_full = lax.ppermute(full, "yl", swap)
    own, theirs = pl.pallas_call(
        own_kernel,
        out_shape=[
            jax.ShapeDtypeStruct((pairs, rows, width), F32),
            jax.ShapeDtypeStruct((pairs,) + near.shape[1:], BF16),
        ],
        in_specs=[VMEM, HBM, HBM, HBM],
        out_specs=[VMEM, VMEM],
        scratch_shapes=[
            pltpu.VMEM((pairs, out_weight.shape[0], width), BF16),
            pltpu.SemaphoreType.DMA((pairs,)),
            pltpu.SemaphoreType.DMA((2,)),
        ],
        name="project_own",
        compiler_params=pltpu.CompilerParams(vmem_limit_bytes=48 * MIB),
        cost_estimate=pl.CostEstimate(flops=300000000, bytes_accessed=8000000, transcendentals=0),
    )(full, out_weight, near, far)
    partial = pl.pallas_call(
        both_kernel,
        out_shape=jax.ShapeDtypeStruct((pairs, rows, width), BF16),
        in_specs=[VMEM] * 3,
        out_specs=VMEM,
        name="project_both",
        compiler_params=pltpu.CompilerParams(vmem_limit_bytes=32 * MIB),
    )(own, theirs_full, theirs)
    sums = lax.all_to_all(partial, "yh", 0, 0, tiled=True)
    return jnp.sum(sums.astype(F32), axis=0).astype(BF16)


def solution(mesh):
    cut = Mesh(mesh.devices.reshape(8, 4, 2, 4, 2), CTX + Y)
    placed = (
        P(CTX, Y),
        P(CTX, Y),
        P(CTX, Y),
        P(Y, None),
        P(Y, None),
        P(CTX, None),
        P(Y, None),
    )
    return jax.shard_map(
        local, mesh=cut, in_specs=placed, out_specs=P(CTX, Y), check_vma=False
    )
```

```python
import math

import jax
import jax.numpy as jnp
from jax import lax
from jax.experimental import pallas as pl
from jax.experimental.pallas import tpu as pltpu
from jax.sharding import Mesh, PartitionSpec as P

HEAD = 128
BLK = 64
NV = 32
CTX = ("z", "x", "c")
Y = ("yh", "yl")
VMEM = pl.BlockSpec(memory_space=pltpu.VMEM)
HBM = pl.BlockSpec(memory_space=pltpu.HBM)
F32 = jnp.float32
BF16 = jnp.bfloat16
LOW = -1e30
FACTOR = math.log2(math.e) / math.sqrt(HEAD)
MIB = 1024 * 1024
NUMBER, VERT = 4, 5


def iota(shape, dim):
    return lax.broadcasted_iota(jnp.int32, shape, dim)


def bits(mask):
    return jnp.where(mask, 1.0, 0.0).astype(BF16)


def pick(mask, rows):
    return jnp.dot(bits(mask), rows, preferred_element_type=F32).astype(BF16)


def pick_t(mask, rows):
    return lax.dot_general(
        bits(mask), rows, (((0,), (0,)), ((), ())), preferred_element_type=F32
    ).astype(BF16)


def dot_t(a, b):
    return lax.dot_general(a, b, (((1,), (1,)), ((), ())), preferred_element_type=F32)


def by_destination(order, rows, heads):
    lanes = rows * heads
    count = rows // 2
    spread = bits(iota((count, lanes), 0) == iota((count, lanes), 1) // (2 * heads))
    piece = jnp.dot(order.astype(F32).astype(BF16), spread, preferred_element_type=F32)
    at = iota((1, lanes), 1)
    target = piece.astype(jnp.int32) * 2 + at % 2 + (at // 2 % heads) * rows
    return iota((lanes, lanes), 0) == target


def head_rows(ref, heads):
    return jnp.concatenate([ref[:, h * HEAD : (h + 1) * HEAD] for h in range(heads)], axis=0)


def load(pairs, sems):
    moves = [pltpu.make_async_copy(a, b, sems.at[i]) for i, (a, b) in enumerate(pairs)]
    for move in moves:
        move.start()
    for move in moves:
        move.wait()


def columns(ref, j, parity):
    width = ref.shape[1] // 8
    start = pl.multiple_of((2 * j + parity) * width, width)
    return ref.at[:, pl.ds(start, width)]


def tiled_vertical(vertical):
    spread = bits(iota((NV, HEAD), 0) == iota((NV, HEAD), 1) % NV)
    return jnp.dot(vertical[...].astype(F32).astype(BF16), spread, preferred_element_type=F32)


def vertical_of(recv):
    tail = recv[0, 8:].astype(F32)
    here = iota(tail.shape, 0) == VERT
    return jnp.sum(jnp.where(here, tail, 0.0), axis=0, keepdims=True).astype(jnp.int32)


def pack_kernel(
    q_in, keys_in, values_in, order_in, vert_in, weight_in, out, kv, sent,
    q, keys, values, order, vertical, sems, wsems,
):
    parity, core = lax.axis_index("yl"), lax.axis_index("c")
    share = sent.shape[0]
    moves = [
        pltpu.make_async_copy(
            columns(weight_in, core * share + j, 1 - parity), sent.at[j], wsems.at[j]
        )
        for j in range(share)
    ]
    loads = [(order_in, order), (vert_in, vertical), (keys_in, keys), (values_in, values), (q_in, q)]
    loads = [pltpu.make_async_copy(a, b, sems.at[i]) for i, (a, b) in enumerate(loads)]
    for move in loads + moves:
        move.start()
    rows = q.shape[0]
    heads = q.shape[1] // HEAD
    count = rows // 2
    new = iota((8 * count, 1), 0)
    slot = new % 8
    source = jnp.where(slot < 4, (slot % 2) * rows + (slot // 2) * BLK + new // 8, -1)
    source = bits(iota((8 * count, 2 * rows), 1) == source)
    owner = bits(iota((8 * count, count), 1) == jnp.where(slot == NUMBER, new // 8, -1))
    diagonal = iota((count, count), 0) == iota((count, count), 1)
    for move in loads[:2]:
        move.wait()
    number = jnp.sum(jnp.where(diagonal, order[...].astype(F32), 0.0), axis=1, keepdims=True)
    number = jnp.broadcast_to(number, (count, HEAD)).astype(BF16)
    numbers = jnp.dot(owner, number, preferred_element_type=F32)
    numbers += jnp.where(slot == VERT, tiled_vertical(vertical), 0.0)
    target = bits(by_destination(order[...], rows, heads))
    for move in loads[2:]:
        move.wait()
    kv[:, :HEAD] = keys[...]
    kv[:, HEAD:] = values[...]
    kv_rows = jnp.dot(
        source, jnp.concatenate([keys[...], values[...]], axis=0), preferred_element_type=F32
    )
    out[:, 8:] = (kv_rows + numbers).astype(BF16).reshape(count, 8, HEAD)
    moved = lax.dot_general(
        target, head_rows(q, heads), (((0,), (0,)), ((), ())), preferred_element_type=F32
    )
    out[:, :8] = moved.astype(BF16).reshape(count, 8, HEAD)
    for move in moves:
        move.wait()


def split3(x):
    high = x.astype(BF16).astype(F32)
    middle = (x - high).astype(BF16).astype(F32)
    return high, middle, x - high - middle


def band_kernel(
    q_in, keys_in, values_in, order_in, offsets_in, vert_in, prev_in, out,
    q, keys, values, order, offsets, vertical, prev, sems,
):
    pairs = [(offsets_in, offsets), (vert_in, vertical), (keys_in, keys), (prev_in, prev)]
    pairs += [(values_in, values), (q_in, q), (order_in, order)]
    moves = [pltpu.make_async_copy(a, b, sems.at[i]) for i, (a, b) in enumerate(pairs)]
    for move in moves:
        move.start()
    for move in moves[:2]:
        move.wait()
    rows = q.shape[0]
    heads = q.shape[1] // HEAD
    count = rows // 2
    chips = out.shape[0]
    band = 2 * rows
    ctx = lax.axis_index(CTX)
    vert = tiled_vertical(vertical).astype(jnp.int32)
    closed = jnp.zeros((1, band), F32)
    part = iota((1, band), 1) // BLK
    for j in range(band // BLK):
        number = ctx * (rows // BLK) + (j - rows // BLK)
        hit = jnp.max(jnp.where(vert == number, 1.0, 0.0), axis=1, keepdims=True)
        hit = jnp.where(number < 0, 1.0, hit)
        closed = jnp.where(part == j, hit, closed)
    lag = rows - iota((heads, band), 1)
    table = jnp.zeros((heads, band), F32)
    offs = offsets[...]
    for k in range(offs.shape[1]):
        table = jnp.where(offs[:, k : k + 1] == lag, 1.0, table)
    for move in moves[2:]:
        move.wait()
    kb = jnp.concatenate([prev[:, :HEAD], keys[...]], axis=0)
    vb = jnp.concatenate([prev[:, HEAD:], values[...]], axis=0)
    lanes = iota((rows, HEAD), 1) % 8
    done = []
    for h in range(heads):
        spread = jnp.broadcast_to(table[h : h + 1], (rows, band))
        slash = pltpu.roll(spread, 0, 1, stride=1, stride_axis=0)
        mask = (slash > 0.5) & (closed < 0.5)
        s = jnp.where(mask, dot_t(q[:, h * HEAD : (h + 1) * HEAD], kb), LOW)
        top = jnp.max(s, axis=1, keepdims=True)
        p = jnp.where(mask, jnp.exp2((s - top) * FACTOR), 0.0)
        total = jnp.sum(p, axis=1, keepdims=True)
        o = jnp.dot(p.astype(BF16), vb, preferred_element_type=F32)
        o = o / jnp.where(total > 0.0, total, 1.0)
        sums = jnp.zeros((rows, HEAD), F32)
        for j, term in enumerate(split3(top) + split3(total)):
            sums = jnp.where(lanes == j, term, sums)
        done.append(jnp.concatenate([o.astype(BF16), sums.astype(BF16)], axis=1))
    moved = pick_t(by_destination(order[...], rows, heads), jnp.concatenate(done, axis=0))
    size = 8 * count
    own = iota((size, HEAD), 1) // 8 == iota((size, HEAD), 0) % 8
    sums = jnp.where(own, moved[:, HEAD:].astype(F32), 0.0).astype(BF16)
    new = iota((8 * chips, 1), 0)
    owner = jnp.where(new % 8 < 2, (new // 8) * 2 + new % 8, -1)
    sums = pick(iota((8 * chips, size), 1) // 8 == owner, sums)
    out[:, :16] = moved[:, :HEAD].astype(F32).reshape(chips, 16, HEAD)
    out[:, 16:] = sums.astype(F32).reshape(chips, 8, HEAD)


def select_kernel(recv, slash, out):
    vert = vertical_of(recv)
    want = ((vert // 2) * 8 + (vert % 2) * 2 + iota((1, HEAD), 1) // NV)[:, : 2 * NV]
    held = recv[:, 8:].reshape(-1, HEAD)
    picked = pick_t(iota((held.shape[0], 2 * NV), 0) == want, held)
    out[:, 2 * NV :] = slash[...]
    for chip in range(out.shape[0]):
        out[chip, : 2 * NV] = picked


def key_positions(vert, core, chips):
    vpos = vert * BLK + (iota((1, HEAD), 1) // NV) * 2 + core
    step = 2 * HEAD // NV
    return jnp.concatenate([vpos + m * step for m in range(chips * NV // HEAD)], axis=1)


def row_positions(recv, rows):
    tail = recv[:, 8:].astype(F32)
    size = 8 * tail.shape[0]
    number = jnp.sum(jnp.where(iota(tail.shape, 1) == NUMBER, tail, 0.0), axis=1, keepdims=True)
    number = jnp.broadcast_to(number, tail.shape).reshape(size, HEAD)[:, :1]
    at = iota((size, 1), 0)
    return (at // 8) * rows + number.astype(jnp.int32) * 2 + at % 2


def half_kernel(recv, mine, out):
    core = lax.axis_index("c")
    size = out.shape[0]
    rows = 2 * recv.shape[0]
    pos = key_positions(vertical_of(recv), core, mine.shape[0])
    qpos = row_positions(recv, rows)
    q = recv[:, :8].reshape(size, HEAD)
    keys = mine[:, :NV].reshape(-1, HEAD)
    vals = mine[:, NV : 2 * NV].reshape(-1, HEAD)
    lane = iota((rows, HEAD), 1)
    for b in range(size // rows):
        cut = slice(b * rows, (b + 1) * rows)
        s = jnp.where(pos <= qpos[cut], dot_t(q[cut], keys), -jnp.inf)
        top = jnp.maximum(jnp.max(s, axis=1, keepdims=True), LOW)
        p = jnp.exp2((s - top) * FACTOR)
        total = jnp.sum(p, axis=1, keepdims=True)
        out[cut, :HEAD] = jnp.dot(p.astype(BF16), vals, preferred_element_type=F32)
        out[cut, HEAD:] = jnp.where(lane == 0, top, total)


def finish_kernel(recv, mine, other, half, out):
    count = recv.shape[0]
    size = 8 * count
    rows = out.shape[0]
    heads = size // rows
    core = lax.axis_index("c")
    first = core == 0
    pos = key_positions(vertical_of(recv), 1 - core, mine.shape[0])
    qpos = row_positions(recv, rows)

    def by_owner(cut):
        a, b = cut(mine), cut(other)
        return jnp.concatenate([jnp.where(first, a, b), jnp.where(first, b, a)], axis=1)

    base = 2 * NV

    def slash_rows(ref):
        return jnp.where(
            first, ref[:, base : base + 8].astype(F32), ref[:, base + 8 : base + 16].astype(F32)
        )

    def sums_row(ref):
        tail = ref[:, base + 16 :].astype(F32)
        which = iota(tail.shape, 1)
        row = jnp.sum(jnp.where(which == core, tail, 0.0), axis=1, keepdims=True)
        return jnp.broadcast_to(row, tail.shape)

    slash = by_owner(slash_rows).reshape(size, HEAD)
    sums = by_owner(sums_row).reshape(size, HEAD)
    lane = iota((size, HEAD), 1)
    own = lane // 8 == iota((size, HEAD), 0) % 8
    top_b = jnp.sum(jnp.where(own & (lane % 8 < 3), sums, 0.0), axis=1, keepdims=True)
    total_b = jnp.sum(jnp.where(own & (lane % 8 >= 3), sums, 0.0), axis=1, keepdims=True)

    q = recv[:, :8].reshape(size, HEAD)
    keys = other[:, :NV].reshape(-1, HEAD)
    vals = other[:, NV : 2 * NV].reshape(-1, HEAD)
    done = []
    for b in range(heads):
        cut = slice(b * rows, (b + 1) * rows)
        s = jnp.where(pos <= qpos[cut], dot_t(q[cut], keys), -jnp.inf)
        top_a = half[cut, HEAD : HEAD + 1]
        top = jnp.maximum(jnp.max(s, axis=1, keepdims=True), jnp.maximum(top_a, top_b[cut]))
        p = jnp.exp2((s - top) * FACTOR)
        share_a = jnp.exp2((top_a - top) * FACTOR)
        share_b = total_b[cut] * jnp.exp2((top_b[cut] - top) * FACTOR)
        total = jnp.sum(p, axis=1, keepdims=True) + share_a * half[cut, HEAD + 1 : HEAD + 2] + share_b
        o = jnp.dot(p.astype(BF16), vals, preferred_element_type=F32)
        o += share_a * half[cut, :HEAD] + share_b * slash[cut]
        done.append((o / total).astype(BF16))
    attended = jnp.concatenate(done, axis=0)
    row = iota((rows, 1), 0)
    cols = iota((rows, size), 1)
    for h in range(heads):
        rows_h = pick(cols == (row // 2) * 8 + h * 2 + row % 2, attended)
        out[:, h * HEAD : (h + 1) * HEAD] = rows_h


def own_kernel(full, weight_in, near, far, out, theirs, weight, sems, tsems):
    parity, core = lax.axis_index("yl"), lax.axis_index("c")
    pair = lax.axis_index("yh")
    share, pairs = near.shape[0], out.shape[0]
    moves = [
        pltpu.make_async_copy(
            columns(weight_in, lax.rem(pair + d, pairs), parity), weight.at[d], sems.at[d]
        )
        for d in range(pairs)
    ]
    late = [
        pltpu.make_async_copy(
            part.at[i], theirs.at[lax.rem(first + i + pairs - pair, pairs)], tsems.at[n * share + i]
        )
        for n, (part, first) in enumerate(((near, core * share), (far, (1 - core) * share)))
        for i in range(share)
    ]
    for move in moves + late:
        move.start()
    for j, move in enumerate(moves):
        move.wait()
        out[j] = jnp.dot(full[...], weight[j], preferred_element_type=F32)
    for move in late:
        move.wait()


def both_kernel(own, full, weight, *outs):
    for d, out in enumerate(outs):
        part = own[d] + jnp.dot(full[...], weight[d], preferred_element_type=F32)
        out[...] = part.astype(BF16)


def local(queries, keys, values, vertical, offsets, send_order, out_weight):
    z_n, x_n, c_n, pairs = (lax.axis_size(a) for a in ("z", "x", "c", "yh"))
    rows = queries.shape[0]
    n_ctx = z_n * x_n * c_n
    chips = z_n * x_n
    large = pltpu.CompilerParams(vmem_limit_bytes=60 * MIB)
    small = pltpu.CompilerParams(vmem_limit_bytes=16 * MIB)
    width = out_weight.shape[1] // (2 * pairs)
    columns_half = (pairs // c_n, out_weight.shape[0], width)
    held = [pltpu.VMEM(a.shape, a.dtype) for a in (queries, keys, values, send_order)]

    packed, kv, sent = pl.pallas_call(
        pack_kernel,
        out_shape=[
            jax.ShapeDtypeStruct((n_ctx, 16, HEAD), BF16),
            jax.ShapeDtypeStruct((rows, 2 * HEAD), BF16),
            jax.ShapeDtypeStruct(columns_half, BF16),
        ],
        in_specs=[HBM] * 6,
        out_specs=[VMEM, VMEM, VMEM],
        scratch_shapes=held + [pltpu.VMEM(vertical.shape, jnp.int32), pltpu.SemaphoreType.DMA((5,)), pltpu.SemaphoreType.DMA((pairs // c_n,))],
        name="pack",
        compiler_params=large,
    )(queries, keys, values, send_order, vertical, out_weight)
    recv = lax.all_to_all(packed, CTX, 0, 0, tiled=True)
    prev = lax.ppermute(kv, CTX, [(i, i + 1) for i in range(n_ctx - 1)])
    swap = [(0, 1), (1, 0)]
    sent, prev = lax.optimization_barrier((sent, prev))
    near = lax.ppermute(sent, "yl", swap)
    slash = pl.pallas_call(
        band_kernel,
        out_shape=jax.ShapeDtypeStruct((chips, 24, HEAD), F32),
        in_specs=[HBM] * 7,
        out_specs=VMEM,
        scratch_shapes=held
        + [pltpu.VMEM(a.shape, a.dtype) for a in (offsets, vertical, prev)]
        + [pltpu.SemaphoreType.DMA((7,))],
        name="slash",
        compiler_params=large,
        cost_estimate=pl.CostEstimate(flops=20000000000, bytes_accessed=1000000, transcendentals=0),
    )(queries, keys, values, send_order, offsets, vertical, prev)
    parts = pl.pallas_call(
        select_kernel,
        out_shape=jax.ShapeDtypeStruct((chips, 2 * NV + 24, HEAD), BF16),
        in_specs=[VMEM] * 2,
        out_specs=VMEM,
        name="select",
        compiler_params=small,
    )(recv, slash.astype(BF16))
    far = lax.ppermute(near, "c", swap)
    mine = lax.all_to_all(parts, ("z", "x"), 0, 0, tiled=True)
    mine, far = lax.optimization_barrier((mine, far))
    other = lax.ppermute(mine, "c", swap)
    half = pl.pallas_call(
        half_kernel,
        out_shape=jax.ShapeDtypeStruct((8 * n_ctx, 2 * HEAD), F32),
        in_specs=[VMEM] * 2,
        out_specs=VMEM,
        name="half",
        compiler_params=pltpu.CompilerParams(vmem_limit_bytes=32 * MIB),
        cost_estimate=pl.CostEstimate(flops=300000000, bytes_accessed=2000000, transcendentals=500000),
    )(recv, mine)
    full = pl.pallas_call(
        finish_kernel,
        out_shape=jax.ShapeDtypeStruct(queries.shape, BF16),
        in_specs=[VMEM] * 4,
        out_specs=VMEM,
        name="finish",
        compiler_params=pltpu.CompilerParams(vmem_limit_bytes=32 * MIB),
    )(recv, mine, other, half)
    theirs_full = lax.ppermute(full, "yl", swap)
    own, theirs = pl.pallas_call(
        own_kernel,
        out_shape=[
            jax.ShapeDtypeStruct((pairs, rows, width), F32),
            jax.ShapeDtypeStruct((pairs,) + near.shape[1:], BF16),
        ],
        in_specs=[VMEM, HBM, HBM, HBM],
        out_specs=[VMEM, VMEM],
        scratch_shapes=[
            pltpu.VMEM((pairs, out_weight.shape[0], width), BF16),
            pltpu.SemaphoreType.DMA((pairs,)),
            pltpu.SemaphoreType.DMA((pairs,)),
        ],
        name="project_own",
        compiler_params=pltpu.CompilerParams(vmem_limit_bytes=48 * MIB),
        cost_estimate=pl.CostEstimate(flops=300000000, bytes_accessed=8000000, transcendentals=0),
    )(full, out_weight, near, far)
    partial = pl.pallas_call(
        both_kernel,
        out_shape=[jax.ShapeDtypeStruct((rows, width), BF16)] * pairs,
        in_specs=[VMEM] * 3,
        out_specs=[VMEM] * pairs,
        name="project_both",
        compiler_params=pltpu.CompilerParams(vmem_limit_bytes=32 * MIB),
    )(own, theirs_full, theirs)
    total = partial[0].astype(F32)
    for d in range(1, pairs):
        route = [(p, (p + d) % pairs) for p in range(pairs)]
        total = total + lax.ppermute(partial[d], "yh", route).astype(F32)
    return total.astype(BF16)


def solution(mesh):
    cut = Mesh(mesh.devices.reshape(8, 4, 2, 4, 2), CTX + Y)
    placed = (
        P(CTX, Y),
        P(CTX, Y),
        P(CTX, Y),
        P(Y, None),
        P(Y, None),
        P(CTX, None),
        P(Y, None),
    )
    return jax.shard_map(
        local, mesh=cut, in_specs=placed, out_specs=P(CTX, Y), check_vma=False
    )
```

```python
import math

import jax
import jax.numpy as jnp
from jax import lax
from jax.experimental import pallas as pl
from jax.experimental.pallas import tpu as pltpu
from jax.sharding import Mesh, PartitionSpec as P

HEAD = 128
BLK = 64
NV = 32
CTX = ("z", "x", "c")
Y = ("yh", "yl")
VMEM = pl.BlockSpec(memory_space=pltpu.VMEM)
HBM = pl.BlockSpec(memory_space=pltpu.HBM)
F32 = jnp.float32
BF16 = jnp.bfloat16
LOW = -1e30
FACTOR = math.log2(math.e) / math.sqrt(HEAD)
MIB = 1024 * 1024
NUMBER, VERT = 4, 5


def iota(shape, dim):
    return lax.broadcasted_iota(jnp.int32, shape, dim)


def bits(mask):
    return jnp.where(mask, 1.0, 0.0).astype(BF16)


def pick(mask, rows):
    return jnp.dot(bits(mask), rows, preferred_element_type=F32).astype(BF16)


def pick_t(mask, rows):
    return lax.dot_general(
        bits(mask), rows, (((0,), (0,)), ((), ())), preferred_element_type=F32
    ).astype(BF16)


def dot_t(a, b):
    return lax.dot_general(a, b, (((1,), (1,)), ((), ())), preferred_element_type=F32)


def by_destination(order, rows, heads):
    lanes = rows * heads
    count = rows // 2
    spread = bits(iota((count, lanes), 0) == iota((count, lanes), 1) // (2 * heads))
    piece = jnp.dot(order.astype(F32).astype(BF16), spread, preferred_element_type=F32)
    at = iota((1, lanes), 1)
    target = piece.astype(jnp.int32) * 2 + at % 2 + (at // 2 % heads) * rows
    return iota((lanes, lanes), 0) == target


def head_rows(ref, heads):
    return jnp.concatenate([ref[:, h * HEAD : (h + 1) * HEAD] for h in range(heads)], axis=0)


def load(pairs, sems):
    moves = [pltpu.make_async_copy(a, b, sems.at[i]) for i, (a, b) in enumerate(pairs)]
    for move in moves:
        move.start()
    for move in moves:
        move.wait()


def columns(ref, j, parity):
    width = ref.shape[1] // 8
    start = pl.multiple_of((2 * j + parity) * width, width)
    return ref.at[:, pl.ds(start, width)]


def tiled_vertical(vertical):
    spread = bits(iota((NV, HEAD), 0) == iota((NV, HEAD), 1) % NV)
    return jnp.dot(vertical[...].astype(F32).astype(BF16), spread, preferred_element_type=F32)


def vertical_of(recv):
    tail = recv[0, 8:].astype(F32)
    here = iota(tail.shape, 0) == VERT
    return jnp.sum(jnp.where(here, tail, 0.0), axis=0, keepdims=True).astype(jnp.int32)


def pack_kernel(
    q_in, keys_in, values_in, order_in, vert_in, weight_in, out, kv, sent,
    q, keys, values, order, vertical, sems, wsems,
):
    parity, core = lax.axis_index("yl"), lax.axis_index("c")
    share = sent.shape[0]
    moves = [
        pltpu.make_async_copy(
            columns(weight_in, core * share + j, 1 - parity), sent.at[j], wsems.at[j]
        )
        for j in range(share)
    ]
    loads = [(order_in, order), (vert_in, vertical), (keys_in, keys), (values_in, values), (q_in, q)]
    loads = [pltpu.make_async_copy(a, b, sems.at[i]) for i, (a, b) in enumerate(loads)]
    for move in loads + moves:
        move.start()
    rows = q.shape[0]
    heads = q.shape[1] // HEAD
    count = rows // 2
    new = iota((8 * count, 1), 0)
    slot = new % 8
    source = jnp.where(slot < 4, (slot % 2) * rows + (slot // 2) * BLK + new // 8, -1)
    source = bits(iota((8 * count, 2 * rows), 1) == source)
    owner = bits(iota((8 * count, count), 1) == jnp.where(slot == NUMBER, new // 8, -1))
    diagonal = iota((count, count), 0) == iota((count, count), 1)
    for move in loads[:2]:
        move.wait()
    number = jnp.sum(jnp.where(diagonal, order[...].astype(F32), 0.0), axis=1, keepdims=True)
    number = jnp.broadcast_to(number, (count, HEAD)).astype(BF16)
    numbers = jnp.dot(owner, number, preferred_element_type=F32)
    numbers += jnp.where(slot == VERT, tiled_vertical(vertical), 0.0)
    target = bits(by_destination(order[...], rows, heads))
    for move in loads[2:]:
        move.wait()
    kv[:, :HEAD] = keys[...]
    kv[:, HEAD:] = values[...]
    kv_rows = jnp.dot(
        source, jnp.concatenate([keys[...], values[...]], axis=0), preferred_element_type=F32
    )
    out[:, 8:] = (kv_rows + numbers).astype(BF16).reshape(count, 8, HEAD)
    moved = lax.dot_general(
        target, head_rows(q, heads), (((0,), (0,)), ((), ())), preferred_element_type=F32
    )
    out[:, :8] = moved.astype(BF16).reshape(count, 8, HEAD)
    for move in moves:
        move.wait()


def split3(x):
    high = x.astype(BF16).astype(F32)
    middle = (x - high).astype(BF16).astype(F32)
    return high, middle, x - high - middle


def band_kernel(
    q_in, keys_in, values_in, order_in, offsets_in, vert_in, prev_in, out,
    q, keys, values, order, offsets, vertical, prev, sems,
):
    pairs = [(offsets_in, offsets), (vert_in, vertical), (keys_in, keys), (prev_in, prev)]
    pairs += [(values_in, values), (q_in, q), (order_in, order)]
    moves = [pltpu.make_async_copy(a, b, sems.at[i]) for i, (a, b) in enumerate(pairs)]
    for move in moves:
        move.start()
    for move in moves[:2]:
        move.wait()
    rows = q.shape[0]
    heads = q.shape[1] // HEAD
    count = rows // 2
    chips = out.shape[0]
    band = 2 * rows
    ctx = lax.axis_index(CTX)
    vert = tiled_vertical(vertical).astype(jnp.int32)
    closed = jnp.zeros((1, band), F32)
    part = iota((1, band), 1) // BLK
    for j in range(band // BLK):
        number = ctx * (rows // BLK) + (j - rows // BLK)
        hit = jnp.max(jnp.where(vert == number, 1.0, 0.0), axis=1, keepdims=True)
        hit = jnp.where(number < 0, 1.0, hit)
        closed = jnp.where(part == j, hit, closed)
    lag = rows - iota((heads, band), 1)
    table = jnp.zeros((heads, band), F32)
    offs = offsets[...]
    for k in range(offs.shape[1]):
        table = jnp.where(offs[:, k : k + 1] == lag, 1.0, table)
    for move in moves[2:]:
        move.wait()
    kb = jnp.concatenate([prev[:, :HEAD], keys[...]], axis=0)
    vb = jnp.concatenate([prev[:, HEAD:], values[...]], axis=0)
    lanes = iota((rows, HEAD), 1) % 8
    done = []
    for h in range(heads):
        spread = jnp.broadcast_to(table[h : h + 1], (rows, band))
        slash = pltpu.roll(spread, 0, 1, stride=1, stride_axis=0)
        mask = (slash > 0.5) & (closed < 0.5)
        s = jnp.where(mask, dot_t(q[:, h * HEAD : (h + 1) * HEAD], kb), LOW)
        top = jnp.max(s, axis=1, keepdims=True)
        p = jnp.where(mask, jnp.exp2((s - top) * FACTOR), 0.0)
        total = jnp.sum(p, axis=1, keepdims=True)
        o = jnp.dot(p.astype(BF16), vb, preferred_element_type=F32)
        o = o / jnp.where(total > 0.0, total, 1.0)
        sums = jnp.zeros((rows, HEAD), F32)
        for j, term in enumerate(split3(top) + split3(total)):
            sums = jnp.where(lanes == j, term, sums)
        done.append(jnp.concatenate([o.astype(BF16), sums.astype(BF16)], axis=1))
    moved = pick_t(by_destination(order[...], rows, heads), jnp.concatenate(done, axis=0))
    size = 8 * count
    own = iota((size, HEAD), 1) // 8 == iota((size, HEAD), 0) % 8
    sums = jnp.where(own, moved[:, HEAD:].astype(F32), 0.0).astype(BF16)
    new = iota((8 * chips, 1), 0)
    owner = jnp.where(new % 8 < 2, (new // 8) * 2 + new % 8, -1)
    sums = pick(iota((8 * chips, size), 1) // 8 == owner, sums)
    out[:, :16] = moved[:, :HEAD].astype(F32).reshape(chips, 16, HEAD)
    out[:, 16:] = sums.astype(F32).reshape(chips, 8, HEAD)


def select_kernel(recv, slash, out):
    vert = vertical_of(recv)
    want = ((vert // 2) * 8 + (vert % 2) * 2 + iota((1, HEAD), 1) // NV)[:, : 2 * NV]
    held = recv[:, 8:].reshape(-1, HEAD)
    picked = pick_t(iota((held.shape[0], 2 * NV), 0) == want, held)
    out[:, 2 * NV :] = slash[...]
    for chip in range(out.shape[0]):
        out[chip, : 2 * NV] = picked


def key_positions(vert, core, chips):
    vpos = vert * BLK + (iota((1, HEAD), 1) // NV) * 2 + core
    step = 2 * HEAD // NV
    return jnp.concatenate([vpos + m * step for m in range(chips * NV // HEAD)], axis=1)


def row_positions(recv, rows):
    tail = recv[:, 8:].astype(F32)
    size = 8 * tail.shape[0]
    number = jnp.sum(jnp.where(iota(tail.shape, 1) == NUMBER, tail, 0.0), axis=1, keepdims=True)
    number = jnp.broadcast_to(number, tail.shape).reshape(size, HEAD)[:, :1]
    at = iota((size, 1), 0)
    return (at // 8) * rows + number.astype(jnp.int32) * 2 + at % 2


def half_kernel(recv, mine, out):
    core = lax.axis_index("c")
    size = out.shape[0]
    rows = 2 * recv.shape[0]
    pos = key_positions(vertical_of(recv), core, mine.shape[0])
    qpos = row_positions(recv, rows)
    q = recv[:, :8].reshape(size, HEAD)
    keys = mine[:, :NV].reshape(-1, HEAD)
    vals = mine[:, NV : 2 * NV].reshape(-1, HEAD)
    lane = iota((rows, HEAD), 1)
    for b in range(size // rows):
        cut = slice(b * rows, (b + 1) * rows)
        s = jnp.where(pos <= qpos[cut], dot_t(q[cut], keys), -jnp.inf)
        top = jnp.maximum(jnp.max(s, axis=1, keepdims=True), LOW)
        p = jnp.exp2((s - top) * FACTOR)
        total = jnp.sum(p, axis=1, keepdims=True)
        out[cut, :HEAD] = jnp.dot(p.astype(BF16), vals, preferred_element_type=F32)
        out[cut, HEAD:] = jnp.where(lane == 0, top, total)


def finish_kernel(recv, mine, other, half, out):
    count = recv.shape[0]
    size = 8 * count
    rows = out.shape[0]
    heads = size // rows
    core = lax.axis_index("c")
    first = core == 0
    pos = key_positions(vertical_of(recv), 1 - core, mine.shape[0])
    qpos = row_positions(recv, rows)

    def by_owner(cut):
        a, b = cut(mine), cut(other)
        return jnp.concatenate([jnp.where(first, a, b), jnp.where(first, b, a)], axis=1)

    base = 2 * NV

    def slash_rows(ref):
        return jnp.where(
            first, ref[:, base : base + 8].astype(F32), ref[:, base + 8 : base + 16].astype(F32)
        )

    def sums_row(ref):
        tail = ref[:, base + 16 :].astype(F32)
        which = iota(tail.shape, 1)
        row = jnp.sum(jnp.where(which == core, tail, 0.0), axis=1, keepdims=True)
        return jnp.broadcast_to(row, tail.shape)

    slash = by_owner(slash_rows).reshape(size, HEAD)
    sums = by_owner(sums_row).reshape(size, HEAD)
    lane = iota((size, HEAD), 1)
    own = lane // 8 == iota((size, HEAD), 0) % 8
    top_b = jnp.sum(jnp.where(own & (lane % 8 < 3), sums, 0.0), axis=1, keepdims=True)
    total_b = jnp.sum(jnp.where(own & (lane % 8 >= 3), sums, 0.0), axis=1, keepdims=True)

    q = recv[:, :8].reshape(size, HEAD)
    keys = other[:, :NV].reshape(-1, HEAD)
    vals = other[:, NV : 2 * NV].reshape(-1, HEAD)
    done = []
    for b in range(heads):
        cut = slice(b * rows, (b + 1) * rows)
        s = jnp.where(pos <= qpos[cut], dot_t(q[cut], keys), -jnp.inf)
        top_a = half[cut, HEAD : HEAD + 1]
        top = jnp.maximum(jnp.max(s, axis=1, keepdims=True), jnp.maximum(top_a, top_b[cut]))
        p = jnp.exp2((s - top) * FACTOR)
        share_a = jnp.exp2((top_a - top) * FACTOR)
        share_b = total_b[cut] * jnp.exp2((top_b[cut] - top) * FACTOR)
        total = jnp.sum(p, axis=1, keepdims=True) + share_a * half[cut, HEAD + 1 : HEAD + 2] + share_b
        o = jnp.dot(p.astype(BF16), vals, preferred_element_type=F32)
        o += share_a * half[cut, :HEAD] + share_b * slash[cut]
        done.append((o / total).astype(BF16))
    attended = jnp.concatenate(done, axis=0)
    row = iota((rows, 1), 0)
    cols = iota((rows, size), 1)
    for h in range(heads):
        rows_h = pick(cols == (row // 2) * 8 + h * 2 + row % 2, attended)
        out[:, h * HEAD : (h + 1) * HEAD] = rows_h


def own_kernel(full, weight_in, near, far, out, theirs, weight, sems, tsems):
    parity, core = lax.axis_index("yl"), lax.axis_index("c")
    share = near.shape[0]
    moves = [
        pltpu.make_async_copy(columns(weight_in, j, parity), weight.at[j], sems.at[j])
        for j in range(out.shape[0])
    ]
    late = [
        pltpu.make_async_copy(part, theirs.at[pl.ds(first, share)], tsems.at[i])
        for i, (part, first) in enumerate(((near, core * share), (far, (1 - core) * share)))
    ]
    for move in moves + late:
        move.start()
    for j, move in enumerate(moves):
        move.wait()
        out[j] = jnp.dot(full[...], weight[j], preferred_element_type=F32)
    for move in late:
        move.wait()


def both_kernel(own, full, weight, out):
    for j in range(out.shape[0]):
        part = own[j] + jnp.dot(full[...], weight[j], preferred_element_type=F32)
        out[j] = part.astype(BF16)


def local(queries, keys, values, vertical, offsets, send_order, out_weight):
    z_n, x_n, c_n, pairs = (lax.axis_size(a) for a in ("z", "x", "c", "yh"))
    rows = queries.shape[0]
    n_ctx = z_n * x_n * c_n
    chips = z_n * x_n
    large = pltpu.CompilerParams(vmem_limit_bytes=60 * MIB)
    small = pltpu.CompilerParams(vmem_limit_bytes=16 * MIB)
    width = out_weight.shape[1] // (2 * pairs)
    columns_half = (pairs // c_n, out_weight.shape[0], width)
    held = [pltpu.VMEM(a.shape, a.dtype) for a in (queries, keys, values, send_order)]

    packed, kv, sent = pl.pallas_call(
        pack_kernel,
        out_shape=[
            jax.ShapeDtypeStruct((n_ctx, 16, HEAD), BF16),
            jax.ShapeDtypeStruct((rows, 2 * HEAD), BF16),
            jax.ShapeDtypeStruct(columns_half, BF16),
        ],
        in_specs=[HBM] * 6,
        out_specs=[VMEM, VMEM, VMEM],
        scratch_shapes=held + [pltpu.VMEM(vertical.shape, jnp.int32), pltpu.SemaphoreType.DMA((5,)), pltpu.SemaphoreType.DMA((pairs // c_n,))],
        name="pack",
        compiler_params=large,
    )(queries, keys, values, send_order, vertical, out_weight)
    recv = lax.all_to_all(packed, CTX, 0, 0, tiled=True)
    prev = lax.ppermute(kv, CTX, [(i, i + 1) for i in range(n_ctx - 1)])
    swap = [(0, 1), (1, 0)]
    near = lax.ppermute(sent, "yl", swap)
    slash = pl.pallas_call(
        band_kernel,
        out_shape=jax.ShapeDtypeStruct((chips, 24, HEAD), F32),
        in_specs=[HBM] * 7,
        out_specs=VMEM,
        scratch_shapes=held
        + [pltpu.VMEM(a.shape, a.dtype) for a in (offsets, vertical, prev)]
        + [pltpu.SemaphoreType.DMA((7,))],
        name="slash",
        compiler_params=large,
        cost_estimate=pl.CostEstimate(flops=100000000, bytes_accessed=1000000, transcendentals=0),
    )(queries, keys, values, send_order, offsets, vertical, prev)
    parts = pl.pallas_call(
        select_kernel,
        out_shape=jax.ShapeDtypeStruct((chips, 2 * NV + 24, HEAD), BF16),
        in_specs=[VMEM] * 2,
        out_specs=VMEM,
        name="select",
        compiler_params=small,
        cost_estimate=pl.CostEstimate(
            flops=10000000000, bytes_accessed=1000000, transcendentals=0
        ),
    )(recv, slash.astype(BF16))
    far = lax.ppermute(near, "c", swap)
    mine = lax.all_to_all(parts, ("z", "x"), 0, 0, tiled=True)
    mine, far = lax.optimization_barrier((mine, far))
    other = lax.ppermute(mine, "c", swap)
    half = pl.pallas_call(
        half_kernel,
        out_shape=jax.ShapeDtypeStruct((8 * n_ctx, 2 * HEAD), F32),
        in_specs=[VMEM] * 2,
        out_specs=VMEM,
        name="half",
        compiler_params=pltpu.CompilerParams(vmem_limit_bytes=32 * MIB),
        cost_estimate=pl.CostEstimate(flops=300000000, bytes_accessed=2000000, transcendentals=500000),
    )(recv, mine)
    full = pl.pallas_call(
        finish_kernel,
        out_shape=jax.ShapeDtypeStruct(queries.shape, BF16),
        in_specs=[VMEM] * 4,
        out_specs=VMEM,
        name="finish",
        compiler_params=pltpu.CompilerParams(vmem_limit_bytes=32 * MIB),
    )(recv, mine, other, half)
    theirs_full = lax.ppermute(full, "yl", swap)
    own, theirs = pl.pallas_call(
        own_kernel,
        out_shape=[
            jax.ShapeDtypeStruct((pairs, rows, width), F32),
            jax.ShapeDtypeStruct((pairs,) + near.shape[1:], BF16),
        ],
        in_specs=[VMEM, HBM, HBM, HBM],
        out_specs=[VMEM, VMEM],
        scratch_shapes=[
            pltpu.VMEM((pairs, out_weight.shape[0], width), BF16),
            pltpu.SemaphoreType.DMA((pairs,)),
            pltpu.SemaphoreType.DMA((2,)),
        ],
        name="project_own",
        compiler_params=pltpu.CompilerParams(vmem_limit_bytes=48 * MIB),
        cost_estimate=pl.CostEstimate(flops=300000000, bytes_accessed=8000000, transcendentals=0),
    )(full, out_weight, near, far)
    partial = pl.pallas_call(
        both_kernel,
        out_shape=jax.ShapeDtypeStruct((pairs, rows, width), BF16),
        in_specs=[VMEM] * 3,
        out_specs=VMEM,
        name="project_both",
        compiler_params=pltpu.CompilerParams(vmem_limit_bytes=32 * MIB),
    )(own, theirs_full, theirs)
    sums = lax.all_to_all(partial, "yh", 0, 0, tiled=True)
    return jnp.sum(sums.astype(F32), axis=0).astype(BF16)


def solution(mesh):
    cut = Mesh(mesh.devices.reshape(8, 4, 2, 4, 2), CTX + Y)
    placed = (
        P(CTX, Y),
        P(CTX, Y),
        P(CTX, Y),
        P(Y, None),
        P(Y, None),
        P(CTX, None),
        P(Y, None),
    )
    return jax.shard_map(
        local, mesh=cut, in_specs=placed, out_specs=P(CTX, Y), check_vma=False
    )
```
